32 devices in a mesh: section: 2 (over core), dp: 8 (over z, y), mp: 2 (over x).
Axes of the slice: x: 2, y: 2, z: 4, core: 2. Of those that a mesh axis runs over, the one named last changes fastest.
Arguments:
- states: bfloat16 [2, 16, 128, 2816], P('section', 'dp'), may hold values from -8 to 8
- injection: bfloat16 [16, 128, 2816], P('dp', None, 'mp'), may hold values from -2.390625 to 2.390625
- cotangent: bfloat16 [16, 128, 2816], P('dp', None, 'mp'), may hold values from -6 to 6
- gain: float32 [2816], P('mp'), may hold values from 0.5 to 1.5
- weight: bfloat16 [2816, 2816], P(None, 'mp'), may hold values from -0.109375 to 0.109375
- exits: int32 [16], P('dp'), may hold values from 1 to 2, as said below
- order: int32 [8, 2], P('dp'), may hold values from 0 to 1, each once within a row
Outputs:
- d_injection: float32 [16, 128, 2816], P('dp', None, 'mp')
- d_weight: float32 [2816, 2816], P(('section', 'dp'), 'mp')
- d_gain: float32 [2816], P('mp')
The draws below stay inside these ranges and needn't reach their ends.
Inputs may be any that keep to these rules, and one draw needn't show every extreme that they name: `exits`: some micro-batch runs all 2 iterations and some only one. `order`: each row is a permutation of 0 .. 1.
All inputs are finite; a program needn't handle non-finite values.
Results may differ from the reference program's by a relative error of at most 0.0033.
Values may be sent and summed in bfloat16 or wider, within the bound.
No kernel may reach another device: no remote copies, remote signals or barrier semaphores. Data moves between devices by JAX's collectives and lax.ppermute only.
A program may use at most 128 MiB of HBM per device.

```python
import jax
import jax.numpy as jnp
from jax import lax

D = 2816
MBD = 2
ROWS = 128
LOOPS = 2
MICRO = 16
N_DP = 8


def draw_exits(key, part):
    key_values, key_order = jax.random.split(key)
    values = jax.random.randint(key_values, (MICRO,), 1, LOOPS + 1)
    shuffled = jax.random.permutation(key_order, MICRO)
    values = values.at[shuffled[0]].set(LOOPS)
    values = values.at[shuffled[1]].set(1)
    return values.astype(jnp.int32)


def with_spikes(drawn, rng, source, target, parts, factor):
    def block_of(position):
        return (jnp.arange(drawn.shape[position]) // (drawn.shape[position] // parts)).reshape((-1,) + (1,) * (drawn.ndim - 1 - position))

    near = jax.random.permutation(rng, parts)[block_of(target)]
    second = (block_of(target) + parts // 2) % parts
    return jnp.where((block_of(source) == near) | (block_of(source) == second), factor * drawn, drawn)


def level_of(key, dims, shards, least, largest):
    def one(dim, shards_of):
        draws = jax.random.uniform(jax.random.fold_in(jax.random.fold_in(key, 6), dim), (shards_of,), jnp.float32, least / len(shards), largest / len(shards))
        return jnp.repeat(jnp.exp(draws), dims[dim] // shards_of).reshape((-1,) + (1,) * (len(dims) - dim - 1))

    level = one(*shards[0])
    for cut in shards[1:]:
        level = level * one(*cut)
    return level


def scatter_about(own_key, dims, spread, reach, cuts=(), kind=jnp.bfloat16):
    factor_of = level_of(own_key, dims, cuts, -0.22, 0.18) if cuts else 1.0
    entries = jax.random.normal(own_key, dims, jnp.float32) * spread * factor_of
    return jnp.minimum(jnp.maximum(entries, -reach), reach).astype(kind)


def heavy_noise(key, dims, scale, limit, cuts, heavy, kind=jnp.bfloat16):
    values = scale * jax.random.normal(key, dims, jnp.float32)
    if cuts:
        values = values * level_of(key, dims, cuts, -0.22, 0.18)
    return jnp.clip(with_spikes(values, jax.random.fold_in(key, 3), *heavy), -limit, limit).astype(kind)


def setup_inputs(seed: int = 0) -> dict:
    splits = jax.random.split(jax.random.key(seed), 8)
    states = heavy_noise(splits[0], (LOOPS, MICRO, ROWS, D), 1.0, 8.0, ((0, 2), (1, 8)), (0, 3, 2, 2.0))
    injection = scatter_about(splits[1], (MICRO, ROWS, D), 0.3, 2.390625, ((0, 8), (2, 2)))
    cotangent = scatter_about(splits[2], (MICRO, ROWS, D), 1.0, 6.0, ((0, 8), (2, 2)))
    gain = jnp.clip(1.0 + 0.1 * jax.random.normal(splits[3], (D,), jnp.float32), 0.5, 1.5)
    weight = scatter_about(splits[4], (D, D), D ** -0.5, 0.109375, ((1, 2),))
    exits = draw_exits(jax.random.fold_in(splits[7], 71), 0)
    order = jax.vmap(lambda own: jax.random.permutation(own, MBD))(jax.random.split(splits[6], N_DP)).reshape((N_DP, MBD)).astype(jnp.int32)
    return dict(states=states, injection=injection, cotangent=cotangent, gain=gain, weight=weight, exits=exits, order=order)


epsilon = 1e-06

def reference(states, injection, cotangent, gain, weight, exits, order):
    slot_micro = (jnp.arange(N_DP, dtype=jnp.int32)[:, None] * MBD + order).reshape(-1).astype(jnp.int32)

    def per_slot(slot, outer):
        d_weight, d_gain, d_injection = outer
        micro_id = slot_micro[slot]
        exit_count = exits[micro_id]
        inj_rows = injection[micro_id].astype(jnp.float32)
        start_grad = cotangent[micro_id].astype(jnp.float32)

        def per_iter(step_num, inner_state):
            carried, weight_acc, gain_acc, inj_acc = inner_state
            level = (exit_count - 1 - step_num).astype(jnp.int32)
            stashed = states[level, slot]
            pre_norm = jnp.dot(stashed, weight, preferred_element_type=jnp.float32) + inj_rows
            scaled = carried * gain
            squares = lax.optimization_barrier(jnp.sum(pre_norm * pre_norm, axis=1))
            inner_sum = lax.optimization_barrier(jnp.sum(scaled * pre_norm, axis=1))
            radius = jnp.sqrt(squares / D + epsilon)
            normed = pre_norm / radius[:, None]
            delta_pre = (scaled - normed * (inner_sum / (radius * D))[:, None]) / radius[:, None]
            delta_bf = delta_pre.astype(jnp.bfloat16)
            new_grad = jnp.dot(delta_bf, weight.T, preferred_element_type=jnp.float32).astype(jnp.bfloat16)
            new_grad = lax.optimization_barrier(new_grad).astype(jnp.float32)
            weight_acc = weight_acc + jnp.dot(stashed.T, delta_bf, preferred_element_type=jnp.float32)
            gain_acc = gain_acc + lax.optimization_barrier(jnp.sum(carried * normed, axis=0))
            return (new_grad, weight_acc, gain_acc, inj_acc + delta_pre)
        zero_inj = jnp.zeros((ROWS, D), jnp.float32)
        result = lax.fori_loop(0, exit_count, per_iter, (start_grad, d_weight, d_gain, zero_inj))
        d_injection = d_injection.at[micro_id].set(result[3])
        return (result[1], result[2], d_injection)
    init_state = (jnp.zeros((D, D), jnp.float32), jnp.zeros((D,), jnp.float32), jnp.zeros((MICRO, ROWS, D), jnp.float32))
    d_weight, d_gain, d_injection = lax.fori_loop(0, MICRO, per_slot, init_state)
    return (d_injection, d_weight, d_gain)
```

```python
import jax
import jax.numpy as jnp
from jax import lax
from jax.sharding import PartitionSpec as P

epsilon = 1e-06
f32, bf16 = jnp.float32, jnp.bfloat16


def swap(value, axis):
    return lax.ppermute(value, axis, [(0, 1), (1, 0)])


def shards(states, injection, cotangent, gain, weight, exits, order):
    stash = states[0]
    slots, rows, features = stash.shape
    half = weight.shape[1]
    sec = lax.axis_index("section")
    mp = lax.axis_index("mp")
    dp_size = lax.axis_size("dp")
    assert slots == 2 and lax.axis_size("section") == 2 and lax.axis_size("mp") == 2

    mine = lax.dynamic_index_in_dim(stash, sec, 0, keepdims=False)
    theirs = lax.dynamic_index_in_dim(stash, 1 - sec, 0, keepdims=False)
    got = swap(theirs, "section")
    state0 = jnp.where(sec == 0, mine, got)
    state1 = jnp.where(sec == 0, got, mine)

    block = features // (2 * dp_size)
    both = jnp.concatenate([state0, state1], axis=0)
    columns = both.T.reshape(2, dp_size, block, 2 * rows).transpose(1, 0, 2, 3)
    columns = columns.reshape(dp_size, 2 * block, 2 * rows)
    columns = lax.all_to_all(columns, "dp", 0, 0, tiled=True)

    micro = order[0, sec]
    deep = exits[micro] > 1
    inj = lax.dynamic_index_in_dim(injection, micro, 0, keepdims=False).astype(f32)
    cot = lax.dynamic_index_in_dim(cotangent, micro, 0, keepdims=False).astype(f32)

    def backward(pre, u, squares, inner):
        radius = jnp.sqrt(squares / features + epsilon)
        normed = pre / radius[:, None]
        delta = (u - normed * (inner / (radius * features))[:, None]) / radius[:, None]
        return normed, delta

    pre1 = jnp.dot(state1, weight, preferred_element_type=f32) + inj
    pre0 = jnp.dot(state0, weight, preferred_element_type=f32) + inj
    u1 = cot * gain
    stats = jnp.stack(
        [jnp.sum(pre1 * pre1, axis=1), jnp.sum(u1 * pre1, axis=1), jnp.sum(pre0 * pre0, axis=1)]
    )
    stats = stats + swap(stats, "mp")
    normed1, delta1 = backward(pre1, u1, stats[0], stats[1])
    delta1 = jnp.where(deep, delta1, 0.0)
    gain1 = jnp.sum(jnp.where(deep, cot * normed1, 0.0), axis=0)
    db1 = delta1.astype(bf16)

    def lower(which):
        part = lax.dynamic_slice_in_dim(weight, which * half, half, 0)
        return lax.dot_general(db1, part, (((1,), (1,)), ((), ())), preferred_element_type=f32)

    sent = swap(lower(1 - mp).astype(bf16), "mp")
    grads1 = lax.all_gather(db1, "dp")
    passed = (lower(mp) + sent.astype(f32)).astype(bf16).astype(f32)

    carried = jnp.where(deep, passed, cot)
    u0 = carried * gain
    inner0 = jnp.sum(u0 * pre0, axis=1)
    inner0 = inner0 + swap(inner0, "mp")
    normed0, delta0 = backward(pre0, u0, stats[2], inner0)
    gain0 = jnp.sum(carried * normed0, axis=0)
    db0 = delta0.astype(bf16)
    grads0 = lax.all_gather(db0, "dp")

    total = delta0 + delta1
    other = swap(total, "section")
    first = micro == 0
    d_injection = jnp.stack([jnp.where(first, total, other), jnp.where(first, other, total)])

    gains = lax.all_gather(gain0 + gain1, ("section", "dp"))
    d_gain = jnp.sum(gains, axis=0)

    def terms(cols, grads):
        return lax.dot_general(cols, grads, (((0, 2), (0, 1)), ((), ())), preferred_element_type=f32)

    def product(k):
        grads = grads1 if k else grads0
        return terms(columns[:, :, k * rows : (k + 1) * rows], grads)

    summed = product(1) + product(0)
    own = lax.dynamic_slice_in_dim(summed, sec * block, block, 0)
    away = lax.dynamic_slice_in_dim(summed, (1 - sec) * block, block, 0)
    d_weight = own + swap(away, "section")
    return (d_injection, d_weight, d_gain)


def solution(mesh):
    return jax.shard_map(
        shards,
        mesh=mesh,
        in_specs=(
            P("section", "dp", None, None),
            P("dp", None, "mp"),
            P("dp", None, "mp"),
            P("mp"),
            P(None, "mp"),
            P("dp"),
            P("dp", None),
        ),
        out_specs=(P("dp", None, "mp"), P(("section", "dp"), "mp"), P("mp")),
        check_vma=False,
    )
```

```python
import functools

import jax
import jax.numpy as jnp
from jax import lax
from jax.experimental import pallas as pl
from jax.experimental.pallas import tpu as pltpu
from jax.sharding import PartitionSpec as P

epsilon = 1e-06
f32, bf16 = jnp.float32, jnp.bfloat16


def swap(value, axis):
    return lax.ppermute(value, axis, [(0, 1), (1, 0)])


def weight_terms(line, spot, cols0, cols1, grads1, own, lefts, rights, lanes):
    rows = own.shape[0]
    height = cols0.shape[1]
    start, width = lanes

    def kernel(spot_ref, cols0_ref, cols1_ref, *refs):
        grads1_refs, own_ref = refs[:line], refs[line]
        left_refs, right_refs = refs[line + 1 : 2 * line], refs[2 * line : 3 * line - 1]
        out_ref, lhs, rhs = refs[3 * line - 1 :]
        at = spot_ref[0]
        for source in range(line):
            lhs[:, source * rows : (source + 1) * rows] = cols0_ref[at ^ source]
            lhs[:, (line + source) * rows : (line + source + 1) * rows] = cols1_ref[source]
            rhs[line + source] = grads1_refs[source][:, start : start + width]
        rhs[at] = own_ref[...]
        for step in range(line - 1):

            @pl.when(at > step)
            def _():
                rhs[at - 1 - step] = left_refs[step][...]

            @pl.when(at + step < line - 1)
            def _():
                rhs[at + 1 + step] = right_refs[step][...]

        out_ref[...] = jnp.dot(
            lhs[...], rhs[...].reshape(2 * line * rows, width), preferred_element_type=f32
        )

    vmem = pl.BlockSpec(memory_space=pltpu.VMEM)
    count = 2 + line + 1 + 2 * (line - 1)
    return pl.pallas_call(
        kernel,
        out_shape=jax.ShapeDtypeStruct((height, width), f32),
        in_specs=[pl.BlockSpec(memory_space=pltpu.SMEM)] + [vmem] * count,
        out_specs=vmem,
        scratch_shapes=[
            pltpu.VMEM((height, 2 * line * rows), bf16),
            pltpu.VMEM((2 * line, rows, width), bf16),
        ],
        compiler_params=pltpu.CompilerParams(vmem_limit_bytes=40 * 2**20),
        cost_estimate=pl.CostEstimate(
            flops=4 * height * line * rows * width, bytes_accessed=2**23, transcendentals=0
        ),
    )(spot, cols0, cols1, *grads1, own, *lefts, *rights)


def shards(states, injection, cotangent, gain, weight, exits, order):
    stash = states[0]
    slots, rows, features = stash.shape
    half = weight.shape[1]
    sec = lax.axis_index("section")
    mp = lax.axis_index("mp")
    dp = lax.axis_index("dp")
    line = lax.axis_size("dp") // 2
    assert slots == 2 and lax.axis_size("section") == 2 and lax.axis_size("mp") == 2
    assert line & (line - 1) == 0
    spot, side = dp // 2, dp % 2

    def across(value, distance):
        return lax.ppermute(value, "dp", [(i, i ^ distance) for i in range(2 * line)])

    def shift(value, sources, by):
        pairs = [(2 * i + j, 2 * (i + by) + j) for i in sources for j in range(2)]
        return lax.ppermute(value, "dp", pairs)

    block = features // (4 * line)
    turned = lax.dynamic_index_in_dim(stash, mp, 0, keepdims=False).T
    turned = turned.reshape(2, line, 2 * block, rows)

    def columns_for(place):
        picked = lax.dynamic_index_in_dim(turned, place, 1, keepdims=False)
        return picked.reshape(4 * block, rows)

    columns = [columns_for(spot)]
    columns += [across(columns_for(spot ^ d), 2 * d) for d in range(1, line)]

    mine = lax.dynamic_index_in_dim(stash, sec, 0, keepdims=False)
    theirs = lax.dynamic_index_in_dim(stash, 1 - sec, 0, keepdims=False)
    got = swap(theirs, "section")

    micro = order[0, sec]
    deep = exits[micro] > 1
    inj = lax.dynamic_index_in_dim(injection, micro, 0, keepdims=False).astype(f32)
    cot = lax.dynamic_index_in_dim(cotangent, micro, 0, keepdims=False).astype(f32)

    def backward(pre, u, squares, inner):
        radius = jnp.sqrt(squares / features + epsilon)
        normed = pre / radius[:, None]
        delta = (u - normed * (inner / (radius * features))[:, None]) / radius[:, None]
        return normed, delta

    pre_mine = jnp.dot(mine, weight, preferred_element_type=f32) + inj
    pre_got = jnp.dot(got, weight, preferred_element_type=f32) + inj
    pre_mine, pre_got = lax.optimization_barrier((pre_mine, pre_got))
    pre1 = jnp.where(sec == 0, pre_got, pre_mine)
    pre0 = jnp.where(sec == 0, pre_mine, pre_got)
    u1 = cot * gain
    stats = jnp.stack(
        [jnp.sum(pre1 * pre1, axis=1), jnp.sum(u1 * pre1, axis=1), jnp.sum(pre0 * pre0, axis=1)]
    )
    stats = stats + swap(stats, "mp")
    normed1, delta1 = backward(pre1, u1, stats[0], stats[1])
    delta1 = jnp.where(deep, delta1, 0.0)
    gain1 = jnp.sum(jnp.where(deep, cot * normed1, 0.0), axis=0)
    db1 = delta1.astype(bf16)

    def lower(which, grads):
        part = lax.dynamic_slice_in_dim(weight, which * half, half, 0)
        return lax.dot_general(part, grads, (((1,), (1,)), ((), ())), preferred_element_type=f32)

    away = lower(1 - mp, db1).astype(bf16)
    sent = swap(away, "mp")
    kept = lower(mp, db1)
    kept, sent, db1 = lax.optimization_barrier((kept, sent, db1))
    grads1 = [db1] + [across(db1, 2 * d) for d in range(1, line)]
    passed = (kept + sent.astype(f32)).astype(bf16).astype(f32).T

    carried = jnp.where(deep, passed, cot)
    u0 = carried * gain
    inner0 = jnp.sum(u0 * pre0, axis=1)
    inner0 = inner0 + swap(inner0, "mp")
    normed0, delta0 = backward(pre0, u0, stats[2], inner0)
    gain0 = jnp.sum(carried * normed0, axis=0)
    db0 = delta0.astype(bf16)

    cut = (half // 2 + 127) // 128 * 128
    lanes = [(0, cut), (cut, half - cut)]
    owns = [db0[:, start : start + width] for start, width in lanes]
    lefts, rights = [[], []], [[], []]
    for step in range(line - 1):
        for h in range(2):
            onward, back = (lefts[h][-1], rights[h][-1]) if step else (owns[h], owns[h])
            lefts[h].append(shift(onward, range(step, line - 1), 1))
            rights[h].append(shift(back, range(1, line - step), -1))

    columns = jnp.stack(columns)
    columns, _ = lax.optimization_barrier((columns, db0))
    both = ("section", "mp")
    near = lax.ppermute(columns, both, [(2, 0), (0, 1), (3, 2), (1, 3)])
    far = lax.ppermute(columns, both, [(2, 1), (1, 2)])
    cols0 = jnp.where(sec == 0, jnp.where(mp == 0, columns, near), jnp.where(mp == 0, far, near))
    cols1 = jnp.where(sec == 0, jnp.where(mp == 0, near, far), jnp.where(mp == 0, near, columns))

    total = delta0 + delta1
    other = swap(total, "section")
    first = micro == 0
    d_injection = jnp.stack([jnp.where(first, total, other), jnp.where(first, other, total)])

    d_gain = gain0 + gain1
    d_gain = d_gain + swap(d_gain, "section")
    distance = 1
    while distance < 2 * line:
        d_gain = d_gain + across(d_gain, distance)
        distance *= 2

    pieces = []
    for h in range(2):
        terms = weight_terms(
            line, spot.reshape(1), cols0, cols1, grads1, owns[h], lefts[h], rights[h], lanes[h]
        )
        terms = terms.reshape(2, 2 * block, lanes[h][1])
        own = lax.dynamic_index_in_dim(terms, sec, 0, keepdims=False)
        away = lax.dynamic_index_in_dim(terms, 1 - sec, 0, keepdims=False)
        chip = (own + swap(away, "section")).reshape(2, block, lanes[h][1])
        own = lax.dynamic_index_in_dim(chip, side, 0, keepdims=False)
        away = lax.dynamic_index_in_dim(chip, 1 - side, 0, keepdims=False).astype(bf16)
        pieces.append(own + across(away, 1).astype(f32))
    d_weight = jnp.concatenate(pieces, axis=1)
    return (d_injection, d_weight, d_gain)


def solution(mesh):
    return jax.shard_map(
        shards,
        mesh=mesh,
        in_specs=(
            P("section", "dp", None, None),
            P("dp", None, "mp"),
            P("dp", None, "mp"),
            P("mp"),
            P(None, "mp"),
            P("dp"),
            P("dp", None),
        ),
        out_specs=(P("dp", None, "mp"), P(("section", "dp"), "mp"), P("mp")),
        check_vma=False,
    )
```

```python
import jax
import jax.numpy as jnp
from jax import lax
from jax.experimental import pallas as pl
from jax.experimental.pallas import tpu as pltpu
from jax.sharding import PartitionSpec as P

epsilon = 1e-06
f32, bf16 = jnp.float32, jnp.bfloat16
VMEM = pl.BlockSpec(memory_space=pltpu.VMEM)
SMEM = pl.BlockSpec(memory_space=pltpu.SMEM)
ANY = pl.BlockSpec(memory_space=pl.ANY)


def call(kernel, outs, ins, scratch=(), limit=24):
    shapes = [jax.ShapeDtypeStruct(shape, kind) for shape, kind in outs]
    specs, values = zip(*ins)
    return pl.pallas_call(
        kernel,
        out_shape=shapes,
        in_specs=list(specs),
        out_specs=[VMEM] * len(shapes),
        scratch_shapes=list(scratch),
        compiler_params=pltpu.CompilerParams(vmem_limit_bytes=limit * 2**20),
        cost_estimate=pl.CostEstimate(flops=1000, bytes_accessed=1000, transcendentals=0),
    )(*values)


def swap(value, axis):
    return lax.ppermute(value, axis, [(0, 1), (1, 0)])


def chunks_of(total, size):
    return [(start, min(size, total - start)) for start in range(0, total, size)]


def to_rows(columns):
    rows = columns[0].shape[0]
    lane = lax.broadcasted_iota(jnp.int32, (rows, 128), 1)
    wide = jnp.zeros((rows, 128), f32)
    for index, column in enumerate(columns):
        wide = jnp.where(lane == index, column, wide)
    return wide.T[:8]


def to_columns(packed):
    return jnp.concatenate([packed] * 16, axis=0).T


def forward(stash, weight, injection, order):
    slots, rows, features = stash.shape
    half = weight.shape[1]
    parts = chunks_of(features, 512)

    def kernel(order_ref, stash_hbm, weight_hbm, inj_ref, keep_ref, send_ref, x, w, acc, sems):
        sec = lax.axis_index("section")
        copies = [pltpu.make_async_copy(stash_hbm, x, sems.at[0])]
        for index, (start, size) in enumerate(parts):
            part = pl.ds(start, size)
            copies.append(
                pltpu.make_async_copy(weight_hbm.at[part], w.at[part], sems.at[index + 1])
            )
        for copy in copies:
            copy.start()
        copies[0].wait()
        for index, (start, size) in enumerate(parts):
            copies[index + 1].wait()
            left = x[:, :, start : start + size].reshape(slots * rows, size)
            term = jnp.dot(left, w[start : start + size], preferred_element_type=f32)
            term = term.reshape(slots, rows, half)
            if index:
                acc[...] += term
            else:
                acc[...] = term
        keep_ref[...] = acc[sec] + inj_ref[order_ref[0, sec]].astype(f32)
        send_ref[...] = acc[1 - sec] + inj_ref[order_ref[0, 1 - sec]].astype(f32)

    return call(
        kernel,
        [((rows, half), f32)] * 2,
        [(SMEM, order), (ANY, stash), (ANY, weight), (VMEM, injection)],
        [
            pltpu.VMEM(stash.shape, bf16),
            pltpu.VMEM(weight.shape, bf16),
            pltpu.VMEM((slots, rows, half), f32),
            pltpu.SemaphoreType.DMA((len(parts) + 1,)),
        ],
        limit=60,
    )


def row_sums(order, cotangent, gain, keep, got):
    rows = keep.shape[0]

    def kernel(order_ref, cot_ref, gain_ref, keep_ref, got_ref, out_ref):
        sec = lax.axis_index("section")
        first = sec == 0
        keep, got = keep_ref[...], got_ref[...]
        pre1, pre0 = jnp.where(first, got, keep), jnp.where(first, keep, got)
        u = cot_ref[order_ref[0, sec]].astype(f32) * gain_ref[...]
        sums = [pre1 * pre1, u * pre1, pre0 * pre0]
        out_ref[...] = to_rows([jnp.sum(each, axis=1, keepdims=True) for each in sums])

    ins = [(SMEM, order), (VMEM, cotangent), (VMEM, gain), (VMEM, keep), (VMEM, got)]
    return call(kernel, [((8, rows), f32)], ins)[0]


def delta_of(pre, u, squares, inner, features):
    radius = jnp.sqrt(squares / features + epsilon)
    inverse = 1.0 / radius
    normed = pre * inverse
    return normed, (u - normed * (inner * inverse / features)) * inverse


def lower_iteration1(order, exits, cotangent, gain, keep, got, sums, others, weight):
    rows, half = keep.shape
    features = weight.shape[0]
    parts = chunks_of(half, 512)

    def kernel(order_ref, exits_ref, cot_ref, gain_ref, keep_ref, got_ref, sums_ref, others_ref,
               weight_hbm, db_ref, delta_ref, gain_out, away_ref, w, sems):
        sec, mp = lax.axis_index("section"), lax.axis_index("mp")
        base = pl.multiple_of((1 - mp) * half, 128)
        copies = []
        for index, (start, size) in enumerate(parts):
            copies.append(
                pltpu.make_async_copy(
                    weight_hbm.at[pl.ds(base + start, size)],
                    w.at[pl.ds(start, size)],
                    sems.at[index],
                )
            )
            copies[-1].start()
        micro = order_ref[0, sec]
        live = jnp.where(exits_ref[micro] > 1, 1.0, 0.0)
        stats = to_columns(sums_ref[...] + others_ref[...])
        pre = jnp.where(sec == 0, got_ref[...], keep_ref[...])
        cot = cot_ref[micro].astype(f32)
        normed, delta = delta_of(pre, cot * gain_ref[...], stats[:, 0:1], stats[:, 1:2], features)
        delta = delta * live
        delta_ref[...] = delta
        db = delta.astype(bf16)
        db_ref[...] = db
        gain_out[...] = jnp.sum(cot * normed, axis=0, keepdims=True) * live
        for index, (start, size) in enumerate(parts):
            copies[index].wait()
            part = w[start : start + size]
            away_ref[start : start + size] = lax.dot_general(
                part, db, (((1,), (1,)), ((), ())), preferred_element_type=f32
            ).astype(bf16)

    return call(
        kernel,
        [((rows, half), bf16), ((rows, half), f32), ((1, half), f32), ((half, rows), bf16)],
        [(SMEM, order), (SMEM, exits), (VMEM, cotangent), (VMEM, gain), (VMEM, keep), (VMEM, got),
         (VMEM, sums), (VMEM, others), (ANY, weight)],
        [pltpu.VMEM((half, half), bf16), pltpu.SemaphoreType.DMA((len(parts),))],
    )


def kept_half(db, weight):
    rows, half = db.shape
    parts = chunks_of(half, 512)

    def kernel(db_ref, weight_hbm, out_ref, w, sems):
        base = pl.multiple_of(lax.axis_index("mp") * half, 128)
        copies = []
        for index, (start, size) in enumerate(parts):
            copies.append(
                pltpu.make_async_copy(
                    weight_hbm.at[pl.ds(base + start, size)],
                    w.at[pl.ds(start, size)],
                    sems.at[index],
                )
            )
            copies[-1].start()
        for index, (start, size) in enumerate(parts):
            copies[index].wait()
            out_ref[start : start + size] = lax.dot_general(
                w[start : start + size],
                db_ref[...],
                (((1,), (1,)), ((), ())),
                preferred_element_type=f32,
            )

    return call(
        kernel,
        [((half, rows), f32)],
        [(VMEM, db), (ANY, weight)],
        [pltpu.VMEM((half, half), bf16), pltpu.SemaphoreType.DMA((len(parts),))],
    )[0]


def carry(order, exits, cotangent, gain, keep, got, kept, sent):
    rows, half = keep.shape

    def kernel(order_ref, exits_ref, cot_ref, gain_ref, keep_ref, got_ref, kept_ref, sent_ref,
               carried_ref, inner_ref):
        sec = lax.axis_index("section")
        micro = order_ref[0, sec]
        passed = (kept_ref[...] + sent_ref[...].astype(f32)).astype(bf16).astype(f32).T
        cot = cot_ref[micro].astype(f32)
        carried = jnp.where(exits_ref[micro] > 1, passed, cot)
        carried_ref[...] = carried
        pre = jnp.where(sec == 0, keep_ref[...], got_ref[...])
        inner = jnp.sum(carried * gain_ref[...] * pre, axis=1, keepdims=True)
        inner_ref[...] = to_rows([inner])

    return call(
        kernel,
        [((rows, half), f32), ((8, rows), f32)],
        [(SMEM, order), (SMEM, exits), (VMEM, cotangent), (VMEM, gain), (VMEM, keep), (VMEM, got),
         (VMEM, kept), (VMEM, sent)],
    )


def iteration0(gain, keep, got, sums, others, carried, inner, inner_other, delta1, gain1, features,
               lanes):
    rows, half = keep.shape

    def kernel(gain_ref, keep_ref, got_ref, sums_ref, others_ref, carried_ref, inner_ref, other_ref,
               delta1_ref, gain1_ref, total_ref, *db_refs):
        sec = lax.axis_index("section")
        squares = to_columns(sums_ref[...] + others_ref[...])[:, 2:3]
        inner = to_columns(inner_ref[...] + other_ref[...])[:, 0:1]
        pre = jnp.where(sec == 0, keep_ref[...], got_ref[...])
        carried = carried_ref[...]
        normed, delta = delta_of(pre, carried * gain_ref[...], squares, inner, features)
        total_ref[:rows] = delta + delta1_ref[...]
        gains = jnp.sum(carried * normed, axis=0, keepdims=True) + gain1_ref[...]
        total_ref[rows:] = jnp.broadcast_to(gains, (8, half))
        for db_ref, (start, width) in zip(db_refs, lanes):
            db_ref[...] = delta[:, start : start + width].astype(bf16)

    values = [gain, keep, got, sums, others, carried, inner, inner_other, delta1, gain1]
    return call(
        kernel,
        [((rows + 8, half), f32)] + [((rows, width), bf16) for _, width in lanes],
        [(VMEM, value) for value in values],
    )


def weight_terms(line, spot, cols0, cols1, grads0, grads1, lanes):
    rows, width = grads0[0].shape
    start = lanes[0]
    height = cols0.shape[1]
    chained = len(grads1) > line

    def kernel(spot_ref, cols0_ref, cols1_ref, *refs):
        out_ref, lhs, rhs = refs[-3:]
        grads0_refs, grads1_refs = refs[:line], refs[line:-3]
        part = slice(start, start + width)
        for source in range(line):
            lhs[:, source * rows : (source + 1) * rows] = cols0_ref[source]
            lhs[:, (line + source) * rows : (line + source + 1) * rows] = cols1_ref[source]
            rhs[source] = grads0_refs[source][...]
        for source in range(2 if chained else line):
            rhs[line + source] = grads1_refs[source][:, part]
        if chained:
            mid_ref, onward_ref, last_ref = grads1_refs[2:]
            inside = (spot_ref[0] == 1) | (spot_ref[0] == 2)

            @pl.when(inside)
            def _():
                rhs[line + 2] = onward_ref[:, part]
                rhs[line + 3] = mid_ref[:, part]

            @pl.when(jnp.logical_not(inside))
            def _():
                rhs[line + 2] = last_ref[:rows, part]
                rhs[line + 3] = last_ref[rows:, part]

        out_ref[...] = jnp.dot(
            lhs[...], rhs[...].reshape(2 * line * rows, width), preferred_element_type=f32
        )

    values = [cols0, cols1, *grads0, *grads1]
    return call(
        kernel,
        [((height, width), f32)],
        [(SMEM, spot)] + [(VMEM, value) for value in values],
        [
            pltpu.VMEM((height, 2 * line * rows), bf16),
            pltpu.VMEM((2 * line, rows, width), bf16),
        ],
    )[0]


def shards(states, injection, cotangent, gain, weight, exits, order):
    stash = states[0]
    slots, rows, features = stash.shape
    half = weight.shape[1]
    sec = lax.axis_index("section")
    mp = lax.axis_index("mp")
    dp = lax.axis_index("dp")
    line = lax.axis_size("dp") // 2
    assert slots == 2 and lax.axis_size("section") == 2 and lax.axis_size("mp") == 2
    assert line & (line - 1) == 0
    spot, side = dp // 2, dp % 2

    def across(value, distance):
        return lax.ppermute(value, "dp", [(i, i ^ distance) for i in range(2 * line)])

    def along(value, moves):
        pairs = [(2 * i + j, 2 * k + j) for i, k in moves for j in range(2)]
        return lax.ppermute(value, "dp", pairs)

    block = features // (4 * line)
    turned = lax.dynamic_index_in_dim(stash, mp, 0, keepdims=False).T
    turned = turned.reshape(2, line, 2 * block, rows)

    def columns_for(place):
        picked = lax.dynamic_index_in_dim(turned, place, 1, keepdims=False)
        return picked.reshape(4 * block, rows)

    columns = [columns_for(spot)]
    columns += [across(columns_for(spot ^ d), 2 * d) for d in range(1, line)]

    gain = gain.reshape(1, half)
    keep, send = forward(stash, weight, injection, order)
    got = swap(send, "section")
    sums = row_sums(order, cotangent, gain, keep, got)
    others = swap(sums, "mp")
    others, columns[1:-1] = lax.optimization_barrier((others, columns[1:-1]))
    db1, delta1, gain1, away = lower_iteration1(
        order, exits, cotangent, gain, keep, got, sums, others, weight
    )
    sent = swap(away, "mp")
    chained = line == 4
    if chained:
        near1 = along(db1, [(0, 1), (1, 0), (2, 3), (3, 2)])
        mid1 = along(db1, [(1, 2), (2, 1)])
        grads1 = [db1, near1, mid1]
    else:
        grads1 = [db1] + [across(db1, 2 * d) for d in range(1, line)]
    kept = kept_half(db1, weight)
    kept, sent, columns, grads1[1] = lax.optimization_barrier((kept, sent, columns, grads1[1]))

    if chained:
        onward1 = along(grads1[1], [(1, 2), (2, 1)])
    carried, inner = carry(order, exits, cotangent, gain, keep, got, kept, sent)
    inner_other = swap(inner, "mp")
    inner_other, grads1[2] = lax.optimization_barrier((inner_other, grads1[2]))
    cut = (half * 5 // 8 + 127) // 128 * 128
    lanes = [(0, cut), (cut, half - cut)]
    total, *owns = iteration0(
        gain, keep, got, sums, others, carried, inner, inner_other, delta1, gain1, features, lanes
    )
    grads0 = [[own] + [across(own, 2 * d) for d in range(1, line)] for own in owns]
    columns = jnp.stack(columns)
    grads0[0][1], total, columns = lax.optimization_barrier((grads0[0][1], total, columns))
    if chained:
        both = jnp.concatenate([grads1[2], onward1], axis=0)
        both, grads0[0][1] = lax.optimization_barrier((both, grads0[0][1]))
        grads1 += [onward1, along(both, [(1, 0), (2, 3)])]

    both = ("section", "mp")
    near = lax.ppermute(columns, both, [(2, 0), (0, 1), (3, 2), (1, 3)])
    far = lax.ppermute(columns, both, [(2, 1), (1, 2)])
    cols0 = jnp.where(sec == 0, jnp.where(mp == 0, columns, near), jnp.where(mp == 0, far, near))
    cols1 = jnp.where(sec == 0, jnp.where(mp == 0, near, far), jnp.where(mp == 0, near, columns))

    other = swap(total, "section")
    first = order[0, sec] == 0
    mine, theirs = total[:rows], other[:rows]
    d_injection = jnp.stack([jnp.where(first, mine, theirs), jnp.where(first, theirs, mine)])

    d_gain = total[rows:] + other[rows:]
    distance = 1
    while distance < 2 * line:
        d_gain = d_gain + across(d_gain, distance)
        distance *= 2
    d_gain = d_gain[0]

    cols0, cols1, d_injection = lax.optimization_barrier((cols0, cols1, d_injection))
    pieces = []
    for h, (start, width) in enumerate(lanes):
        terms = weight_terms(
            line, spot.reshape(1), cols0, cols1, grads0[h], grads1, (start, width)
        )
        terms = terms.reshape(2, 2 * block, width)
        mine = lax.dynamic_index_in_dim(terms, sec, 0, keepdims=False)
        away = lax.dynamic_index_in_dim(terms, 1 - sec, 0, keepdims=False)
        chip = (mine + swap(away, "section")).reshape(2, block, width)
        mine = lax.dynamic_index_in_dim(chip, side, 0, keepdims=False)
        away = lax.dynamic_index_in_dim(chip, 1 - side, 0, keepdims=False).astype(bf16)
        if h == 0:
            away, d_gain, grads0[1] = lax.optimization_barrier((away, d_gain, grads0[1]))
        pieces.append(mine + across(away, 1).astype(f32))
    d_weight = jnp.concatenate(pieces, axis=1)
    return (d_injection, d_weight, d_gain)


def solution(mesh):
    return jax.shard_map(
        shards,
        mesh=mesh,
        in_specs=(
            P("section", "dp", None, None),
            P("dp", None, "mp"),
            P("dp", None, "mp"),
            P("mp"),
            P(None, "mp"),
            P("dp"),
            P("dp", None),
        ),
        out_specs=(P("dp", None, "mp"), P(("section", "dp"), "mp"), P("mp")),
        check_vma=False,
    )
```

```python
import jax
import jax.numpy as jnp
from jax import lax
from jax.experimental import pallas as pl
from jax.experimental.pallas import tpu as pltpu
from jax.sharding import PartitionSpec as P

epsilon = 1e-06
f32, bf16 = jnp.float32, jnp.bfloat16
VMEM = pl.BlockSpec(memory_space=pltpu.VMEM)
SMEM = pl.BlockSpec(memory_space=pltpu.SMEM)
ANY = pl.BlockSpec(memory_space=pl.ANY)


def call(kernel, outs, ins, scratch=(), limit=24):
    shapes = [jax.ShapeDtypeStruct(shape, kind) for shape, kind in outs]
    specs, values = zip(*ins)
    return pl.pallas_call(
        kernel,
        out_shape=shapes,
        in_specs=list(specs),
        out_specs=[VMEM] * len(shapes),
        scratch_shapes=list(scratch),
        compiler_params=pltpu.CompilerParams(vmem_limit_bytes=limit * 2**20),
        cost_estimate=pl.CostEstimate(flops=1000, bytes_accessed=1000, transcendentals=0),
    )(*values)


def swap(value, axis):
    return lax.ppermute(value, axis, [(0, 1), (1, 0)])


def chunks_of(total, size):
    return [(start, min(size, total - start)) for start in range(0, total, size)]


def to_rows(columns):
    rows = columns[0].shape[0]
    lane = lax.broadcasted_iota(jnp.int32, (rows, 128), 1)
    wide = jnp.zeros((rows, 128), f32)
    for index, column in enumerate(columns):
        wide = jnp.where(lane == index, column, wide)
    return wide.T[:8]


def to_columns(packed):
    return jnp.concatenate([packed] * 16, axis=0).T


def forward(stash, weight, injection, order):
    slots, rows, features = stash.shape
    half = weight.shape[1]
    parts = chunks_of(half, 256)

    def kernel(order_ref, stash_hbm, weight_hbm, inj_ref, keep_ref, send_ref, x, w, acc, sems):
        sec = lax.axis_index("section")
        copies = [pltpu.make_async_copy(stash_hbm, x, sems.at[0])]
        for index, (start, size) in enumerate(parts):
            part = pl.ds(start, size)
            copies.append(
                pltpu.make_async_copy(weight_hbm.at[:, part], w.at[:, part], sems.at[index + 1])
            )
        for copy in copies:
            copy.start()
        mine, theirs = order_ref[0, sec], order_ref[0, 1 - sec]
        copies[0].wait()
        for index, (start, size) in enumerate(parts):
            copies[index + 1].wait()
            part = slice(start, start + size)
            left = x[...].reshape(slots * rows, features)
            term = jnp.dot(left, w[:, part], preferred_element_type=f32)
            acc[:, :, :size] = term.reshape(slots, rows, size)
            keep_ref[:, part] = acc[sec, :, :size] + inj_ref[mine, :, part].astype(f32)
            send_ref[:, part] = acc[1 - sec, :, :size] + inj_ref[theirs, :, part].astype(f32)

    return call(
        kernel,
        [((rows, half), f32)] * 2,
        [(SMEM, order), (ANY, stash), (ANY, weight), (VMEM, injection)],
        [
            pltpu.VMEM(stash.shape, bf16),
            pltpu.VMEM(weight.shape, bf16),
            pltpu.VMEM((slots, rows, 256), f32),
            pltpu.SemaphoreType.DMA((len(parts) + 1,)),
        ],
        limit=60,
    )


def row_sums(order, cotangent, gain, keep, got):
    rows = keep.shape[0]

    def kernel(order_ref, cot_ref, gain_ref, keep_ref, got_ref, out_ref):
        sec = lax.axis_index("section")
        first = sec == 0
        keep, got = keep_ref[...], got_ref[...]
        pre1, pre0 = jnp.where(first, got, keep), jnp.where(first, keep, got)
        u = cot_ref[order_ref[0, sec]].astype(f32) * gain_ref[...]
        sums = [pre1 * pre1, u * pre1, pre0 * pre0]
        out_ref[...] = to_rows([jnp.sum(each, axis=1, keepdims=True) for each in sums])

    ins = [(SMEM, order), (VMEM, cotangent), (VMEM, gain), (VMEM, keep), (VMEM, got)]
    return call(kernel, [((8, rows), f32)], ins)[0]


def delta_of(pre, u, squares, inner, features):
    radius = jnp.sqrt(squares / features + epsilon)
    inverse = 1.0 / radius
    normed = pre * inverse
    return normed, (u - normed * (inner * inverse / features)) * inverse


def lower_iteration1(order, exits, cotangent, gain, keep, got, sums, others, weight):
    rows, half = keep.shape
    features = weight.shape[0]
    parts = chunks_of(half, 512)

    def kernel(order_ref, exits_ref, cot_ref, gain_ref, keep_ref, got_ref, sums_ref, others_ref,
               weight_hbm, db_ref, delta_ref, gain_out, away_ref, w, sems):
        sec, mp = lax.axis_index("section"), lax.axis_index("mp")
        base = pl.multiple_of((1 - mp) * half, 128)
        copies = []
        for index, (start, size) in enumerate(parts):
            copies.append(
                pltpu.make_async_copy(
                    weight_hbm.at[pl.ds(base + start, size)],
                    w.at[pl.ds(start, size)],
                    sems.at[index],
                )
            )
            copies[-1].start()
        micro = order_ref[0, sec]
        live = jnp.where(exits_ref[micro] > 1, 1.0, 0.0)
        stats = to_columns(sums_ref[...] + others_ref[...])
        pre = jnp.where(sec == 0, got_ref[...], keep_ref[...])
        cot = cot_ref[micro].astype(f32)
        normed, delta = delta_of(pre, cot * gain_ref[...], stats[:, 0:1], stats[:, 1:2], features)
        delta = delta * live
        delta_ref[...] = delta
        db = delta.astype(bf16)
        db_ref[...] = db
        gain_out[...] = jnp.sum(cot * normed, axis=0, keepdims=True) * live
        for index, (start, size) in enumerate(parts):
            copies[index].wait()
            part = w[start : start + size]
            away_ref[start : start + size] = lax.dot_general(
                part, db, (((1,), (1,)), ((), ())), preferred_element_type=f32
            ).astype(bf16)

    return call(
        kernel,
        [((rows, half), bf16), ((rows, half), f32), ((1, half), f32), ((half, rows), bf16)],
        [(SMEM, order), (SMEM, exits), (VMEM, cotangent), (VMEM, gain), (VMEM, keep), (VMEM, got),
         (VMEM, sums), (VMEM, others), (ANY, weight)],
        [pltpu.VMEM((half, half), bf16), pltpu.SemaphoreType.DMA((len(parts),))],
        limit=54,
    )


def kept_half(db, weight):
    rows, half = db.shape
    parts = chunks_of(half, 512)

    def kernel(db_ref, weight_hbm, out_ref, w, sems):
        base = pl.multiple_of(lax.axis_index("mp") * half, 128)
        copies = []
        for index, (start, size) in enumerate(parts):
            copies.append(
                pltpu.make_async_copy(
                    weight_hbm.at[pl.ds(base + start, size)],
                    w.at[pl.ds(start, size)],
                    sems.at[index],
                )
            )
            copies[-1].start()
        for index, (start, size) in enumerate(parts):
            copies[index].wait()
            out_ref[start : start + size] = lax.dot_general(
                w[start : start + size],
                db_ref[...],
                (((1,), (1,)), ((), ())),
                preferred_element_type=f32,
            )

    return call(
        kernel,
        [((half, rows), f32)],
        [(VMEM, db), (ANY, weight)],
        [pltpu.VMEM((half, half), bf16), pltpu.SemaphoreType.DMA((len(parts),))],
        limit=54,
    )[0]


def carry(order, exits, cotangent, gain, keep, got, kept, sent):
    rows, half = keep.shape

    def kernel(order_ref, exits_ref, cot_ref, gain_ref, keep_ref, got_ref, kept_ref, sent_ref,
               carried_ref, inner_ref):
        sec = lax.axis_index("section")
        micro = order_ref[0, sec]
        passed = (kept_ref[...] + sent_ref[...].astype(f32)).astype(bf16).astype(f32).T
        cot = cot_ref[micro].astype(f32)
        carried = jnp.where(exits_ref[micro] > 1, passed, cot)
        carried_ref[...] = carried
        pre = jnp.where(sec == 0, keep_ref[...], got_ref[...])
        inner = jnp.sum(carried * gain_ref[...] * pre, axis=1, keepdims=True)
        inner_ref[...] = to_rows([inner])

    return call(
        kernel,
        [((rows, half), f32), ((8, rows), f32)],
        [(SMEM, order), (SMEM, exits), (VMEM, cotangent), (VMEM, gain), (VMEM, keep), (VMEM, got),
         (VMEM, kept), (VMEM, sent)],
    )


def iteration0(gain, keep, got, sums, others, carried, inner, inner_other, delta1, gain1, features):
    rows, half = keep.shape

    def kernel(gain_ref, keep_ref, got_ref, sums_ref, others_ref, carried_ref, inner_ref, other_ref,
               delta1_ref, gain1_ref, total_ref, db_ref):
        sec = lax.axis_index("section")
        squares = to_columns(sums_ref[...] + others_ref[...])[:, 2:3]
        inner = to_columns(inner_ref[...] + other_ref[...])[:, 0:1]
        pre = jnp.where(sec == 0, keep_ref[...], got_ref[...])
        carried = carried_ref[...]
        normed, delta = delta_of(pre, carried * gain_ref[...], squares, inner, features)
        total_ref[:rows] = delta + delta1_ref[...]
        gains = jnp.sum(carried * normed, axis=0, keepdims=True) + gain1_ref[...]
        total_ref[rows:] = jnp.broadcast_to(gains, (8, half))
        db_ref[...] = delta.astype(bf16)

    values = [gain, keep, got, sums, others, carried, inner, inner_other, delta1, gain1]
    return call(
        kernel,
        [((rows + 8, half), f32), ((rows, half), bf16)],
        [(VMEM, value) for value in values],
    )


def other_slot(columns, rows):
    height = columns[0].shape[0]

    def kernel(*refs):
        for k in range(2):

            @pl.when(lax.axis_index("section") == k)
            def _():
                for chip, ref in enumerate(refs[:-1]):
                    refs[-1][chip] = ref[:, (1 - k) * rows : (2 - k) * rows]

    outs = [((len(columns), height, rows), bf16)]
    return call(kernel, outs, [(VMEM, value) for value in columns])[0]


def left_side(columns, others):
    height, rows = others.shape[1:]
    group = len(columns)

    def kernel(*refs):
        own_refs, others_ref, out_ref = refs[:group], refs[group], refs[group + 1]
        for k in range(2):

            @pl.when(lax.axis_index("section") == k)
            def _():
                for chip in range(group):
                    own = slice((k * group + chip) * rows, (k * group + chip + 1) * rows)
                    out_ref[:, own] = own_refs[chip][:, k * rows : (k + 1) * rows]
                    base = ((1 - k) * group + chip) * rows
                    out_ref[:, base : base + rows] = others_ref[chip]

    values = [*columns, others]
    return call(
        kernel, [((height, 2 * group * rows), bf16)], [(VMEM, value) for value in values]
    )[0]


def weight_terms(left, grads, lanes):
    rows = grads[0].shape[0]
    height = left.shape[0]
    start, width = lanes

    def kernel(left_ref, *refs):
        grads_refs, (keep_ref, send_ref, right) = refs[:-3], refs[-3:]
        for index, grads_ref in enumerate(grads_refs):
            right[index * rows : (index + 1) * rows] = grads_ref[:, start : start + width]
        for k, (first, second) in enumerate([(keep_ref, send_ref), (send_ref, keep_ref)]):

            @pl.when(lax.axis_index("section") == k)
            def _():
                terms = jnp.dot(left_ref[...], right[...], preferred_element_type=f32)
                first[...] = terms[: height // 2]
                second[...] = terms[height // 2 :]

    return call(
        kernel,
        [((height // 2, width), f32)] * 2,
        [(VMEM, value) for value in [left, *grads]],
        [pltpu.VMEM((len(grads) * rows, width), bf16)],
    )


def chip_sum(keep, other, block):
    height, width = keep.shape

    def kernel(keep_ref, other_ref, own_ref, *away_refs):
        total = keep_ref[...] + other_ref[...]
        own_ref[...] = total[:block]
        for index, away_ref in enumerate(away_refs):
            away_ref[...] = total[(index + 1) * block : (index + 2) * block].astype(bf16)

    outs = [((block, width), f32)] + [((block, width), bf16)] * (height // block - 1)
    return call(kernel, outs, [(VMEM, keep), (VMEM, other)])


def final_sum(own, others, half):
    block = own[0].shape[0]
    count = len(others[0])

    def kernel(*refs):
        start = 0
        for part in range(len(own)):
            own_ref, *other_refs = refs[part * (count + 1) : (part + 1) * (count + 1)]
            total = own_ref[...]
            for other_ref in other_refs:
                total = total + other_ref[...].astype(f32)
            width = own_ref.shape[1]
            refs[-1][:, start : start + width] = total
            start += width

    values = [value for mine, theirs in zip(own, others) for value in (mine, *theirs)]
    return call(kernel, [((block, half), f32)], [(VMEM, value) for value in values])[0]


def place(order, total, other, rows):
    half = total.shape[1]

    def kernel(order_ref, total_ref, other_ref, out_ref):
        micro = order_ref[0, lax.axis_index("section")]
        out_ref[micro] = total_ref[:rows]
        out_ref[1 - micro] = other_ref[:rows]

    ins = [(SMEM, order), (VMEM, total), (VMEM, other)]
    return call(kernel, [((2, rows, half), f32)], ins)[0]


def shards(states, injection, cotangent, gain, weight, exits, order):
    stash = states[0]
    slots, rows, features = stash.shape
    half = weight.shape[1]
    dp = lax.axis_index("dp")
    chips = lax.axis_size("dp")
    group = 4
    groups = chips // group
    assert slots == 2 and lax.axis_size("section") == 2 and lax.axis_size("mp") == 2
    assert chips % group == 0 and groups & (groups - 1) == 0

    def across(value, distance):
        return lax.ppermute(value, "dp", [(i, i ^ distance) for i in range(chips)])

    def gathered(value):
        return [value] + [across(value, distance) for distance in range(1, group)]

    block = features // (2 * chips)
    turned = stash.reshape(slots * rows, features).T.reshape(2, chips, block, slots * rows)

    def columns_for(chip):
        picked = [
            lax.dynamic_index_in_dim(turned, chip ^ (group * other), 1, keepdims=False)
            for other in range(groups)
        ]
        return jnp.stack(picked, axis=1).reshape(2 * groups * block, slots * rows)

    pieces = [columns_for(dp ^ distance) for distance in range(group)]
    stash, pieces = lax.optimization_barrier((stash, pieces))
    columns = pieces[:1] + [across(pieces[distance], distance) for distance in range(1, group)]

    gain = gain.reshape(1, half)
    keep, send = forward(stash, weight, injection, order)
    got = swap(send, "section")
    sums = row_sums(order, cotangent, gain, keep, got)
    others = swap(sums, "mp")
    db1, delta1, gain1, away = lower_iteration1(
        order, exits, cotangent, gain, keep, got, sums, others, weight
    )
    sent = swap(away, "mp")
    grads1 = gathered(db1)
    kept = kept_half(db1, weight)
    kept, sent, columns, grads1[1:3] = lax.optimization_barrier((kept, sent, columns, grads1[1:3]))

    theirs = swap(other_slot(columns, rows), "section")
    carried, inner = carry(order, exits, cotangent, gain, keep, got, kept, sent)
    inner_other = swap(inner, "mp")
    inner_other, theirs = lax.optimization_barrier((inner_other, theirs))
    total, db0 = iteration0(
        gain, keep, got, sums, others, carried, inner, inner_other, delta1, gain1, features
    )
    grads0 = gathered(db0)
    left = left_side(columns, theirs)

    other = swap(total, "section")
    d_injection = place(order, total, other, rows)

    d_gain = total[rows:] + other[rows:]
    distance = 1
    while distance < chips:
        d_gain = d_gain + across(d_gain, distance)
        distance *= 2
    d_gain = d_gain[0]

    left, grads0, grads1, d_gain, d_injection = lax.optimization_barrier(
        (left, grads0, grads1, d_gain, d_injection)
    )
    cut = (half // 2 + 127) // 128 * 128
    own, others = [], []
    for lanes in [(0, cut), (cut, half - cut)]:
        keep, send = weight_terms(left, grads0 + grads1, lanes)
        mine, *aways = chip_sum(keep, swap(send, "section"), block)
        own.append(mine)
        others.append([across(away, group * (i + 1)) for i, away in enumerate(aways)])
    d_weight = final_sum(own, others, half)
    return (d_injection, d_weight, d_gain)


def solution(mesh):
    return jax.shard_map(
        shards,
        mesh=mesh,
        in_specs=(
            P("section", "dp", None, None),
            P("dp", None, "mp"),
            P("dp", None, "mp"),
            P("mp"),
            P(None, "mp"),
            P("dp"),
            P("dp", None),
        ),
        out_specs=(P("dp", None, "mp"), P(("section", "dp"), "mp"), P("mp")),
        check_vma=False,
    )
```

```python
import jax
import jax.numpy as jnp
from jax import lax
from jax.experimental import pallas as pl
from jax.experimental.pallas import tpu as pltpu
from jax.sharding import PartitionSpec as P

epsilon = 1e-06
f32, bf16 = jnp.float32, jnp.bfloat16
VMEM = pl.BlockSpec(memory_space=pltpu.VMEM)
SMEM = pl.BlockSpec(memory_space=pltpu.SMEM)
ANY = pl.BlockSpec(memory_space=pl.ANY)


def call(kernel, outs, ins, scratch=(), limit=24):
    shapes = [jax.ShapeDtypeStruct(shape, kind) for shape, kind in outs]
    specs, values = zip(*ins)
    return pl.pallas_call(
        kernel,
        out_shape=shapes,
        in_specs=list(specs),
        out_specs=[VMEM] * len(shapes),
        scratch_shapes=list(scratch),
        compiler_params=pltpu.CompilerParams(vmem_limit_bytes=limit * 2**20),
        cost_estimate=pl.CostEstimate(flops=1000, bytes_accessed=1000, transcendentals=0),
    )(*values)


def swap(value, axis):
    return lax.ppermute(value, axis, [(0, 1), (1, 0)])


def chunks_of(total, size):
    return [(start, min(size, total - start)) for start in range(0, total, size)]


def to_rows(columns):
    rows = columns[0].shape[0]
    lane = lax.broadcasted_iota(jnp.int32, (rows, 128), 1)
    wide = jnp.zeros((rows, 128), f32)
    for index, column in enumerate(columns):
        wide = jnp.where(lane == index, column, wide)
    return wide.T[:8]


def to_columns(packed):
    return jnp.concatenate([packed] * 16, axis=0).T


def forward(stash, weight, injection, order):
    slots, rows, features = stash.shape
    half = weight.shape[1]

    def kernel(order_ref, stash_ref, weight_ref, inj_ref, keep_ref, send_ref, acc):
        sec = lax.axis_index("section")
        left = stash_ref[...].reshape(slots * rows, features)
        for start, size in chunks_of(half, 512):
            part = slice(start, start + size)
            term = jnp.dot(left, weight_ref[:, part], preferred_element_type=f32)
            acc[:, :, part] = term.reshape(slots, rows, size)
        keep_ref[...] = acc[sec] + inj_ref[order_ref[0, sec]].astype(f32)
        send_ref[...] = acc[1 - sec] + inj_ref[order_ref[0, 1 - sec]].astype(f32)

    return call(
        kernel,
        [((rows, half), f32)] * 2,
        [(SMEM, order), (VMEM, stash), (VMEM, weight), (VMEM, injection)],
        [pltpu.VMEM((slots, rows, half), f32)],
    )


def row_sums(order, cotangent, gain, keep, got):
    rows = keep.shape[0]

    def kernel(order_ref, cot_ref, gain_ref, keep_ref, got_ref, out_ref):
        sec = lax.axis_index("section")
        first = sec == 0
        keep, got = keep_ref[...], got_ref[...]
        pre1, pre0 = jnp.where(first, got, keep), jnp.where(first, keep, got)
        u = cot_ref[order_ref[0, sec]].astype(f32) * gain_ref[...]
        sums = [pre1 * pre1, u * pre1, pre0 * pre0]
        out_ref[...] = to_rows([jnp.sum(each, axis=1, keepdims=True) for each in sums])

    ins = [(SMEM, order), (VMEM, cotangent), (VMEM, gain), (VMEM, keep), (VMEM, got)]
    return call(kernel, [((8, rows), f32)], ins)[0]


def delta_of(pre, u, squares, inner, features):
    radius = jnp.sqrt(squares / features + epsilon)
    inverse = 1.0 / radius
    normed = pre * inverse
    return normed, (u - normed * (inner * inverse / features)) * inverse


def lower_iteration1(order, exits, cotangent, gain, keep, got, sums, others, weight):
    rows, half = keep.shape
    features = weight.shape[0]

    def kernel(order_ref, exits_ref, cot_ref, gain_ref, keep_ref, got_ref, sums_ref, others_ref,
               weight_ref, db_ref, delta_ref, gain_out, away_ref):
        sec, mp = lax.axis_index("section"), lax.axis_index("mp")
        micro = order_ref[0, sec]
        live = jnp.where(exits_ref[micro] > 1, 1.0, 0.0)
        stats = to_columns(sums_ref[...] + others_ref[...])
        pre = jnp.where(sec == 0, got_ref[...], keep_ref[...])
        cot = cot_ref[micro].astype(f32)
        normed, delta = delta_of(pre, cot * gain_ref[...], stats[:, 0:1], stats[:, 1:2], features)
        delta = delta * live
        delta_ref[...] = delta
        db = delta.astype(bf16)
        db_ref[...] = db
        gain_out[...] = jnp.sum(cot * normed, axis=0, keepdims=True) * live
        part = weight_ref[pl.ds(pl.multiple_of((1 - mp) * half, 128), half)]
        away_ref[...] = lax.dot_general(
            part, db, (((1,), (1,)), ((), ())), preferred_element_type=f32
        ).astype(bf16)

    return call(
        kernel,
        [((rows, half), bf16), ((rows, half), f32), ((1, half), f32), ((half, rows), bf16)],
        [(SMEM, order), (SMEM, exits), (VMEM, cotangent), (VMEM, gain), (VMEM, keep), (VMEM, got),
         (VMEM, sums), (VMEM, others), (VMEM, weight)],
    )


def kept_half(db, weight):
    rows, half = db.shape

    def kernel(db_ref, weight_ref, out_ref):
        part = weight_ref[pl.ds(pl.multiple_of(lax.axis_index("mp") * half, 128), half)]
        out_ref[...] = lax.dot_general(
            part, db_ref[...], (((1,), (1,)), ((), ())), preferred_element_type=f32
        )

    return call(kernel, [((half, rows), f32)], [(VMEM, db), (VMEM, weight)])[0]


def carry(order, exits, cotangent, gain, keep, got, kept, sent):
    rows, half = keep.shape

    def kernel(order_ref, exits_ref, cot_ref, gain_ref, keep_ref, got_ref, kept_ref, sent_ref,
               carried_ref, inner_ref):
        sec = lax.axis_index("section")
        micro = order_ref[0, sec]
        passed = (kept_ref[...] + sent_ref[...].astype(f32)).astype(bf16).astype(f32).T
        cot = cot_ref[micro].astype(f32)
        carried = jnp.where(exits_ref[micro] > 1, passed, cot)
        carried_ref[...] = carried
        pre = jnp.where(sec == 0, keep_ref[...], got_ref[...])
        inner = jnp.sum(carried * gain_ref[...] * pre, axis=1, keepdims=True)
        inner_ref[...] = to_rows([inner])

    return call(
        kernel,
        [((rows, half), f32), ((8, rows), f32)],
        [(SMEM, order), (SMEM, exits), (VMEM, cotangent), (VMEM, gain), (VMEM, keep), (VMEM, got),
         (VMEM, kept), (VMEM, sent)],
    )


def iteration0(gain, keep, got, sums, others, carried, inner, inner_other, delta1, gain1, features):
    rows, half = keep.shape

    def kernel(gain_ref, keep_ref, got_ref, sums_ref, others_ref, carried_ref, inner_ref, other_ref,
               delta1_ref, gain1_ref, total_ref, db_ref):
        sec = lax.axis_index("section")
        squares = to_columns(sums_ref[...] + others_ref[...])[:, 2:3]
        inner = to_columns(inner_ref[...] + other_ref[...])[:, 0:1]
        pre = jnp.where(sec == 0, keep_ref[...], got_ref[...])
        carried = carried_ref[...]
        normed, delta = delta_of(pre, carried * gain_ref[...], squares, inner, features)
        total_ref[:rows] = delta + delta1_ref[...]
        gains = jnp.sum(carried * normed, axis=0, keepdims=True) + gain1_ref[...]
        total_ref[rows:] = jnp.broadcast_to(gains, (8, half))
        db_ref[...] = delta.astype(bf16)

    values = [gain, keep, got, sums, others, carried, inner, inner_other, delta1, gain1]
    return call(
        kernel,
        [((rows + 8, half), f32), ((rows, half), bf16)],
        [(VMEM, value) for value in values],
    )


def other_slot(columns, rows):
    height = columns[0].shape[0]

    def kernel(*refs):
        for k in range(2):

            @pl.when(lax.axis_index("section") == k)
            def _():
                for chip, ref in enumerate(refs[:-1]):
                    refs[-1][chip] = ref[:, (1 - k) * rows : (2 - k) * rows]

    outs = [((len(columns), height, rows), bf16)]
    return call(kernel, outs, [(VMEM, value) for value in columns])[0]


def left_side(columns, others):
    height, rows = others.shape[1:]
    group = len(columns)

    def kernel(*refs):
        own_refs, others_ref, out_ref = refs[:group], refs[group], refs[group + 1]
        for k in range(2):

            @pl.when(lax.axis_index("section") == k)
            def _():
                for chip in range(group):
                    own = slice((k * group + chip) * rows, (k * group + chip + 1) * rows)
                    out_ref[:, own] = own_refs[chip][:, k * rows : (k + 1) * rows]
                    base = ((1 - k) * group + chip) * rows
                    out_ref[:, base : base + rows] = others_ref[chip]

    values = [*columns, others]
    return call(
        kernel, [((height, 2 * group * rows), bf16)], [(VMEM, value) for value in values]
    )[0]


def weight_terms(left, grads, lanes):
    rows = grads[0].shape[0]
    height = left.shape[0]
    start, width = lanes

    def kernel(left_ref, *refs):
        grads_refs, (keep_ref, send_ref, right) = refs[:-3], refs[-3:]
        for index, grads_ref in enumerate(grads_refs):
            right[index * rows : (index + 1) * rows] = grads_ref[:, start : start + width]
        for k, (first, second) in enumerate([(keep_ref, send_ref), (send_ref, keep_ref)]):

            @pl.when(lax.axis_index("section") == k)
            def _():
                terms = jnp.dot(left_ref[...], right[...], preferred_element_type=f32)
                first[...] = terms[: height // 2]
                second[...] = terms[height // 2 :]

    return call(
        kernel,
        [((height // 2, width), f32)] * 2,
        [(VMEM, value) for value in [left, *grads]],
        [pltpu.VMEM((len(grads) * rows, width), bf16)],
    )


def chip_sum(keep, other, block):
    height, width = keep.shape

    def kernel(keep_ref, other_ref, own_ref, *away_refs):
        total = keep_ref[...] + other_ref[...]
        own_ref[...] = total[:block]
        for index, away_ref in enumerate(away_refs):
            away_ref[...] = total[(index + 1) * block : (index + 2) * block].astype(bf16)

    outs = [((block, width), f32)] + [((block, width), bf16)] * (height // block - 1)
    return call(kernel, outs, [(VMEM, keep), (VMEM, other)])


def final_sum(own, others, half):
    block = own[0].shape[0]
    count = len(others[0])

    def kernel(*refs):
        start = 0
        for part in range(len(own)):
            own_ref, *other_refs = refs[part * (count + 1) : (part + 1) * (count + 1)]
            total = own_ref[...]
            for other_ref in other_refs:
                total = total + other_ref[...].astype(f32)
            width = own_ref.shape[1]
            refs[-1][:, start : start + width] = total
            start += width

    values = [value for mine, theirs in zip(own, others) for value in (mine, *theirs)]
    return call(kernel, [((block, half), f32)], [(VMEM, value) for value in values])[0]


def place(order, total, other, rows):
    half = total.shape[1]

    def kernel(order_ref, total_ref, other_ref, out_ref):
        micro = order_ref[0, lax.axis_index("section")]
        out_ref[micro] = total_ref[:rows]
        out_ref[1 - micro] = other_ref[:rows]

    ins = [(SMEM, order), (VMEM, total), (VMEM, other)]
    return call(kernel, [((2, rows, half), f32)], ins)[0]


def shards(states, injection, cotangent, gain, weight, exits, order):
    stash = states[0]
    slots, rows, features = stash.shape
    half = weight.shape[1]
    dp = lax.axis_index("dp")
    chips = lax.axis_size("dp")
    group = 4
    groups = chips // group
    assert slots == 2 and lax.axis_size("section") == 2 and lax.axis_size("mp") == 2
    assert chips % group == 0 and groups & (groups - 1) == 0

    def across(value, distance):
        return lax.ppermute(value, "dp", [(i, i ^ distance) for i in range(chips)])

    def gathered(value):
        return [value] + [across(value, distance) for distance in range(1, group)]

    block = features // (2 * chips)
    turned = stash.reshape(slots * rows, features).T.reshape(2, chips, block, slots * rows)

    def columns_for(chip):
        picked = [
            lax.dynamic_index_in_dim(turned, chip ^ (group * other), 1, keepdims=False)
            for other in range(groups)
        ]
        return jnp.stack(picked, axis=1).reshape(2 * groups * block, slots * rows)

    pieces = [columns_for(dp ^ distance) for distance in range(group)]
    stash, pieces = lax.optimization_barrier((stash, pieces))
    columns = pieces[:1] + [across(pieces[distance], distance) for distance in range(1, group)]

    gain = gain.reshape(1, half)
    keep, send = forward(stash, weight, injection, order)
    got = swap(send, "section")
    sums = row_sums(order, cotangent, gain, keep, got)
    others = swap(sums, "mp")
    db1, delta1, gain1, away = lower_iteration1(
        order, exits, cotangent, gain, keep, got, sums, others, weight
    )
    sent = swap(away, "mp")
    grads1 = gathered(db1)
    kept = kept_half(db1, weight)
    kept, sent, columns, grads1[1:3] = lax.optimization_barrier((kept, sent, columns, grads1[1:3]))

    theirs = swap(other_slot(columns, rows), "section")
    carried, inner = carry(order, exits, cotangent, gain, keep, got, kept, sent)
    inner_other = swap(inner, "mp")
    inner_other, theirs, grads1[3] = lax.optimization_barrier((inner_other, theirs, grads1[3]))
    total, db0 = iteration0(
        gain, keep, got, sums, others, carried, inner, inner_other, delta1, gain1, features
    )
    grads0 = gathered(db0)
    left = left_side(columns, theirs)
    left, grads0, total = lax.optimization_barrier((left, grads0, total))
    other = swap(total, "section")

    d_gain = total[rows:] + other[rows:]
    distance = group
    while distance < chips:
        d_gain = d_gain + across(d_gain, distance)
        distance *= 2
    cut = (half // 2 + 127) // 128 * 128
    own, others = [], []
    for part, lanes in enumerate([(0, cut), (cut, half - cut)]):
        keep, send = weight_terms(left, grads0 + grads1, lanes)
        mine, *aways = chip_sum(keep, swap(send, "section"), block)
        aways, d_gain, total, other = lax.optimization_barrier((aways, d_gain, total, other))
        own.append(mine)
        others.append([across(away, group * (i + 1)) for i, away in enumerate(aways)])
    d_weight = final_sum(own, others, half)
    first, second, third = (across(d_gain, distance) for distance in range(1, group))
    d_gain = (d_gain + first) + (second + third)
    d_injection = place(order, total, other, rows)
    return (d_injection, d_weight, d_gain[0])


def solution(mesh):
    return jax.shard_map(
        shards,
        mesh=mesh,
        in_specs=(
            P("section", "dp", None, None),
            P("dp", None, "mp"),
            P("dp", None, "mp"),
            P("mp"),
            P(None, "mp"),
            P("dp"),
            P("dp", None),
        ),
        out_specs=(P("dp", None, "mp"), P(("section", "dp"), "mp"), P("mp")),
        check_vma=False,
    )
```

```python
import jax
import jax.numpy as jnp
from jax import lax
from jax.experimental import pallas as pl
from jax.experimental.pallas import tpu as pltpu
from jax.sharding import PartitionSpec as P

epsilon = 1e-06
f32, bf16 = jnp.float32, jnp.bfloat16
VMEM = pl.BlockSpec(memory_space=pltpu.VMEM)
SMEM = pl.BlockSpec(memory_space=pltpu.SMEM)
ANY = pl.BlockSpec(memory_space=pl.ANY)


def call(kernel, outs, ins, scratch=(), limit=24):
    shapes = [jax.ShapeDtypeStruct(shape, kind) for shape, kind in outs]
    specs, values = zip(*ins)
    return pl.pallas_call(
        kernel,
        out_shape=shapes,
        in_specs=list(specs),
        out_specs=[VMEM] * len(shapes),
        scratch_shapes=list(scratch),
        compiler_params=pltpu.CompilerParams(vmem_limit_bytes=limit * 2**20),
        cost_estimate=pl.CostEstimate(flops=1000, bytes_accessed=1000, transcendentals=0),
    )(*values)


def swap(value, axis):
    return lax.ppermute(value, axis, [(0, 1), (1, 0)])


def chunks_of(total, size):
    return [(start, min(size, total - start)) for start in range(0, total, size)]


def to_rows(columns):
    rows = columns[0].shape[0]
    lane = lax.broadcasted_iota(jnp.int32, (rows, 128), 1)
    wide = jnp.zeros((rows, 128), f32)
    for index, column in enumerate(columns):
        wide = jnp.where(lane == index, column, wide)
    return wide.T[:8]


def to_columns(packed):
    return jnp.concatenate([packed] * 16, axis=0).T


def load(stash, weight, chips, group):
    slots, rows, features = stash.shape
    block = features // (2 * chips)
    groups = chips // group
    height = 2 * groups * block
    parts = chunks_of(features, 512)

    def kernel(stash_hbm, weight_hbm, w, *refs):
        *out_refs, x, turned, sems = refs
        copy = pltpu.make_async_copy(stash_hbm.at[lax.axis_index("mp")], x, sems.at[len(parts)])
        copy.start()
        copies = []
        for index, (start, size) in enumerate(parts):
            part = pl.ds(start, size)
            copies.append(pltpu.make_async_copy(weight_hbm.at[part], w.at[part], sems.at[index]))
            copies[-1].start()
        copy.wait()
        turned[...] = x[...].T
        dp = lax.axis_index("dp")
        for distance, out_ref in enumerate(out_refs):
            for half in range(2):
                for other in range(groups):
                    chip = dp ^ (distance + group * other)
                    source = pl.multiple_of((half * chips + chip) * block, 16)
                    base = (half * groups + other) * block
                    out_ref[base : base + block] = turned[pl.ds(source, block)]
        for each in copies:
            each.wait()

    pieces = group if block % 16 == 0 else 0
    weight, *columns = call(
        kernel,
        [(weight.shape, bf16)] + [((height, rows), bf16)] * pieces,
        [(ANY, stash), (ANY, weight)],
        [
            pltpu.VMEM((rows, features), bf16),
            pltpu.VMEM((features, rows), bf16),
            pltpu.SemaphoreType.DMA((len(parts) + 1,)),
        ],
        limit=42,
    )
    if not columns:
        turned = lax.dynamic_index_in_dim(stash, lax.axis_index("mp"), 0, keepdims=False).T
        turned = turned.reshape(2, chips, block, rows)
        for distance in range(group):
            picked = [
                lax.dynamic_index_in_dim(
                    turned, lax.axis_index("dp") ^ (distance + group * other), 1, keepdims=False
                )
                for other in range(groups)
            ]
            columns.append(jnp.stack(picked, axis=1).reshape(height, rows))
    return weight, columns


def forward(stash, weight, injection, order):
    slots, rows, features = stash.shape
    half = weight.shape[1]

    def kernel(order_ref, stash_ref, weight_ref, inj_ref, keep_ref, send_ref, acc):
        sec = lax.axis_index("section")
        left = stash_ref[...].reshape(slots * rows, features)
        for start, size in chunks_of(half, 512):
            part = slice(start, start + size)
            term = jnp.dot(left, weight_ref[:, part], preferred_element_type=f32)
            acc[:, :, part] = term.reshape(slots, rows, size)
        keep_ref[...] = acc[sec] + inj_ref[order_ref[0, sec]].astype(f32)
        send_ref[...] = acc[1 - sec] + inj_ref[order_ref[0, 1 - sec]].astype(f32)

    return call(
        kernel,
        [((rows, half), f32)] * 2,
        [(SMEM, order), (VMEM, stash), (VMEM, weight), (VMEM, injection)],
        [pltpu.VMEM((slots, rows, half), f32)],
    )


def row_sums(order, cotangent, gain, keep, got):
    rows = keep.shape[0]

    def kernel(order_ref, cot_ref, gain_ref, keep_ref, got_ref, out_ref):
        sec = lax.axis_index("section")
        first = sec == 0
        keep, got = keep_ref[...], got_ref[...]
        pre1, pre0 = jnp.where(first, got, keep), jnp.where(first, keep, got)
        u = cot_ref[order_ref[0, sec]].astype(f32) * gain_ref[...]
        sums = [pre1 * pre1, u * pre1, pre0 * pre0]
        out_ref[...] = to_rows([jnp.sum(each, axis=1, keepdims=True) for each in sums])

    ins = [(SMEM, order), (VMEM, cotangent), (VMEM, gain), (VMEM, keep), (VMEM, got)]
    return call(kernel, [((8, rows), f32)], ins)[0]


def delta_of(pre, u, squares, inner, features):
    radius = jnp.sqrt(squares / features + epsilon)
    inverse = 1.0 / radius
    normed = pre * inverse
    return normed, (u - normed * (inner * inverse / features)) * inverse


def lower_iteration1(order, exits, cotangent, gain, keep, got, sums, others, weight):
    rows, half = keep.shape
    features = weight.shape[0]

    def kernel(order_ref, exits_ref, cot_ref, gain_ref, keep_ref, got_ref, sums_ref, others_ref,
               weight_ref, db_ref, delta_ref, gain_out, away_ref):
        sec, mp = lax.axis_index("section"), lax.axis_index("mp")
        micro = order_ref[0, sec]
        live = jnp.where(exits_ref[micro] > 1, 1.0, 0.0)
        stats = to_columns(sums_ref[...] + others_ref[...])
        pre = jnp.where(sec == 0, got_ref[...], keep_ref[...])
        cot = cot_ref[micro].astype(f32)
        normed, delta = delta_of(pre, cot * gain_ref[...], stats[:, 0:1], stats[:, 1:2], features)
        delta = delta * live
        delta_ref[...] = delta
        db = delta.astype(bf16)
        db_ref[...] = db
        gain_out[...] = jnp.sum(cot * normed, axis=0, keepdims=True) * live
        part = weight_ref[pl.ds(pl.multiple_of((1 - mp) * half, 128), half)]
        away_ref[...] = lax.dot_general(
            part, db, (((1,), (1,)), ((), ())), preferred_element_type=f32
        ).astype(bf16)

    return call(
        kernel,
        [((rows, half), bf16), ((rows, half), f32), ((1, half), f32), ((half, rows), bf16)],
        [(SMEM, order), (SMEM, exits), (VMEM, cotangent), (VMEM, gain), (VMEM, keep), (VMEM, got),
         (VMEM, sums), (VMEM, others), (VMEM, weight)],
    )


def kept_half(db, weight):
    rows, half = db.shape

    def kernel(db_ref, weight_ref, out_ref):
        part = weight_ref[pl.ds(pl.multiple_of(lax.axis_index("mp") * half, 128), half)]
        out_ref[...] = lax.dot_general(
            part, db_ref[...], (((1,), (1,)), ((), ())), preferred_element_type=f32
        )

    return call(kernel, [((half, rows), f32)], [(VMEM, db), (VMEM, weight)])[0]


def carry(order, exits, cotangent, gain, keep, got, sums, others, kept, sent, gain1, features):
    rows, half = keep.shape

    def kernel(order_ref, exits_ref, cot_ref, gain_ref, keep_ref, got_ref, sums_ref, others_ref,
               kept_ref, sent_ref, gain1_ref, carried_ref, inner_ref, gain_out):
        sec = lax.axis_index("section")
        micro = order_ref[0, sec]
        passed = (kept_ref[...] + sent_ref[...].astype(f32)).astype(bf16).astype(f32).T
        cot = cot_ref[micro].astype(f32)
        carried = jnp.where(exits_ref[micro] > 1, passed, cot)
        carried_ref[...] = carried
        pre = jnp.where(sec == 0, keep_ref[...], got_ref[...])
        inner = jnp.sum(carried * gain_ref[...] * pre, axis=1, keepdims=True)
        inner_ref[...] = to_rows([inner])
        squares = to_columns(sums_ref[...] + others_ref[...])[:, 2:3]
        inverse = 1.0 / jnp.sqrt(squares / features + epsilon)
        gains = jnp.sum(carried * (pre * inverse), axis=0, keepdims=True) + gain1_ref[...]
        gain_out[...] = jnp.broadcast_to(gains, (8, half))

    return call(
        kernel,
        [((rows, half), f32), ((8, rows), f32), ((8, half), f32)],
        [(SMEM, order), (SMEM, exits)]
        + [
            (VMEM, value)
            for value in (cotangent, gain, keep, got, sums, others, kept, sent, gain1)
        ],
    )


def iteration0(gain, keep, got, sums, others, carried, inner, inner_other, delta1, features):
    rows, half = keep.shape

    def kernel(gain_ref, keep_ref, got_ref, sums_ref, others_ref, carried_ref, inner_ref, other_ref,
               delta1_ref, total_ref, db_ref):
        sec = lax.axis_index("section")
        squares = to_columns(sums_ref[...] + others_ref[...])[:, 2:3]
        inner = to_columns(inner_ref[...] + other_ref[...])[:, 0:1]
        pre = jnp.where(sec == 0, keep_ref[...], got_ref[...])
        _, delta = delta_of(pre, carried_ref[...] * gain_ref[...], squares, inner, features)
        total_ref[...] = delta + delta1_ref[...]
        db_ref[...] = delta.astype(bf16)

    values = [gain, keep, got, sums, others, carried, inner, inner_other, delta1]
    return call(
        kernel,
        [((rows, half), f32), ((rows, half), bf16)],
        [(VMEM, value) for value in values],
    )


def stacked(columns):
    def kernel(*refs):
        for chip, ref in enumerate(refs[:-1]):
            refs[-1][chip] = ref[...]

    outs = [((len(columns), *columns[0].shape), bf16)]
    return call(kernel, outs, [(VMEM, value) for value in columns])[0]


def left_side(columns, near, far):
    group, height, rows = columns.shape

    def kernel(own_ref, near_ref, far_ref, out_ref):
        place = 2 * lax.axis_index("section") + lax.axis_index("mp")
        sources = [(own_ref, near_ref), (near_ref, far_ref), (far_ref, near_ref), (near_ref, own_ref)]
        for index, pair in enumerate(sources):

            @pl.when(place == index)
            def _():
                for k, ref in enumerate(pair):
                    for chip in range(group):
                        base = (k * group + chip) * rows
                        out_ref[:, base : base + rows] = ref[chip]

    return call(
        kernel,
        [((height, 2 * group * rows), bf16)],
        [(VMEM, value) for value in (columns, near, far)],
    )[0]


def weight_terms(left, grads, lanes):
    rows = grads[0].shape[0]
    height = left.shape[0]
    start, width = lanes

    def kernel(left_ref, *refs):
        grads_refs, (keep_ref, send_ref, right) = refs[:-3], refs[-3:]
        for index, grads_ref in enumerate(grads_refs):
            right[index * rows : (index + 1) * rows] = grads_ref[:, start : start + width]
        for k, (first, second) in enumerate([(keep_ref, send_ref), (send_ref, keep_ref)]):

            @pl.when(lax.axis_index("section") == k)
            def _():
                terms = jnp.dot(left_ref[...], right[...], preferred_element_type=f32)
                first[...] = terms[: height // 2]
                second[...] = terms[height // 2 :]

    return call(
        kernel,
        [((height // 2, width), f32)] * 2,
        [(VMEM, value) for value in [left, *grads]],
        [pltpu.VMEM((len(grads) * rows, width), bf16)],
    )


def chip_sum(keep, other, block):
    height, width = keep.shape

    def kernel(keep_ref, other_ref, own_ref, *away_refs):
        total = keep_ref[...] + other_ref[...]
        own_ref[...] = total[:block]
        for index, away_ref in enumerate(away_refs):
            away_ref[...] = total[(index + 1) * block : (index + 2) * block].astype(bf16)

    outs = [((block, width), f32)] + [((block, width), bf16)] * (height // block - 1)
    return call(kernel, outs, [(VMEM, keep), (VMEM, other)])


def final_sum(own, others, half):
    block = own[0].shape[0]
    count = len(others[0])

    def kernel(*refs):
        start = 0
        for part in range(len(own)):
            own_ref, *other_refs = refs[part * (count + 1) : (part + 1) * (count + 1)]
            total = own_ref[...]
            for other_ref in other_refs:
                total = total + other_ref[...].astype(f32)
            width = own_ref.shape[1]
            refs[-1][:, start : start + width] = total
            start += width

    values = [value for mine, theirs in zip(own, others) for value in (mine, *theirs)]
    return call(kernel, [((block, half), f32)], [(VMEM, value) for value in values])[0]


def place(order, total, other):
    rows, half = total.shape

    def kernel(order_ref, total_ref, other_ref, out_ref):
        micro = order_ref[0, lax.axis_index("section")]
        out_ref[micro] = total_ref[...]
        out_ref[1 - micro] = other_ref[...]

    ins = [(SMEM, order), (VMEM, total), (VMEM, other)]
    return call(kernel, [((2, rows, half), f32)], ins)[0]


def shards(states, injection, cotangent, gain, weight, exits, order):
    stash = states[0]
    slots, rows, features = stash.shape
    half = weight.shape[1]
    dp = lax.axis_index("dp")
    chips = lax.axis_size("dp")
    group = 4
    groups = chips // group
    assert slots == 2 and lax.axis_size("section") == 2 and lax.axis_size("mp") == 2
    assert chips % group == 0 and groups & (groups - 1) == 0

    def across(value, distance):
        return lax.ppermute(value, "dp", [(i, i ^ distance) for i in range(chips)])

    def gathered(value):
        return [value] + [across(value, distance) for distance in range(1, group)]

    block = features // (2 * chips)
    weight, columns = load(stash, weight, chips, group)
    columns = columns[:1] + [across(columns[distance], distance) for distance in range(1, group)]

    gain = gain.reshape(1, half)
    keep, send = forward(stash, weight, injection, order)
    got = swap(send, "section")
    sums = row_sums(order, cotangent, gain, keep, got)
    others = swap(sums, "mp")
    others, columns = lax.optimization_barrier((others, columns))
    db1, delta1, gain1, away = lower_iteration1(
        order, exits, cotangent, gain, keep, got, sums, others, weight
    )
    sent = swap(away, "mp")
    grads1 = gathered(db1)
    kept = kept_half(db1, weight)
    kept, sent, grads1[1:3] = lax.optimization_barrier((kept, sent, grads1[1:3]))

    carried, inner, gains = carry(
        order, exits, cotangent, gain, keep, got, sums, others, kept, sent, gain1, features
    )
    inner_other, gains_other = swap(inner, "mp"), swap(gains, "section")
    columns = stacked(columns)
    inner_other, gains_other, columns, grads1[3] = lax.optimization_barrier(
        (inner_other, gains_other, columns, grads1[3])
    )
    total, db0 = iteration0(
        gain, keep, got, sums, others, carried, inner, inner_other, delta1, features
    )
    grads0 = gathered(db0)
    columns, total = lax.optimization_barrier((columns, total))
    both = ("section", "mp")
    near = lax.ppermute(columns, both, [(2, 0), (0, 1), (3, 2), (1, 3)])
    far = lax.ppermute(columns, both, [(2, 1), (1, 2)])
    left = left_side(columns, near, far)

    d_gain = gains + gains_other
    distance = group
    while distance < chips:
        d_gain = d_gain + across(d_gain, distance)
        distance *= 2
    left, grads0, d_gain = lax.optimization_barrier((left, grads0, d_gain))

    cut = (half // 2 + 127) // 128 * 128
    terms = [
        weight_terms(left, grads0 + grads1, lanes) for lanes in [(0, cut), (cut, half - cut)]
    ]
    arrived = [swap(send, "section") for _, send in terms]
    own, others = [], []
    for part, (keep, _) in enumerate(terms):
        mine, *aways = chip_sum(keep, arrived[part], block)
        aways, d_gain, total, *arrived[part + 1 :] = lax.optimization_barrier(
            (aways, d_gain, total, *arrived[part + 1 :])
        )
        if part == 0:
            other = swap(total, "section")
        own.append(mine)
        others.append([across(away, group * (i + 1)) for i, away in enumerate(aways)])
    d_injection = place(order, total, other)
    others[1], d_injection = lax.optimization_barrier((others[1], d_injection))
    d_weight = final_sum(own, others, half)
    first, second, third = (across(d_gain, distance) for distance in range(1, group))
    d_gain = (d_gain + first) + (second + third)
    return (d_injection, d_weight, d_gain[0])


def solution(mesh):
    return jax.shard_map(
        shards,
        mesh=mesh,
        in_specs=(
            P("section", "dp", None, None),
            P("dp", None, "mp"),
            P("dp", None, "mp"),
            P("mp"),
            P(None, "mp"),
            P("dp"),
            P("dp", None),
        ),
        out_specs=(P("dp", None, "mp"), P(("section", "dp"), "mp"), P("mp")),
        check_vma=False,
    )
```

```python
import jax
import jax.numpy as jnp
from jax import lax
from jax.experimental import pallas as pl
from jax.experimental.pallas import tpu as pltpu
from jax.sharding import PartitionSpec as P

epsilon = 1e-06
f32, bf16 = jnp.float32, jnp.bfloat16
VMEM = pl.BlockSpec(memory_space=pltpu.VMEM)
SMEM = pl.BlockSpec(memory_space=pltpu.SMEM)
ANY = pl.BlockSpec(memory_space=pl.ANY)


def call(kernel, outs, ins, scratch=(), limit=24):
    shapes = [jax.ShapeDtypeStruct(shape, kind) for shape, kind in outs]
    specs, values = zip(*ins)
    return pl.pallas_call(
        kernel,
        out_shape=shapes,
        in_specs=list(specs),
        out_specs=[VMEM] * len(shapes),
        scratch_shapes=list(scratch),
        compiler_params=pltpu.CompilerParams(vmem_limit_bytes=limit * 2**20),
        cost_estimate=pl.CostEstimate(flops=1000, bytes_accessed=1000, transcendentals=0),
    )(*values)


def swap(value, axis):
    return lax.ppermute(value, axis, [(0, 1), (1, 0)])


def chunks_of(total, size):
    return [(start, min(size, total - start)) for start in range(0, total, size)]


def to_rows(columns):
    rows = columns[0].shape[0]
    lane = lax.broadcasted_iota(jnp.int32, (rows, 128), 1)
    wide = jnp.zeros((rows, 128), f32)
    for index, column in enumerate(columns):
        wide = jnp.where(lane == index, column, wide)
    return wide.T[:8]


def to_columns(packed):
    return jnp.concatenate([packed] * 16, axis=0).T


def load(stash, weight, chips, group):
    slots, rows, features = stash.shape
    block = features // (2 * chips)
    groups = chips // group
    height = 2 * groups * block
    parts = chunks_of(features, 512)

    def kernel(stash_hbm, weight_hbm, w, *refs):
        *out_refs, x, turned, sems = refs
        copy = pltpu.make_async_copy(stash_hbm.at[lax.axis_index("mp")], x, sems.at[len(parts)])
        copy.start()
        copies = []
        for index, (start, size) in enumerate(parts):
            part = pl.ds(start, size)
            copies.append(pltpu.make_async_copy(weight_hbm.at[part], w.at[part], sems.at[index]))
            copies[-1].start()
        copy.wait()
        turned[...] = x[...].T
        dp = lax.axis_index("dp")
        for distance, out_ref in enumerate(out_refs):
            for half in range(2):
                for other in range(groups):
                    chip = dp ^ (distance + group * other)
                    source = pl.multiple_of((half * chips + chip) * block, 16)
                    base = (half * groups + other) * block
                    out_ref[base : base + block] = turned[pl.ds(source, block)]
        for each in copies:
            each.wait()

    pieces = group if block % 16 == 0 else 0
    weight, *columns = call(
        kernel,
        [(weight.shape, bf16)] + [((height, rows), bf16)] * pieces,
        [(ANY, stash), (ANY, weight)],
        [
            pltpu.VMEM((rows, features), bf16),
            pltpu.VMEM((features, rows), bf16),
            pltpu.SemaphoreType.DMA((len(parts) + 1,)),
        ],
        limit=42,
    )
    if not columns:
        turned = lax.dynamic_index_in_dim(stash, lax.axis_index("mp"), 0, keepdims=False).T
        turned = turned.reshape(2, chips, block, rows)
        for distance in range(group):
            picked = [
                lax.dynamic_index_in_dim(
                    turned, lax.axis_index("dp") ^ (distance + group * other), 1, keepdims=False
                )
                for other in range(groups)
            ]
            columns.append(jnp.stack(picked, axis=1).reshape(height, rows))
    return weight, columns


def forward(stash, weight, injection, order):
    slots, rows, features = stash.shape
    half = weight.shape[1]

    def kernel(order_ref, stash_ref, weight_ref, inj_ref, keep_ref, send_ref, acc):
        sec = lax.axis_index("section")
        left = stash_ref[...].reshape(slots * rows, features)
        for start, size in chunks_of(half, 512):
            part = slice(start, start + size)
            term = jnp.dot(left, weight_ref[:, part], preferred_element_type=f32)
            acc[:, :, part] = term.reshape(slots, rows, size)
        keep_ref[...] = acc[sec] + inj_ref[order_ref[0, sec]].astype(f32)
        send_ref[...] = acc[1 - sec] + inj_ref[order_ref[0, 1 - sec]].astype(f32)

    return call(
        kernel,
        [((rows, half), f32)] * 2,
        [(SMEM, order), (VMEM, stash), (VMEM, weight), (VMEM, injection)],
        [pltpu.VMEM((slots, rows, half), f32)],
    )


def row_sums(order, cotangent, gain, keep, got):
    rows = keep.shape[0]

    def kernel(order_ref, cot_ref, gain_ref, keep_ref, got_ref, out_ref):
        sec = lax.axis_index("section")
        first = sec == 0
        keep, got = keep_ref[...], got_ref[...]
        pre1, pre0 = jnp.where(first, got, keep), jnp.where(first, keep, got)
        u = cot_ref[order_ref[0, sec]].astype(f32) * gain_ref[...]
        sums = [pre1 * pre1, u * pre1, pre0 * pre0]
        out_ref[...] = to_rows([jnp.sum(each, axis=1, keepdims=True) for each in sums])

    ins = [(SMEM, order), (VMEM, cotangent), (VMEM, gain), (VMEM, keep), (VMEM, got)]
    return call(kernel, [((8, rows), f32)], ins)[0]


def delta_of(pre, u, squares, inner, features):
    radius = jnp.sqrt(squares / features + epsilon)
    inverse = 1.0 / radius
    normed = pre * inverse
    return normed, (u - normed * (inner * inverse / features)) * inverse


def lower_iteration1(order, exits, cotangent, gain, keep, got, sums, others, weight):
    rows, half = keep.shape
    features = weight.shape[0]

    def kernel(order_ref, exits_ref, cot_ref, gain_ref, keep_ref, got_ref, sums_ref, others_ref,
               weight_ref, db_ref, delta_ref, gain_out, away_ref):
        sec, mp = lax.axis_index("section"), lax.axis_index("mp")
        micro = order_ref[0, sec]
        live = jnp.where(exits_ref[micro] > 1, 1.0, 0.0)
        stats = to_columns(sums_ref[...] + others_ref[...])
        pre = jnp.where(sec == 0, got_ref[...], keep_ref[...])
        cot = cot_ref[micro].astype(f32)
        normed, delta = delta_of(pre, cot * gain_ref[...], stats[:, 0:1], stats[:, 1:2], features)
        delta = delta * live
        delta_ref[...] = delta
        db = delta.astype(bf16)
        db_ref[...] = db
        gain_out[...] = jnp.sum(cot * normed, axis=0, keepdims=True) * live
        part = weight_ref[pl.ds(pl.multiple_of((1 - mp) * half, 128), half)]
        away_ref[...] = lax.dot_general(
            part, db, (((1,), (1,)), ((), ())), preferred_element_type=f32
        ).astype(bf16)

    return call(
        kernel,
        [((rows, half), bf16), ((rows, half), f32), ((1, half), f32), ((half, rows), bf16)],
        [(SMEM, order), (SMEM, exits), (VMEM, cotangent), (VMEM, gain), (VMEM, keep), (VMEM, got),
         (VMEM, sums), (VMEM, others), (VMEM, weight)],
    )


def kept_half(db, weight):
    rows, half = db.shape

    def kernel(db_ref, weight_ref, out_ref):
        part = weight_ref[pl.ds(pl.multiple_of(lax.axis_index("mp") * half, 128), half)]
        out_ref[...] = lax.dot_general(
            part, db_ref[...], (((1,), (1,)), ((), ())), preferred_element_type=f32
        )

    return call(kernel, [((half, rows), f32)], [(VMEM, db), (VMEM, weight)])[0]


def carry(order, exits, cotangent, gain, keep, got, sums, others, kept, sent, gain1, features):
    rows, half = keep.shape

    def kernel(order_ref, exits_ref, cot_ref, gain_ref, keep_ref, got_ref, sums_ref, others_ref,
               kept_ref, sent_ref, gain1_ref, carried_ref, inner_ref, gain_out):
        sec = lax.axis_index("section")
        micro = order_ref[0, sec]
        passed = (kept_ref[...] + sent_ref[...].astype(f32)).astype(bf16).astype(f32).T
        cot = cot_ref[micro].astype(f32)
        carried = jnp.where(exits_ref[micro] > 1, passed, cot)
        carried_ref[...] = carried
        pre = jnp.where(sec == 0, keep_ref[...], got_ref[...])
        inner = jnp.sum(carried * gain_ref[...] * pre, axis=1, keepdims=True)
        inner_ref[...] = to_rows([inner])
        squares = to_columns(sums_ref[...] + others_ref[...])[:, 2:3]
        inverse = 1.0 / jnp.sqrt(squares / features + epsilon)
        gains = jnp.sum(carried * (pre * inverse), axis=0, keepdims=True) + gain1_ref[...]
        gain_out[...] = jnp.broadcast_to(gains, (8, half))

    return call(
        kernel,
        [((rows, half), f32), ((8, rows), f32), ((8, half), f32)],
        [(SMEM, order), (SMEM, exits)]
        + [
            (VMEM, value)
            for value in (cotangent, gain, keep, got, sums, others, kept, sent, gain1)
        ],
    )


def iteration0(gain, keep, got, sums, others, carried, inner, inner_other, delta1, features):
    rows, half = keep.shape

    def kernel(gain_ref, keep_ref, got_ref, sums_ref, others_ref, carried_ref, inner_ref, other_ref,
               delta1_ref, total_ref, db_ref):
        sec = lax.axis_index("section")
        squares = to_columns(sums_ref[...] + others_ref[...])[:, 2:3]
        inner = to_columns(inner_ref[...] + other_ref[...])[:, 0:1]
        pre = jnp.where(sec == 0, keep_ref[...], got_ref[...])
        _, delta = delta_of(pre, carried_ref[...] * gain_ref[...], squares, inner, features)
        total_ref[...] = delta + delta1_ref[...]
        db_ref[...] = delta.astype(bf16)

    values = [gain, keep, got, sums, others, carried, inner, inner_other, delta1]
    return call(
        kernel,
        [((rows, half), f32), ((rows, half), bf16)],
        [(VMEM, value) for value in values],
    )


def stacked(columns):
    def kernel(*refs):
        for chip, ref in enumerate(refs[:-1]):
            refs[-1][chip] = ref[...]

    outs = [((len(columns), *columns[0].shape), bf16)]
    return call(kernel, outs, [(VMEM, value) for value in columns])[0]


def left_side(columns, near, far):
    group, height, rows = columns.shape

    def kernel(own_ref, near_ref, far_ref, out_ref):
        place = 2 * lax.axis_index("section") + lax.axis_index("mp")
        sources = [(own_ref, near_ref), (near_ref, far_ref), (far_ref, near_ref), (near_ref, own_ref)]
        for index, pair in enumerate(sources):

            @pl.when(place == index)
            def _():
                for k, ref in enumerate(pair):
                    for chip in range(group):
                        base = (k * group + chip) * rows
                        out_ref[:, base : base + rows] = ref[chip]

    return call(
        kernel,
        [((height, 2 * group * rows), bf16)],
        [(VMEM, value) for value in (columns, near, far)],
    )[0]


def weight_terms(left, grads, lanes):
    rows = grads[0].shape[0]
    height = left.shape[0]
    start, width = lanes

    def kernel(left_ref, *refs):
        grads_refs, (keep_ref, send_ref, right) = refs[:-3], refs[-3:]
        for index, grads_ref in enumerate(grads_refs):
            right[index * rows : (index + 1) * rows] = grads_ref[:, start : start + width]
        for k, (first, second) in enumerate([(keep_ref, send_ref), (send_ref, keep_ref)]):

            @pl.when(lax.axis_index("section") == k)
            def _():
                terms = jnp.dot(left_ref[...], right[...], preferred_element_type=f32)
                first[...] = terms[: height // 2]
                second[...] = terms[height // 2 :]

    return call(
        kernel,
        [((height // 2, width), f32)] * 2,
        [(VMEM, value) for value in [left, *grads]],
        [pltpu.VMEM((len(grads) * rows, width), bf16)],
    )


def chip_sum(keep, other, block, gains=()):
    height, width = keep.shape
    extra = 16 if gains else 0

    def kernel(keep_ref, other_ref, *refs):
        gain_refs, (own_ref, *away_refs) = refs[: len(gains)], refs[len(gains) :]
        total = keep_ref[...] + other_ref[...]
        own_ref[...] = total[:block]
        for index, away_ref in enumerate(away_refs):
            away_ref[:block] = total[(index + 1) * block : (index + 2) * block].astype(bf16)
        if gains:
            rest = gain_refs[0][:1] + gain_refs[1][:1]
            half = rest.shape[1]
            packed = []
            for _ in range(3):
                high = rest.astype(bf16).astype(f32)
                rest = rest - high
                tail = high[:, half - width :]
                packed += [high[:, :width], tail]
            packed.append(jnp.zeros((extra - len(packed), width), f32))
            for away_ref in away_refs:
                away_ref[block:] = jnp.concatenate(packed, axis=0).astype(bf16)

    outs = [((block, width), f32)] + [((block + extra, width), bf16)] * (height // block - 1)
    return call(kernel, outs, [(VMEM, value) for value in (keep, other, *gains)])


def gain_sum(gains, others, block):
    half = gains[0].shape[1]
    width = others[0].shape[1]

    def kernel(mine_ref, core_ref, *refs):
        total = mine_ref[:1] + core_ref[:1]
        for ref in refs[:-1]:
            packed = ref[block:].astype(f32)
            heads = packed[0:1] + packed[2:3] + packed[4:5]
            tails = packed[1:2] + packed[3:4] + packed[5:6]
            total = total + jnp.concatenate([heads, tails[:, 2 * width - half :]], axis=1)
        refs[-1][...] = jnp.broadcast_to(total, (8, half))

    return call(kernel, [((8, half), f32)], [(VMEM, value) for value in (*gains, *others)])[0]


def final_sum(own, others, half):
    block = own[0].shape[0]
    count = len(others[0])

    def kernel(*refs):
        start = 0
        for part in range(len(own)):
            own_ref, *other_refs = refs[part * (count + 1) : (part + 1) * (count + 1)]
            total = own_ref[...]
            for other_ref in other_refs:
                total = total + other_ref[:block].astype(f32)
            width = own_ref.shape[1]
            refs[-1][:, start : start + width] = total
            start += width

    values = [value for mine, theirs in zip(own, others) for value in (mine, *theirs)]
    return call(kernel, [((block, half), f32)], [(VMEM, value) for value in values])[0]


def place(order, total, other):
    rows, half = total.shape

    def kernel(order_ref, total_ref, other_ref, out_ref):
        micro = order_ref[0, lax.axis_index("section")]
        out_ref[micro] = total_ref[...]
        out_ref[1 - micro] = other_ref[...]

    ins = [(SMEM, order), (VMEM, total), (VMEM, other)]
    return call(kernel, [((2, rows, half), f32)], ins)[0]


def shards(states, injection, cotangent, gain, weight, exits, order):
    stash = states[0]
    slots, rows, features = stash.shape
    half = weight.shape[1]
    dp = lax.axis_index("dp")
    chips = lax.axis_size("dp")
    group = 4
    groups = chips // group
    assert slots == 2 and lax.axis_size("section") == 2 and lax.axis_size("mp") == 2
    assert chips % group == 0 and groups & (groups - 1) == 0

    def across(value, distance):
        return lax.ppermute(value, "dp", [(i, i ^ distance) for i in range(chips)])

    def gathered(value):
        return [value] + [across(value, distance) for distance in range(1, group)]

    block = features // (2 * chips)
    weight, columns = load(stash, weight, chips, group)
    columns = columns[:1] + [across(columns[distance], distance) for distance in range(1, group)]

    gain = gain.reshape(1, half)
    keep, send = forward(stash, weight, injection, order)
    got = swap(send, "section")
    sums = row_sums(order, cotangent, gain, keep, got)
    others = swap(sums, "mp")
    others, columns = lax.optimization_barrier((others, columns))
    db1, delta1, gain1, away = lower_iteration1(
        order, exits, cotangent, gain, keep, got, sums, others, weight
    )
    sent = swap(away, "mp")
    grads1 = gathered(db1)
    kept = kept_half(db1, weight)
    kept, sent = lax.optimization_barrier((kept, sent))

    carried, inner, gains = carry(
        order, exits, cotangent, gain, keep, got, sums, others, kept, sent, gain1, features
    )
    inner_other, gains_other = swap(inner, "mp"), swap(gains, "section")
    columns = stacked(columns)
    inner_other, gains_other, columns, *grads1[1:] = lax.optimization_barrier(
        (inner_other, gains_other, columns, *grads1[1:])
    )
    total, db0 = iteration0(
        gain, keep, got, sums, others, carried, inner, inner_other, delta1, features
    )
    grads0 = gathered(db0)
    columns, total = lax.optimization_barrier((columns, total))
    both = ("section", "mp")
    near = lax.ppermute(columns, both, [(2, 0), (0, 1), (3, 2), (1, 3)])
    far = lax.ppermute(columns, both, [(2, 1), (1, 2)])
    left = left_side(columns, near, far)

    left, grads0 = lax.optimization_barrier((left, grads0))

    cut = (half * 9 // 16 + 127) // 128 * 128
    gains = (gains, gains_other)
    terms = [
        weight_terms(left, grads0 + grads1, lanes) for lanes in [(0, cut), (cut, half - cut)]
    ]
    arrived = [swap(send, "section") for _, send in terms]
    own, others = [], []
    for part, (keep, _) in enumerate(terms):
        mine, *aways = chip_sum(keep, arrived[part], block, () if part else gains)
        aways, total, *arrived[part + 1 :] = lax.optimization_barrier(
            (aways, total, *arrived[part + 1 :])
        )
        if part == 0:
            other = swap(total, "section")
        own.append(mine)
        others.append([across(away, group * (i + 1)) for i, away in enumerate(aways)])
    d_injection = place(order, total, other)

    d_gain = gain_sum(gains, others[0], block)
    first, second, third = (across(d_gain, distance) for distance in range(1, group))
    d_gain = ((d_gain + first) + (second + third))[0]
    others[1], d_injection, d_gain = lax.optimization_barrier((others[1], d_injection, d_gain))
    d_weight = final_sum(own, others, half)
    return (d_injection, d_weight, d_gain)


def solution(mesh):
    return jax.shard_map(
        shards,
        mesh=mesh,
        in_specs=(
            P("section", "dp", None, None),
            P("dp", None, "mp"),
            P("dp", None, "mp"),
            P("mp"),
            P(None, "mp"),
            P("dp"),
            P("dp", None),
        ),
        out_specs=(P("dp", None, "mp"), P(("section", "dp"), "mp"), P("mp")),
        check_vma=False,
    )
```

```python
import jax
import jax.numpy as jnp
from jax import lax
from jax.experimental import pallas as pl
from jax.experimental.pallas import tpu as pltpu
from jax.sharding import PartitionSpec as P

epsilon = 1e-06
f32, bf16 = jnp.float32, jnp.bfloat16
VMEM = pl.BlockSpec(memory_space=pltpu.VMEM)
SMEM = pl.BlockSpec(memory_space=pltpu.SMEM)
HBM = pl.BlockSpec(memory_space=pltpu.HBM)


def call(kernel, outs, ins, scratch=(), limit=24):
    shapes = [jax.ShapeDtypeStruct(shape, kind) for shape, kind in outs]
    specs, values = zip(*ins)
    return pl.pallas_call(
        kernel,
        out_shape=shapes,
        in_specs=list(specs),
        out_specs=[VMEM] * len(shapes),
        scratch_shapes=list(scratch),
        compiler_params=pltpu.CompilerParams(vmem_limit_bytes=limit * 2**20),
        cost_estimate=pl.CostEstimate(flops=1000, bytes_accessed=1000, transcendentals=0),
    )(*values)


def swap(value, axis):
    return lax.ppermute(value, axis, [(0, 1), (1, 0)])


def opposite(value):
    return lax.ppermute(value, ("section", "mp"), [(i, 3 - i) for i in range(4)])


def own_slot():
    return lax.axis_index("section") ^ lax.axis_index("mp")


def chunks_of(total, size):
    return [(start, min(size, total - start)) for start in range(0, total, size)]


def to_rows(columns):
    rows = columns[0].shape[0]
    lane = lax.broadcasted_iota(jnp.int32, (rows, 128), 1)
    wide = jnp.zeros((rows, 128), f32)
    for index, column in enumerate(columns):
        wide = jnp.where(lane == index, column, wide)
    return wide.T[:8]


def to_columns(packed):
    return jnp.concatenate([packed] * 16, axis=0).T


def load(stash, weight, chips, group):
    slots, rows, features = stash.shape
    block = features // (2 * chips)
    groups = chips // group
    height = 2 * groups * block
    parts = chunks_of(features, 512)

    def kernel(stash_hbm, weight_hbm, w, x, *refs):
        *out_refs, turned, sems = refs
        copy = pltpu.make_async_copy(stash_hbm, x, sems.at[len(parts)])
        copy.start()
        copies = []
        for index, (start, size) in enumerate(parts):
            part = pl.ds(start, size)
            copies.append(pltpu.make_async_copy(weight_hbm.at[part], w.at[part], sems.at[index]))
            copies[-1].start()
        copy.wait()
        turned[...] = x[own_slot()].T
        dp = lax.axis_index("dp")
        for distance, out_ref in enumerate(out_refs):
            for half in range(2):
                for other in range(groups):
                    chip = dp ^ (distance + group * other)
                    source = pl.multiple_of((half * chips + chip) * block, 16)
                    base = (half * groups + other) * block
                    out_ref[base : base + block] = turned[pl.ds(source, block)]
        for each in copies:
            each.wait()

    pieces = group if block % 16 == 0 else 0
    weight, loaded, *columns = call(
        kernel,
        [(weight.shape, bf16), (stash.shape, bf16)] + [((height, rows), bf16)] * pieces,
        [(HBM, stash), (HBM, weight)],
        [
            pltpu.VMEM((features, rows), bf16),
            pltpu.SemaphoreType.DMA((len(parts) + 1,)),
        ],
        limit=42,
    )
    if not columns:
        turned = lax.dynamic_index_in_dim(stash, own_slot(), 0, keepdims=False).T
        turned = turned.reshape(2, chips, block, rows)
        for distance in range(group):
            picked = [
                lax.dynamic_index_in_dim(
                    turned, lax.axis_index("dp") ^ (distance + group * other), 1, keepdims=False
                )
                for other in range(groups)
            ]
            columns.append(jnp.stack(picked, axis=1).reshape(height, rows))
    return weight, loaded, columns


def forward(stash, weight, injection, order):
    slots, rows, features = stash.shape
    half = weight.shape[1]

    def kernel(order_ref, stash_ref, weight_ref, inj_ref, keep_ref, send_ref, acc):
        slot = own_slot()
        left = stash_ref[...].reshape(slots * rows, features)
        for start, size in chunks_of(half, 512):
            part = slice(start, start + size)
            term = jnp.dot(left, weight_ref[:, part], preferred_element_type=f32)
            acc[:, :, part] = term.reshape(slots, rows, size)
        keep_ref[...] = acc[slot] + inj_ref[order_ref[0, slot]].astype(f32)
        send_ref[...] = acc[1 - slot] + inj_ref[order_ref[0, 1 - slot]].astype(f32)

    return call(
        kernel,
        [((rows, half), f32)] * 2,
        [(SMEM, order), (VMEM, stash), (VMEM, weight), (VMEM, injection)],
        [pltpu.VMEM((slots, rows, half), f32)],
    )


def row_sums(order, cotangent, gain, keep, got):
    rows = keep.shape[0]

    def kernel(order_ref, cot_ref, gain_ref, keep_ref, got_ref, out_ref):
        sec = lax.axis_index("section")
        first = sec == 0
        keep, got = keep_ref[...], got_ref[...]
        pre1, pre0 = jnp.where(first, got, keep), jnp.where(first, keep, got)
        u = cot_ref[order_ref[0, own_slot()]].astype(f32) * gain_ref[...]
        sums = [pre1 * pre1, u * pre1, pre0 * pre0]
        out_ref[...] = to_rows([jnp.sum(each, axis=1, keepdims=True) for each in sums])

    ins = [(SMEM, order), (VMEM, cotangent), (VMEM, gain), (VMEM, keep), (VMEM, got)]
    return call(kernel, [((8, rows), f32)], ins)[0]


def delta_of(pre, u, squares, inner, features):
    radius = jnp.sqrt(squares / features + epsilon)
    inverse = 1.0 / radius
    normed = pre * inverse
    return normed, (u - normed * (inner * inverse / features)) * inverse


def lower_iteration1(order, exits, cotangent, gain, keep, got, sums, others, weight):
    rows, half = keep.shape
    features = weight.shape[0]

    def kernel(order_ref, exits_ref, cot_ref, gain_ref, keep_ref, got_ref, sums_ref, others_ref,
               weight_ref, db_ref, delta_ref, gain_out, away_ref):
        sec, mp = lax.axis_index("section"), lax.axis_index("mp")
        micro = order_ref[0, own_slot()]
        live = jnp.where(exits_ref[micro] > 1, 1.0, 0.0)
        stats = to_columns(sums_ref[...] + others_ref[...])
        pre = jnp.where(sec == 0, got_ref[...], keep_ref[...])
        cot = cot_ref[micro].astype(f32)
        normed, delta = delta_of(pre, cot * gain_ref[...], stats[:, 0:1], stats[:, 1:2], features)
        delta = delta * live
        delta_ref[...] = delta
        db = delta.astype(bf16)
        db_ref[...] = db
        gain_out[...] = jnp.sum(cot * normed, axis=0, keepdims=True) * live
        part = weight_ref[pl.ds(pl.multiple_of((1 - mp) * half, 128), half)]
        away_ref[...] = lax.dot_general(
            part, db, (((1,), (1,)), ((), ())), preferred_element_type=f32
        ).astype(bf16)

    return call(
        kernel,
        [((rows, half), bf16), ((rows, half), f32), ((1, half), f32), ((half, rows), bf16)],
        [(SMEM, order), (SMEM, exits), (VMEM, cotangent), (VMEM, gain), (VMEM, keep), (VMEM, got),
         (VMEM, sums), (VMEM, others), (VMEM, weight)],
    )


def kept_half(db, weight):
    rows, half = db.shape

    def kernel(db_ref, weight_ref, out_ref):
        part = weight_ref[pl.ds(pl.multiple_of(lax.axis_index("mp") * half, 128), half)]
        out_ref[...] = lax.dot_general(
            part, db_ref[...], (((1,), (1,)), ((), ())), preferred_element_type=f32
        )

    return call(kernel, [((half, rows), f32)], [(VMEM, db), (VMEM, weight)])[0]


def carry(order, exits, cotangent, gain, keep, got, sums, others, kept, sent, gain1, features):
    rows, half = keep.shape

    def kernel(order_ref, exits_ref, cot_ref, gain_ref, keep_ref, got_ref, sums_ref, others_ref,
               kept_ref, sent_ref, gain1_ref, carried_ref, inner_ref, gain_out):
        sec = lax.axis_index("section")
        micro = order_ref[0, own_slot()]
        passed = (kept_ref[...] + sent_ref[...].astype(f32)).astype(bf16).astype(f32).T
        cot = cot_ref[micro].astype(f32)
        carried = jnp.where(exits_ref[micro] > 1, passed, cot)
        carried_ref[...] = carried
        pre = jnp.where(sec == 0, keep_ref[...], got_ref[...])
        inner = jnp.sum(carried * gain_ref[...] * pre, axis=1, keepdims=True)
        inner_ref[...] = to_rows([inner])
        squares = to_columns(sums_ref[...] + others_ref[...])[:, 2:3]
        inverse = 1.0 / jnp.sqrt(squares / features + epsilon)
        gains = jnp.sum(carried * (pre * inverse), axis=0, keepdims=True) + gain1_ref[...]
        gain_out[...] = jnp.broadcast_to(gains, (8, half))

    return call(
        kernel,
        [((rows, half), f32), ((8, rows), f32), ((8, half), f32)],
        [(SMEM, order), (SMEM, exits)]
        + [
            (VMEM, value)
            for value in (cotangent, gain, keep, got, sums, others, kept, sent, gain1)
        ],
    )


def iteration0(gain, keep, got, sums, others, carried, inner, inner_other, delta1, features):
    rows, half = keep.shape

    def kernel(gain_ref, keep_ref, got_ref, sums_ref, others_ref, carried_ref, inner_ref, other_ref,
               delta1_ref, total_ref, db_ref):
        sec = lax.axis_index("section")
        squares = to_columns(sums_ref[...] + others_ref[...])[:, 2:3]
        inner = to_columns(inner_ref[...] + other_ref[...])[:, 0:1]
        pre = jnp.where(sec == 0, keep_ref[...], got_ref[...])
        _, delta = delta_of(pre, carried_ref[...] * gain_ref[...], squares, inner, features)
        total_ref[...] = delta + delta1_ref[...]
        db_ref[...] = delta.astype(bf16)

    values = [gain, keep, got, sums, others, carried, inner, inner_other, delta1]
    return call(
        kernel,
        [((rows, half), f32), ((rows, half), bf16)],
        [(VMEM, value) for value in values],
    )


def stacked(columns):
    def kernel(*refs):
        for chip, ref in enumerate(refs[:-1]):
            refs[-1][chip] = ref[...]

    outs = [((len(columns), *columns[0].shape), bf16)]
    return call(kernel, outs, [(VMEM, value) for value in columns])[0]


def left_side(columns, others):
    group, height, rows = columns.shape

    def kernel(own_ref, other_ref, out_ref):
        for index, pair in enumerate([(own_ref, other_ref), (other_ref, own_ref)]):

            @pl.when(lax.axis_index("section") == index)
            def _():
                for k, ref in enumerate(pair):
                    for chip in range(group):
                        base = (k * group + chip) * rows
                        out_ref[:, base : base + rows] = ref[chip]

    return call(
        kernel,
        [((height, 2 * group * rows), bf16)],
        [(VMEM, value) for value in (columns, others)],
    )[0]


def weight_terms(left, grads, lanes):
    rows = grads[0].shape[0]
    height = left.shape[0]
    start, width = lanes

    def kernel(left_ref, *refs):
        grads_refs, (keep_ref, send_ref, right) = refs[:-3], refs[-3:]
        for index, grads_ref in enumerate(grads_refs):
            right[index * rows : (index + 1) * rows] = grads_ref[:, start : start + width]
        for k, (first, second) in enumerate([(keep_ref, send_ref), (send_ref, keep_ref)]):

            @pl.when(lax.axis_index("section") == k)
            def _():
                terms = jnp.dot(left_ref[...], right[...], preferred_element_type=f32)
                first[...] = terms[: height // 2]
                second[...] = terms[height // 2 :]

    return call(
        kernel,
        [((height // 2, width), f32)] * 2,
        [(VMEM, value) for value in [left, *grads]],
        [pltpu.VMEM((len(grads) * rows, width), bf16)],
    )


def chip_sum(keep, other, block, gains=()):
    height, width = keep.shape
    extra = 16 if gains else 0

    def kernel(keep_ref, other_ref, *refs):
        gain_refs, (own_ref, *away_refs) = refs[: len(gains)], refs[len(gains) :]
        total = keep_ref[...] + other_ref[...]
        own_ref[...] = total[:block]
        for index, away_ref in enumerate(away_refs):
            away_ref[:block] = total[(index + 1) * block : (index + 2) * block].astype(bf16)
        if gains:
            rest = group_gains(gain_refs)
            half = rest.shape[1]
            packed = []
            for _ in range(3):
                high = rest.astype(bf16).astype(f32)
                rest = rest - high
                tail = high[:, half - width :]
                packed += [high[:, :width], tail]
            packed.append(jnp.zeros((extra - len(packed), width), f32))
            for away_ref in away_refs:
                away_ref[block:] = jnp.concatenate(packed, axis=0).astype(bf16)

    outs = [((block, width), f32)] + [((block + extra, width), bf16)] * (height // block - 1)
    return call(kernel, outs, [(VMEM, value) for value in (keep, other, *gains)])


def group_gains(refs):
    return refs[0][:1] + refs[1][:1]


def final_sum(own, others, gains, half):
    block, first_width = own[0].shape
    count = len(others[0])

    def kernel(*refs):
        gain_refs, refs = refs[: len(gains)], refs[len(gains) :]
        weight_out, gain_out = refs[-2:]
        start = 0
        for part in range(len(own)):
            own_ref, *other_refs = refs[part * (count + 1) : (part + 1) * (count + 1)]
            total = own_ref[...]
            for other_ref in other_refs:
                total = total + other_ref[:block].astype(f32)
            width = own_ref.shape[1]
            weight_out[:, start : start + width] = total
            start += width
        sums = [group_gains(gain_refs)]
        for ref in refs[1 : count + 1]:
            packed = ref[block:].astype(f32)
            heads = packed[0:1] + packed[2:3] + packed[4:5]
            tails = packed[1:2] + packed[3:4] + packed[5:6]
            tails = tails[:, 2 * first_width - half :]
            sums.append(jnp.concatenate([heads, tails], axis=1))
        while len(sums) > 1:
            sums = [a + b for a, b in zip(sums[::2], sums[1::2])]
        gain_out[...] = sums[0]

    values = [value for mine, theirs in zip(own, others) for value in (mine, *theirs)]
    ins = [(VMEM, value) for value in (*gains, *values)]
    return call(kernel, [((block, half), f32), ((1, half), f32)], ins)


def place(order, total, other):
    rows, half = total.shape

    def kernel(order_ref, total_ref, other_ref, out_ref):
        micro = order_ref[0, own_slot()]
        out_ref[micro] = total_ref[...]
        out_ref[1 - micro] = other_ref[...]

    ins = [(SMEM, order), (VMEM, total), (VMEM, other)]
    return call(kernel, [((2, rows, half), f32)], ins)[0]


def shards(states, injection, cotangent, gain, weight, exits, order):
    stash = states[0]
    slots, rows, features = stash.shape
    half = weight.shape[1]
    dp = lax.axis_index("dp")
    chips = lax.axis_size("dp")
    group = 4
    groups = chips // group
    assert slots == 2 and lax.axis_size("section") == 2 and lax.axis_size("mp") == 2
    assert chips % group == 0 and groups & (groups - 1) == 0

    def across(value, distance):
        return lax.ppermute(value, "dp", [(i, i ^ distance) for i in range(chips)])

    def gathered(value):
        return [value] + [across(value, distance) for distance in range(1, group)]

    block = features // (2 * chips)
    weight, stash, columns = load(stash, weight, chips, group)
    columns = columns[:1] + [across(columns[distance], distance) for distance in range(1, group)]

    gain = gain.reshape(1, half)
    keep, send = forward(stash, weight, injection, order)
    got = swap(send, "section")
    sums = row_sums(order, cotangent, gain, keep, got)
    others = opposite(sums)
    others, columns = lax.optimization_barrier((others, columns))
    db1, delta1, gain1, away = lower_iteration1(
        order, exits, cotangent, gain, keep, got, sums, others, weight
    )
    sent = opposite(away)
    grads1 = gathered(db1)
    kept = kept_half(db1, weight)
    kept, sent = lax.optimization_barrier((kept, sent))

    carried, inner, gains = carry(
        order, exits, cotangent, gain, keep, got, sums, others, kept, sent, gain1, features
    )
    inner_other, gains_other = opposite(inner), swap(gains, "section")
    columns = stacked(columns)
    gains = gains + gains_other
    near_gains = across(gains, 1)
    inner_other, near_gains, columns, *grads1[1:] = lax.optimization_barrier(
        (inner_other, near_gains, columns, *grads1[1:])
    )
    total, db0 = iteration0(
        gain, keep, got, sums, others, carried, inner, inner_other, delta1, features
    )
    grads0 = gathered(db0)
    columns, total = lax.optimization_barrier((columns, total))
    left = left_side(columns, opposite(columns))

    gains = gains + near_gains
    gains = [gains, across(gains, 2)]
    left, grads0, gains = lax.optimization_barrier((left, grads0, gains))

    cut = (half * 9 // 16 + 127) // 128 * 128
    terms = [
        weight_terms(left, grads0 + grads1, lanes) for lanes in [(0, cut), (cut, half - cut)]
    ]
    arrived = [swap(send, "section") for _, send in terms]
    own, others = [], []
    for part, (keep, _) in enumerate(terms):
        if part:
            keep, *_ = lax.optimization_barrier((keep, *aways))
            total, *_ = lax.optimization_barrier((total, *aways))
        mine, *aways = chip_sum(keep, arrived[part], block, () if part else gains)
        own.append(mine)
        others.append([across(away, group * (i + 1)) for i, away in enumerate(aways)])
    d_injection = place(order, total, swap(total, "section"))
    others[1], d_injection = lax.optimization_barrier((others[1], d_injection))
    d_weight, d_gain = final_sum(own, others, gains, half)
    return (d_injection, d_weight, d_gain[0])


def solution(mesh):
    return jax.shard_map(
        shards,
        mesh=mesh,
        in_specs=(
            P("section", "dp", None, None),
            P("dp", None, "mp"),
            P("dp", None, "mp"),
            P("mp"),
            P(None, "mp"),
            P("dp"),
            P("dp", None),
        ),
        out_specs=(P("dp", None, "mp"), P(("section", "dp"), "mp"), P("mp")),
        check_vma=False,
    )
```

```python
import jax
import jax.numpy as jnp
from jax import lax
from jax.experimental import pallas as pl
from jax.experimental.pallas import tpu as pltpu
from jax.sharding import PartitionSpec as P

epsilon = 1e-06
f32, bf16 = jnp.float32, jnp.bfloat16
VMEM = pl.BlockSpec(memory_space=pltpu.VMEM)
SMEM = pl.BlockSpec(memory_space=pltpu.SMEM)
HBM = pl.BlockSpec(memory_space=pltpu.HBM)


def call(kernel, outs, ins, scratch=(), limit=24):
    shapes = [jax.ShapeDtypeStruct(shape, kind) for shape, kind in outs]
    specs, values = zip(*ins)
    return pl.pallas_call(
        kernel,
        out_shape=shapes,
        in_specs=list(specs),
        out_specs=[VMEM] * len(shapes),
        scratch_shapes=list(scratch),
        compiler_params=pltpu.CompilerParams(vmem_limit_bytes=limit * 2**20),
        cost_estimate=pl.CostEstimate(flops=1000, bytes_accessed=1000, transcendentals=0),
    )(*values)


def swap(value, axis):
    return lax.ppermute(value, axis, [(0, 1), (1, 0)])


def opposite(value):
    return lax.ppermute(value, ("section", "mp"), [(i, 3 - i) for i in range(4)])


def own_slot():
    return lax.axis_index("section") ^ lax.axis_index("mp")


def chunks_of(total, size):
    return [(start, min(size, total - start)) for start in range(0, total, size)]


def to_rows(columns):
    rows = columns[0].shape[0]
    lane = lax.broadcasted_iota(jnp.int32, (rows, 128), 1)
    wide = jnp.zeros((rows, 128), f32)
    for index, column in enumerate(columns):
        wide = jnp.where(lane == index, column, wide)
    return wide.T[:8]


def to_columns(packed):
    return jnp.concatenate([packed] * 16, axis=0).T


def load(weight):
    parts = chunks_of(weight.shape[0], 512)

    def kernel(weight_hbm, w, sems):
        copies = []
        for index, (start, size) in enumerate(parts):
            part = pl.ds(start, size)
            copies.append(pltpu.make_async_copy(weight_hbm.at[part], w.at[part], sems.at[index]))
            copies[-1].start()
        for copy in copies:
            copy.wait()

    return call(
        kernel,
        [(weight.shape, bf16)],
        [(HBM, weight)],
        [pltpu.SemaphoreType.DMA((len(parts),))],
        limit=42,
    )[0]


def forward(stash, weight, injection, order, chips, group):
    slots, rows, features = stash.shape
    half = weight.shape[1]
    block = features // (2 * chips)
    groups = chips // group
    height = 2 * groups * block

    def kernel(order_ref, stash_ref, weight_ref, inj_ref, keep_ref, send_ref, *refs):
        *out_refs, turned, acc = refs
        slot = own_slot()
        left = stash_ref[...].reshape(slots * rows, features)
        for start, size in chunks_of(half, 512):
            part = slice(start, start + size)
            term = jnp.dot(left, weight_ref[:, part], preferred_element_type=f32)
            acc[:, :, part] = term.reshape(slots, rows, size)
        keep_ref[...] = acc[slot] + inj_ref[order_ref[0, slot]].astype(f32)
        send_ref[...] = acc[1 - slot] + inj_ref[order_ref[0, 1 - slot]].astype(f32)
        if out_refs:
            turned[...] = stash_ref[slot].T
        dp = lax.axis_index("dp")
        for distance, out_ref in enumerate(out_refs):
            for half_index in range(2):
                for other in range(groups):
                    chip = dp ^ (distance + group * other)
                    source = pl.multiple_of((half_index * chips + chip) * block, 16)
                    base = (half_index * groups + other) * block
                    out_ref[base : base + block] = turned[pl.ds(source, block)]

    pieces = group if block % 16 == 0 else 0
    keep, send, *columns = call(
        kernel,
        [((rows, half), f32)] * 2 + [((height, rows), bf16)] * pieces,
        [(SMEM, order), (VMEM, stash), (VMEM, weight), (VMEM, injection)],
        [pltpu.VMEM((features, rows), bf16), pltpu.VMEM((slots, rows, half), f32)],
    )
    if not columns:
        turned = lax.dynamic_index_in_dim(stash, own_slot(), 0, keepdims=False).T
        turned = turned.reshape(2, chips, block, rows)
        for distance in range(group):
            picked = [
                lax.dynamic_index_in_dim(
                    turned, lax.axis_index("dp") ^ (distance + group * other), 1, keepdims=False
                )
                for other in range(groups)
            ]
            columns.append(jnp.stack(picked, axis=1).reshape(height, rows))
    return keep, send, columns


def row_sums(order, cotangent, gain, keep, got):
    rows = keep.shape[0]

    def kernel(order_ref, cot_ref, gain_ref, keep_ref, got_ref, out_ref):
        sec = lax.axis_index("section")
        first = sec == 0
        keep, got = keep_ref[...], got_ref[...]
        pre1, pre0 = jnp.where(first, got, keep), jnp.where(first, keep, got)
        u = cot_ref[order_ref[0, own_slot()]].astype(f32) * gain_ref[...]
        sums = [pre1 * pre1, u * pre1, pre0 * pre0]
        out_ref[...] = to_rows([jnp.sum(each, axis=1, keepdims=True) for each in sums])

    ins = [(SMEM, order), (VMEM, cotangent), (VMEM, gain), (VMEM, keep), (VMEM, got)]
    return call(kernel, [((8, rows), f32)], ins)[0]


def delta_of(pre, u, squares, inner, features):
    radius = jnp.sqrt(squares / features + epsilon)
    inverse = 1.0 / radius
    normed = pre * inverse
    return normed, (u - normed * (inner * inverse / features)) * inverse


def lower_iteration1(order, exits, cotangent, gain, keep, got, sums, others, weight):
    rows, half = keep.shape
    features = weight.shape[0]

    def kernel(order_ref, exits_ref, cot_ref, gain_ref, keep_ref, got_ref, sums_ref, others_ref,
               weight_ref, db_ref, delta_ref, gain_out, away_ref):
        sec, mp = lax.axis_index("section"), lax.axis_index("mp")
        micro = order_ref[0, own_slot()]
        live = jnp.where(exits_ref[micro] > 1, 1.0, 0.0)
        stats = to_columns(sums_ref[...] + others_ref[...])
        pre = jnp.where(sec == 0, got_ref[...], keep_ref[...])
        cot = cot_ref[micro].astype(f32)
        normed, delta = delta_of(pre, cot * gain_ref[...], stats[:, 0:1], stats[:, 1:2], features)
        delta = delta * live
        delta_ref[...] = delta
        db = delta.astype(bf16)
        db_ref[...] = db
        gain_out[...] = jnp.sum(cot * normed, axis=0, keepdims=True) * live
        part = weight_ref[pl.ds(pl.multiple_of((1 - mp) * half, 128), half)]
        away_ref[...] = lax.dot_general(
            part, db, (((1,), (1,)), ((), ())), preferred_element_type=f32
        ).astype(bf16)

    return call(
        kernel,
        [((rows, half), bf16), ((rows, half), f32), ((1, half), f32), ((half, rows), bf16)],
        [(SMEM, order), (SMEM, exits), (VMEM, cotangent), (VMEM, gain), (VMEM, keep), (VMEM, got),
         (VMEM, sums), (VMEM, others), (VMEM, weight)],
    )


def kept_half(db, weight):
    rows, half = db.shape

    def kernel(db_ref, weight_ref, out_ref):
        part = weight_ref[pl.ds(pl.multiple_of(lax.axis_index("mp") * half, 128), half)]
        out_ref[...] = lax.dot_general(
            part, db_ref[...], (((1,), (1,)), ((), ())), preferred_element_type=f32
        )

    return call(kernel, [((half, rows), f32)], [(VMEM, db), (VMEM, weight)])[0]


def carry(order, exits, cotangent, gain, keep, got, sums, others, kept, sent, gain1, features):
    rows, half = keep.shape

    def kernel(order_ref, exits_ref, cot_ref, gain_ref, keep_ref, got_ref, sums_ref, others_ref,
               kept_ref, sent_ref, gain1_ref, carried_ref, inner_ref, gain_out):
        sec = lax.axis_index("section")
        micro = order_ref[0, own_slot()]
        passed = (kept_ref[...] + sent_ref[...].astype(f32)).astype(bf16).astype(f32).T
        cot = cot_ref[micro].astype(f32)
        carried = jnp.where(exits_ref[micro] > 1, passed, cot)
        carried_ref[...] = carried
        pre = jnp.where(sec == 0, keep_ref[...], got_ref[...])
        inner = jnp.sum(carried * gain_ref[...] * pre, axis=1, keepdims=True)
        inner_ref[...] = to_rows([inner])
        squares = to_columns(sums_ref[...] + others_ref[...])[:, 2:3]
        inverse = 1.0 / jnp.sqrt(squares / features + epsilon)
        gains = jnp.sum(carried * (pre * inverse), axis=0, keepdims=True) + gain1_ref[...]
        gain_out[...] = jnp.broadcast_to(gains, (8, half))

    return call(
        kernel,
        [((rows, half), f32), ((8, rows), f32), ((8, half), f32)],
        [(SMEM, order), (SMEM, exits)]
        + [
            (VMEM, value)
            for value in (cotangent, gain, keep, got, sums, others, kept, sent, gain1)
        ],
    )


def iteration0(gain, keep, got, sums, others, carried, inner, inner_other, delta1, features):
    rows, half = keep.shape

    def kernel(gain_ref, keep_ref, got_ref, sums_ref, others_ref, carried_ref, inner_ref, other_ref,
               delta1_ref, total_ref, db_ref):
        sec = lax.axis_index("section")
        squares = to_columns(sums_ref[...] + others_ref[...])[:, 2:3]
        inner = to_columns(inner_ref[...] + other_ref[...])[:, 0:1]
        pre = jnp.where(sec == 0, keep_ref[...], got_ref[...])
        _, delta = delta_of(pre, carried_ref[...] * gain_ref[...], squares, inner, features)
        total_ref[...] = delta + delta1_ref[...]
        db_ref[...] = delta.astype(bf16)

    values = [gain, keep, got, sums, others, carried, inner, inner_other, delta1]
    return call(
        kernel,
        [((rows, half), f32), ((rows, half), bf16)],
        [(VMEM, value) for value in values],
    )


def stacked(columns):
    def kernel(*refs):
        for chip, ref in enumerate(refs[:-1]):
            refs[-1][chip] = ref[...]

    outs = [((len(columns), *columns[0].shape), bf16)]
    return call(kernel, outs, [(VMEM, value) for value in columns])[0]


def left_side(columns, others):
    group, height, rows = columns.shape

    def kernel(own_ref, other_ref, out_ref):
        for index, pair in enumerate([(own_ref, other_ref), (other_ref, own_ref)]):

            @pl.when(lax.axis_index("section") == index)
            def _():
                for k, ref in enumerate(pair):
                    for chip in range(group):
                        base = (k * group + chip) * rows
                        out_ref[:, base : base + rows] = ref[chip]

    return call(
        kernel,
        [((height, 2 * group * rows), bf16)],
        [(VMEM, value) for value in (columns, others)],
    )[0]


def weight_terms(left, grads, lanes):
    rows = grads[0].shape[0]
    height = left.shape[0]
    start, width = lanes

    def kernel(left_ref, *refs):
        grads_refs, (keep_ref, send_ref, right) = refs[:-3], refs[-3:]
        for index, grads_ref in enumerate(grads_refs):
            right[index * rows : (index + 1) * rows] = grads_ref[:, start : start + width]
        for k, (first, second) in enumerate([(keep_ref, send_ref), (send_ref, keep_ref)]):

            @pl.when(lax.axis_index("section") == k)
            def _():
                terms = jnp.dot(left_ref[...], right[...], preferred_element_type=f32)
                first[...] = terms[: height // 2]
                second[...] = terms[height // 2 :]

    return call(
        kernel,
        [((height // 2, width), f32)] * 2,
        [(VMEM, value) for value in [left, *grads]],
        [pltpu.VMEM((len(grads) * rows, width), bf16)],
    )


def chip_sum(keep, other, block):
    height, width = keep.shape

    def kernel(keep_ref, other_ref, own_ref, *away_refs):
        total = keep_ref[...] + other_ref[...]
        own_ref[...] = total[:block]
        for index, away_ref in enumerate(away_refs):
            away_ref[...] = total[(index + 1) * block : (index + 2) * block].astype(bf16)

    outs = [((block, width), f32)] + [((block, width), bf16)] * (height // block - 1)
    return call(kernel, outs, [(VMEM, keep), (VMEM, other)])


def final_sum(own, others, gains, half):
    block = own[0].shape[0]
    count = len(others[0])

    def kernel(*refs):
        gain_refs, refs = refs[: len(gains)], refs[len(gains) :]
        weight_out, gain_out = refs[-2:]
        start = 0
        for part in range(len(own)):
            own_ref, *other_refs = refs[part * (count + 1) : (part + 1) * (count + 1)]
            total = own_ref[...]
            for other_ref in other_refs:
                total = total + other_ref[...].astype(f32)
            width = own_ref.shape[1]
            weight_out[:, start : start + width] = total
            start += width
        sums = [ref[:1] for ref in gain_refs]
        while len(sums) > 1:
            sums = [a + b for a, b in zip(sums[::2], sums[1::2])]
        gain_out[...] = sums[0].reshape(half)

    values = [value for mine, theirs in zip(own, others) for value in (mine, *theirs)]
    ins = [(VMEM, value) for value in (*gains, *values)]
    return call(kernel, [((block, half), f32), ((half,), f32)], ins)


def place(order, total, other):
    rows, half = total.shape

    def kernel(order_ref, total_ref, other_ref, out_ref):
        micro = order_ref[0, own_slot()]
        out_ref[micro] = total_ref[...]
        out_ref[1 - micro] = other_ref[...]

    ins = [(SMEM, order), (VMEM, total), (VMEM, other)]
    return call(kernel, [((2, rows, half), f32)], ins)[0]


def shards(states, injection, cotangent, gain, weight, exits, order):
    stash = states[0]
    slots, rows, features = stash.shape
    half = weight.shape[1]
    dp = lax.axis_index("dp")
    chips = lax.axis_size("dp")
    group = 4
    groups = chips // group
    assert slots == 2 and lax.axis_size("section") == 2 and lax.axis_size("mp") == 2
    assert chips % group == 0 and groups & (groups - 1) == 0

    def across(value, distance):
        return lax.ppermute(value, "dp", [(i, i ^ distance) for i in range(chips)])

    def gathered(value):
        return [value] + [across(value, distance) for distance in range(1, group)]

    block = features // (2 * chips)
    gain = gain.reshape(1, half)
    weight = load(weight)
    keep, send, columns = forward(stash, weight, injection, order, chips, group)
    columns = columns[:1] + [across(columns[distance], distance) for distance in range(1, group)]
    got = swap(send, "section")
    sums = row_sums(order, cotangent, gain, keep, got)
    others = opposite(sums)
    others, columns = lax.optimization_barrier((others, columns))
    db1, delta1, gain1, away = lower_iteration1(
        order, exits, cotangent, gain, keep, got, sums, others, weight
    )
    sent = opposite(away)
    grads1 = gathered(db1)
    kept = kept_half(db1, weight)
    kept, sent = lax.optimization_barrier((kept, sent))

    carried, inner, gains = carry(
        order, exits, cotangent, gain, keep, got, sums, others, kept, sent, gain1, features
    )
    inner_other, gains_other = opposite(inner), swap(gains, "section")
    columns = stacked(columns)
    gains = gains + gains_other
    near_gains = across(gains, 1)
    inner_other, near_gains, columns, *grads1[1:] = lax.optimization_barrier(
        (inner_other, near_gains, columns, *grads1[1:])
    )
    total, db0 = iteration0(
        gain, keep, got, sums, others, carried, inner, inner_other, delta1, features
    )
    grads0 = gathered(db0)
    columns, total = lax.optimization_barrier((columns, total))
    left = left_side(columns, opposite(columns))

    gains = gains + near_gains
    far_gains = across(gains, 2)
    left, grads0, far_gains = lax.optimization_barrier((left, grads0, far_gains))
    gains = gains + far_gains

    cut = (half // 2 + 127) // 128 * 128
    terms = [
        weight_terms(left, grads0 + grads1, lanes) for lanes in [(0, cut), (cut, half - cut)]
    ]
    arrived = [swap(send, "section") for _, send in terms]
    own, others = [], []
    for part, (keep, _) in enumerate(terms):
        if part:
            keep, *_ = lax.optimization_barrier((keep, *aways))
            total, *_ = lax.optimization_barrier((total, *aways))
        mine, *aways = chip_sum(keep, arrived[part], block)
        own.append(mine)
        others.append([across(away, group * (i + 1)) for i, away in enumerate(aways)])
    gains, *_ = lax.optimization_barrier((gains, *aways))
    gains = [gains] + [across(gains, group * other) for other in range(1, groups)]
    d_injection = place(order, total, swap(total, "section"))
    others[1], d_injection = lax.optimization_barrier((others[1], d_injection))
    d_weight, d_gain = final_sum(own, others, gains, half)
    return (d_injection, d_weight, d_gain)


def solution(mesh):
    return jax.shard_map(
        shards,
        mesh=mesh,
        in_specs=(
            P("section", "dp", None, None),
            P("dp", None, "mp"),
            P("dp", None, "mp"),
            P("mp"),
            P(None, "mp"),
            P("dp"),
            P("dp", None),
        ),
        out_specs=(P("dp", None, "mp"), P(("section", "dp"), "mp"), P("mp")),
        check_vma=False,
    )
```

```python
import jax
import jax.numpy as jnp
from jax import lax
from jax.experimental import pallas as pl
from jax.experimental.pallas import tpu as pltpu
from jax.sharding import PartitionSpec as P

epsilon = 1e-06
f32, bf16 = jnp.float32, jnp.bfloat16
VMEM = pl.BlockSpec(memory_space=pltpu.VMEM)
SMEM = pl.BlockSpec(memory_space=pltpu.SMEM)
HBM = pl.BlockSpec(memory_space=pltpu.HBM)


def call(kernel, outs, ins, scratch=(), limit=24):
    shapes = [jax.ShapeDtypeStruct(shape, kind) for shape, kind in outs]
    specs, values = zip(*ins)
    return pl.pallas_call(
        kernel,
        out_shape=shapes,
        in_specs=list(specs),
        out_specs=[VMEM] * len(shapes),
        scratch_shapes=list(scratch),
        compiler_params=pltpu.CompilerParams(vmem_limit_bytes=limit * 2**20),
        cost_estimate=pl.CostEstimate(flops=1000, bytes_accessed=1000, transcendentals=0),
    )(*values)


def swap(value, axis):
    return lax.ppermute(value, axis, [(0, 1), (1, 0)])


def opposite(value):
    return lax.ppermute(value, ("section", "mp"), [(i, 3 - i) for i in range(4)])


def own_slot():
    return lax.axis_index("section") ^ lax.axis_index("mp")


def chunks_of(total, size):
    return [(start, min(size, total - start)) for start in range(0, total, size)]


def to_rows(columns):
    rows = columns[0].shape[0]
    lane = lax.broadcasted_iota(jnp.int32, (rows, 128), 1)
    wide = jnp.zeros((rows, 128), f32)
    for index, column in enumerate(columns):
        wide = jnp.where(lane == index, column, wide)
    return wide.T[:8]


def to_columns(packed):
    return jnp.concatenate([packed] * 16, axis=0).T


def load(weight):
    parts = chunks_of(weight.shape[0], 512)

    def kernel(weight_hbm, w, sems):
        copies = []
        for index, (start, size) in enumerate(parts):
            part = pl.ds(start, size)
            copies.append(pltpu.make_async_copy(weight_hbm.at[part], w.at[part], sems.at[index]))
            copies[-1].start()
        for copy in copies:
            copy.wait()

    return call(
        kernel,
        [(weight.shape, bf16)],
        [(HBM, weight)],
        [pltpu.SemaphoreType.DMA((len(parts),))],
        limit=42,
    )[0]


def forward(stash, weight, injection, order, chips, group):
    slots, rows, features = stash.shape
    half = weight.shape[1]
    block = features // (2 * chips)
    groups = chips // group
    height = 2 * groups * block

    def kernel(order_ref, stash_ref, weight_ref, inj_ref, keep_ref, send_ref, *refs):
        *out_refs, turned, acc = refs
        slot = own_slot()
        left = stash_ref[...].reshape(slots * rows, features)
        for start, size in chunks_of(half, 512):
            part = slice(start, start + size)
            term = jnp.dot(left, weight_ref[:, part], preferred_element_type=f32)
            acc[:, :, part] = term.reshape(slots, rows, size)
        keep_ref[...] = acc[slot] + inj_ref[order_ref[0, slot]].astype(f32)
        send_ref[...] = acc[1 - slot] + inj_ref[order_ref[0, 1 - slot]].astype(f32)
        if out_refs:
            turned[...] = stash_ref[slot].T
        dp = lax.axis_index("dp")
        for distance, out_ref in enumerate(out_refs):
            for half_index in range(2):
                for other in range(groups):
                    chip = dp ^ (distance + group * other)
                    source = pl.multiple_of((half_index * chips + chip) * block, 16)
                    base = (half_index * groups + other) * block
                    out_ref[base : base + block] = turned[pl.ds(source, block)]

    pieces = group if block % 16 == 0 else 0
    keep, send, *columns = call(
        kernel,
        [((rows, half), f32)] * 2 + [((height, rows), bf16)] * pieces,
        [(SMEM, order), (VMEM, stash), (VMEM, weight), (VMEM, injection)],
        [pltpu.VMEM((features, rows), bf16), pltpu.VMEM((slots, rows, half), f32)],
    )
    if not columns:
        turned = lax.dynamic_index_in_dim(stash, own_slot(), 0, keepdims=False).T
        turned = turned.reshape(2, chips, block, rows)
        for distance in range(group):
            picked = [
                lax.dynamic_index_in_dim(
                    turned, lax.axis_index("dp") ^ (distance + group * other), 1, keepdims=False
                )
                for other in range(groups)
            ]
            columns.append(jnp.stack(picked, axis=1).reshape(height, rows))
    return keep, send, columns


def row_sums(order, cotangent, gain, keep, got):
    rows = keep.shape[0]

    def kernel(order_ref, cot_ref, gain_ref, keep_ref, got_ref, out_ref):
        sec = lax.axis_index("section")
        first = sec == 0
        keep, got = keep_ref[...], got_ref[...]
        pre1, pre0 = jnp.where(first, got, keep), jnp.where(first, keep, got)
        u = cot_ref[order_ref[0, own_slot()]].astype(f32) * gain_ref[...]
        sums = [pre1 * pre1, u * pre1, pre0 * pre0]
        out_ref[...] = to_rows([jnp.sum(each, axis=1, keepdims=True) for each in sums])

    ins = [(SMEM, order), (VMEM, cotangent), (VMEM, gain), (VMEM, keep), (VMEM, got)]
    return call(kernel, [((8, rows), f32)], ins)[0]


def delta_of(pre, u, squares, inner, features):
    radius = jnp.sqrt(squares / features + epsilon)
    inverse = 1.0 / radius
    normed = pre * inverse
    return normed, (u - normed * (inner * inverse / features)) * inverse


def lower_iteration1(order, exits, cotangent, gain, keep, got, sums, others, weight):
    rows, half = keep.shape
    features = weight.shape[0]

    def kernel(order_ref, exits_ref, cot_ref, gain_ref, keep_ref, got_ref, sums_ref, others_ref,
               weight_ref, db_ref, delta_ref, gain_out, away_ref):
        sec, mp = lax.axis_index("section"), lax.axis_index("mp")
        micro = order_ref[0, own_slot()]
        live = jnp.where(exits_ref[micro] > 1, 1.0, 0.0)
        stats = to_columns(sums_ref[...] + others_ref[...])
        pre = jnp.where(sec == 0, got_ref[...], keep_ref[...])
        cot = cot_ref[micro].astype(f32)
        normed, delta = delta_of(pre, cot * gain_ref[...], stats[:, 0:1], stats[:, 1:2], features)
        delta = delta * live
        delta_ref[...] = delta
        db = delta.astype(bf16)
        db_ref[...] = db
        gain_out[...] = jnp.sum(cot * normed, axis=0, keepdims=True) * live
        part = weight_ref[pl.ds(pl.multiple_of((1 - mp) * half, 128), half)]
        away_ref[...] = lax.dot_general(
            part, db, (((1,), (1,)), ((), ())), preferred_element_type=f32
        ).astype(bf16)

    return call(
        kernel,
        [((rows, half), bf16), ((rows, half), f32), ((1, half), f32), ((half, rows), bf16)],
        [(SMEM, order), (SMEM, exits), (VMEM, cotangent), (VMEM, gain), (VMEM, keep), (VMEM, got),
         (VMEM, sums), (VMEM, others), (VMEM, weight)],
    )


def kept_half(db, weight):
    rows, half = db.shape

    def kernel(db_ref, weight_ref, out_ref):
        part = weight_ref[pl.ds(pl.multiple_of(lax.axis_index("mp") * half, 128), half)]
        out_ref[...] = lax.dot_general(
            part, db_ref[...], (((1,), (1,)), ((), ())), preferred_element_type=f32
        )

    return call(kernel, [((half, rows), f32)], [(VMEM, db), (VMEM, weight)])[0]


def carry(order, exits, cotangent, gain, keep, got, sums, others, kept, sent, gain1, features):
    rows, half = keep.shape

    def kernel(order_ref, exits_ref, cot_ref, gain_ref, keep_ref, got_ref, sums_ref, others_ref,
               kept_ref, sent_ref, gain1_ref, carried_ref, inner_ref, gain_out):
        sec = lax.axis_index("section")
        micro = order_ref[0, own_slot()]
        passed = (kept_ref[...] + sent_ref[...].astype(f32)).astype(bf16).astype(f32).T
        cot = cot_ref[micro].astype(f32)
        carried = jnp.where(exits_ref[micro] > 1, passed, cot)
        carried_ref[...] = carried
        pre = jnp.where(sec == 0, keep_ref[...], got_ref[...])
        inner = jnp.sum(carried * gain_ref[...] * pre, axis=1, keepdims=True)
        inner_ref[...] = to_rows([inner])
        squares = to_columns(sums_ref[...] + others_ref[...])[:, 2:3]
        inverse = 1.0 / jnp.sqrt(squares / features + epsilon)
        gains = jnp.sum(carried * (pre * inverse), axis=0, keepdims=True) + gain1_ref[...]
        gain_out[...] = jnp.broadcast_to(gains, (8, half))

    return call(
        kernel,
        [((rows, half), f32), ((8, rows), f32), ((8, half), f32)],
        [(SMEM, order), (SMEM, exits)]
        + [
            (VMEM, value)
            for value in (cotangent, gain, keep, got, sums, others, kept, sent, gain1)
        ],
    )


def iteration0(gain, keep, got, sums, others, carried, inner, inner_other, delta1, features):
    rows, half = keep.shape

    def kernel(gain_ref, keep_ref, got_ref, sums_ref, others_ref, carried_ref, inner_ref, other_ref,
               delta1_ref, total_ref, db_ref):
        sec = lax.axis_index("section")
        squares = to_columns(sums_ref[...] + others_ref[...])[:, 2:3]
        inner = to_columns(inner_ref[...] + other_ref[...])[:, 0:1]
        pre = jnp.where(sec == 0, keep_ref[...], got_ref[...])
        _, delta = delta_of(pre, carried_ref[...] * gain_ref[...], squares, inner, features)
        total_ref[...] = delta + delta1_ref[...]
        db_ref[...] = delta.astype(bf16)

    values = [gain, keep, got, sums, others, carried, inner, inner_other, delta1]
    return call(
        kernel,
        [((rows, half), f32), ((rows, half), bf16)],
        [(VMEM, value) for value in values],
    )


def stacked(columns):
    def kernel(*refs):
        for chip, ref in enumerate(refs[:-1]):
            refs[-1][chip] = ref[...]

    outs = [((len(columns), *columns[0].shape), bf16)]
    return call(kernel, outs, [(VMEM, value) for value in columns])[0]


def left_side(columns, others):
    group, height, rows = columns.shape

    def kernel(own_ref, other_ref, out_ref):
        for index, pair in enumerate([(own_ref, other_ref), (other_ref, own_ref)]):

            @pl.when(lax.axis_index("section") == index)
            def _():
                for k, ref in enumerate(pair):
                    for chip in range(group):
                        base = (k * group + chip) * rows
                        out_ref[:, base : base + rows] = ref[chip]

    return call(
        kernel,
        [((height, 2 * group * rows), bf16)],
        [(VMEM, value) for value in (columns, others)],
    )[0]


def weight_terms(left, grads, lanes):
    rows = grads[0].shape[0]
    height = left.shape[0]
    start, width = lanes

    def kernel(left_ref, *refs):
        grads_refs, (keep_ref, send_ref, right) = refs[:-3], refs[-3:]
        for index, grads_ref in enumerate(grads_refs):
            right[index * rows : (index + 1) * rows] = grads_ref[:, start : start + width]
        for k, (first, second) in enumerate([(keep_ref, send_ref), (send_ref, keep_ref)]):

            @pl.when(lax.axis_index("section") == k)
            def _():
                terms = jnp.dot(left_ref[...], right[...], preferred_element_type=f32)
                first[...] = terms[: height // 2]
                second[...] = terms[height // 2 :]

    return call(
        kernel,
        [((height // 2, width), f32)] * 2,
        [(VMEM, value) for value in [left, *grads]],
        [pltpu.VMEM((len(grads) * rows, width), bf16)],
    )


def chip_sum(keep, other, block):
    height, width = keep.shape

    def kernel(keep_ref, other_ref, own_ref, *away_refs):
        total = keep_ref[...] + other_ref[...]
        own_ref[...] = total[:block]
        for index, away_ref in enumerate(away_refs):
            away_ref[...] = total[(index + 1) * block : (index + 2) * block].astype(bf16)

    outs = [((block, width), f32)] + [((block, width), bf16)] * (height // block - 1)
    return call(kernel, outs, [(VMEM, keep), (VMEM, other)])


def final_sum(own, others, gains, half):
    block = own[0].shape[0]
    count = len(others[0])

    def kernel(*refs):
        gain_refs, refs = refs[: len(gains)], refs[len(gains) :]
        weight_out, gain_out = refs[-2:]
        start = 0
        for part in range(len(own)):
            own_ref, *other_refs = refs[part * (count + 1) : (part + 1) * (count + 1)]
            total = own_ref[...]
            for other_ref in other_refs:
                total = total + other_ref[...].astype(f32)
            width = own_ref.shape[1]
            weight_out[:, start : start + width] = total
            start += width
        sums = [ref[:1] for ref in gain_refs]
        while len(sums) > 1:
            sums = [a + b for a, b in zip(sums[::2], sums[1::2])]
        gain_out[...] = sums[0].reshape(half)

    values = [value for mine, theirs in zip(own, others) for value in (mine, *theirs)]
    ins = [(VMEM, value) for value in (*gains, *values)]
    return call(kernel, [((block, half), f32), ((half,), f32)], ins)


def place(order, total, other):
    rows, half = total.shape

    def kernel(order_ref, total_ref, other_ref, out_ref):
        micro = order_ref[0, own_slot()]
        out_ref[micro] = total_ref[...]
        out_ref[1 - micro] = other_ref[...]

    ins = [(SMEM, order), (VMEM, total), (VMEM, other)]
    return call(kernel, [((2, rows, half), f32)], ins)[0]


def shards(states, injection, cotangent, gain, weight, exits, order):
    stash = states[0]
    slots, rows, features = stash.shape
    half = weight.shape[1]
    dp = lax.axis_index("dp")
    chips = lax.axis_size("dp")
    group = 4
    groups = chips // group
    assert slots == 2 and lax.axis_size("section") == 2 and lax.axis_size("mp") == 2
    assert chips % group == 0 and groups & (groups - 1) == 0

    def across(value, distance):
        return lax.ppermute(value, "dp", [(i, i ^ distance) for i in range(chips)])

    def gathered(value):
        return [value] + [across(value, distance) for distance in range(1, group)]

    block = features // (2 * chips)
    gain = gain.reshape(1, half)
    weight = load(weight)
    keep, send, columns = forward(stash, weight, injection, order, chips, group)
    columns = columns[:1] + [across(columns[distance], distance) for distance in range(1, group)]
    got = swap(send, "section")
    sums = row_sums(order, cotangent, gain, keep, got)
    others = opposite(sums)
    others, columns[1:-1] = lax.optimization_barrier((others, columns[1:-1]))
    db1, delta1, gain1, away = lower_iteration1(
        order, exits, cotangent, gain, keep, got, sums, others, weight
    )
    sent = opposite(away)
    grads1 = gathered(db1)
    kept = kept_half(db1, weight)
    kept, sent, columns[-1] = lax.optimization_barrier((kept, sent, columns[-1]))

    carried, inner, gains = carry(
        order, exits, cotangent, gain, keep, got, sums, others, kept, sent, gain1, features
    )
    inner_other, gains_other = opposite(inner), swap(gains, "section")
    columns = stacked(columns)
    gains = gains + gains_other
    near_gains = across(gains, 1)
    inner_other, near_gains, columns, *grads1[1:] = lax.optimization_barrier(
        (inner_other, near_gains, columns, *grads1[1:])
    )
    total, db0 = iteration0(
        gain, keep, got, sums, others, carried, inner, inner_other, delta1, features
    )
    grads0 = gathered(db0)
    columns, total = lax.optimization_barrier((columns, total))
    left = left_side(columns, opposite(columns))

    gains = gains + near_gains
    far_gains = across(gains, 2)
    left, grads0, far_gains = lax.optimization_barrier((left, grads0, far_gains))
    gains = gains + far_gains

    cut = (half // 2 + 127) // 128 * 128
    terms = [
        weight_terms(left, grads0 + grads1, lanes) for lanes in [(0, cut), (cut, half - cut)]
    ]
    arrived = [swap(send, "section") for _, send in terms]
    own, others = [], []
    for part, (keep, _) in enumerate(terms):
        if part:
            keep, *_ = lax.optimization_barrier((keep, *aways))
            total, *_ = lax.optimization_barrier((total, *aways))
        mine, *aways = chip_sum(keep, arrived[part], block)
        own.append(mine)
        others.append([across(away, group * (i + 1)) for i, away in enumerate(aways)])
    gains, *_ = lax.optimization_barrier((gains, *aways))
    gains = [gains] + [across(gains, group * other) for other in range(1, groups)]
    d_injection = place(order, total, swap(total, "section"))
    others[1], d_injection = lax.optimization_barrier((others[1], d_injection))
    d_weight, d_gain = final_sum(own, others, gains, half)
    return (d_injection, d_weight, d_gain)


def solution(mesh):
    return jax.shard_map(
        shards,
        mesh=mesh,
        in_specs=(
            P("section", "dp", None, None),
            P("dp", None, "mp"),
            P("dp", None, "mp"),
            P("mp"),
            P(None, "mp"),
            P("dp"),
            P("dp", None),
        ),
        out_specs=(P("dp", None, "mp"), P(("section", "dp"), "mp"), P("mp")),
        check_vma=False,
    )
```

```python
import jax
import jax.numpy as jnp
from jax import lax
from jax.experimental import pallas as pl
from jax.experimental.pallas import tpu as pltpu
from jax.sharding import PartitionSpec as P

epsilon = 1e-06
f32, bf16 = jnp.float32, jnp.bfloat16
VMEM = pl.BlockSpec(memory_space=pltpu.VMEM)
SMEM = pl.BlockSpec(memory_space=pltpu.SMEM)
HBM = pl.BlockSpec(memory_space=pltpu.HBM)


def call(kernel, outs, ins, scratch=(), limit=24):
    shapes = [jax.ShapeDtypeStruct(shape, kind) for shape, kind in outs]
    specs, values = zip(*ins)
    return pl.pallas_call(
        kernel,
        out_shape=shapes,
        in_specs=list(specs),
        out_specs=[VMEM] * len(shapes),
        scratch_shapes=list(scratch),
        compiler_params=pltpu.CompilerParams(vmem_limit_bytes=limit * 2**20),
        cost_estimate=pl.CostEstimate(flops=1000, bytes_accessed=1000, transcendentals=0),
    )(*values)


def swap(value, axis):
    return lax.ppermute(value, axis, [(0, 1), (1, 0)])


def opposite(value):
    return lax.ppermute(value, ("section", "mp"), [(i, 3 - i) for i in range(4)])


def own_slot():
    return lax.axis_index("section") ^ lax.axis_index("mp")


def chunks_of(total, size):
    return [(start, min(size, total - start)) for start in range(0, total, size)]


def to_rows(columns):
    rows = columns[0].shape[0]
    lane = lax.broadcasted_iota(jnp.int32, (rows, 128), 1)
    wide = jnp.zeros((rows, 128), f32)
    for index, column in enumerate(columns):
        wide = jnp.where(lane == index, column, wide)
    return wide.T[:8]


def to_columns(packed):
    return jnp.concatenate([packed] * 16, axis=0).T


def load(weight):
    parts = chunks_of(weight.shape[0], 512)

    def kernel(weight_hbm, w, sems):
        copies = []
        for index, (start, size) in enumerate(parts):
            part = pl.ds(start, size)
            copies.append(pltpu.make_async_copy(weight_hbm.at[part], w.at[part], sems.at[index]))
            copies[-1].start()
        for copy in copies:
            copy.wait()

    return call(
        kernel,
        [(weight.shape, bf16)],
        [(HBM, weight)],
        [pltpu.SemaphoreType.DMA((len(parts),))],
        limit=42,
    )[0]


def forward(stash, weight, injection, order, chips, group):
    slots, rows, features = stash.shape
    half = weight.shape[1]
    block = features // (2 * chips)
    groups = chips // group
    height = 2 * groups * block

    def kernel(order_ref, stash_ref, weight_ref, inj_ref, keep_ref, send_ref, *refs):
        *out_refs, turned, acc = refs
        slot = own_slot()
        left = stash_ref[...].reshape(slots * rows, features)
        for start, size in chunks_of(half, 512):
            part = slice(start, start + size)
            term = jnp.dot(left, weight_ref[:, part], preferred_element_type=f32)
            acc[:, :, part] = term.reshape(slots, rows, size)
        keep_ref[...] = acc[slot] + inj_ref[order_ref[0, slot]].astype(f32)
        send_ref[...] = acc[1 - slot] + inj_ref[order_ref[0, 1 - slot]].astype(f32)
        if out_refs:
            turned[...] = stash_ref[slot].T
        dp = lax.axis_index("dp")
        for distance, out_ref in enumerate(out_refs):
            for half_index in range(2):
                for other in range(groups):
                    chip = dp ^ (distance + group * other)
                    source = pl.multiple_of((half_index * chips + chip) * block, 16)
                    base = (half_index * groups + other) * block
                    out_ref[base : base + block] = turned[pl.ds(source, block)]

    pieces = group if block % 16 == 0 else 0
    keep, send, *columns = call(
        kernel,
        [((rows, half), f32)] * 2 + [((height, rows), bf16)] * pieces,
        [(SMEM, order), (VMEM, stash), (VMEM, weight), (VMEM, injection)],
        [pltpu.VMEM((features, rows), bf16), pltpu.VMEM((slots, rows, half), f32)],
    )
    if not columns:
        turned = lax.dynamic_index_in_dim(stash, own_slot(), 0, keepdims=False).T
        turned = turned.reshape(2, chips, block, rows)
        for distance in range(group):
            picked = [
                lax.dynamic_index_in_dim(
                    turned, lax.axis_index("dp") ^ (distance + group * other), 1, keepdims=False
                )
                for other in range(groups)
            ]
            columns.append(jnp.stack(picked, axis=1).reshape(height, rows))
    return keep, send, columns


def row_sums(order, cotangent, gain, keep, got):
    rows = keep.shape[0]

    def kernel(order_ref, cot_ref, gain_ref, keep_ref, got_ref, out_ref):
        sec = lax.axis_index("section")
        first = sec == 0
        keep, got = keep_ref[...], got_ref[...]
        pre1, pre0 = jnp.where(first, got, keep), jnp.where(first, keep, got)
        u = cot_ref[order_ref[0, own_slot()]].astype(f32) * gain_ref[...]
        sums = [pre1 * pre1, u * pre1, pre0 * pre0]
        out_ref[...] = to_rows([jnp.sum(each, axis=1, keepdims=True) for each in sums])

    ins = [(SMEM, order), (VMEM, cotangent), (VMEM, gain), (VMEM, keep), (VMEM, got)]
    return call(kernel, [((8, rows), f32)], ins)[0]


def delta_of(pre, u, squares, inner, features):
    radius = jnp.sqrt(squares / features + epsilon)
    inverse = 1.0 / radius
    normed = pre * inverse
    return normed, (u - normed * (inner * inverse / features)) * inverse


def lower_iteration1(order, exits, cotangent, gain, keep, got, sums, others, weight):
    rows, half = keep.shape
    features = weight.shape[0]

    def kernel(order_ref, exits_ref, cot_ref, gain_ref, keep_ref, got_ref, sums_ref, others_ref,
               weight_ref, db_ref, delta_ref, gain_out, away_ref):
        sec, mp = lax.axis_index("section"), lax.axis_index("mp")
        micro = order_ref[0, own_slot()]
        live = jnp.where(exits_ref[micro] > 1, 1.0, 0.0)
        stats = to_columns(sums_ref[...] + others_ref[...])
        pre = jnp.where(sec == 0, got_ref[...], keep_ref[...])
        cot = cot_ref[micro].astype(f32)
        normed, delta = delta_of(pre, cot * gain_ref[...], stats[:, 0:1], stats[:, 1:2], features)
        delta = delta * live
        delta_ref[...] = delta
        db = delta.astype(bf16)
        db_ref[...] = db
        gain_out[...] = jnp.sum(cot * normed, axis=0, keepdims=True) * live
        part = weight_ref[pl.ds(pl.multiple_of((1 - mp) * half, 128), half)]
        away_ref[...] = lax.dot_general(
            part, db, (((1,), (1,)), ((), ())), preferred_element_type=f32
        ).astype(bf16)

    return call(
        kernel,
        [((rows, half), bf16), ((rows, half), f32), ((1, half), f32), ((half, rows), bf16)],
        [(SMEM, order), (SMEM, exits), (VMEM, cotangent), (VMEM, gain), (VMEM, keep), (VMEM, got),
         (VMEM, sums), (VMEM, others), (VMEM, weight)],
    )


def kept_half(db, weight):
    rows, half = db.shape

    def kernel(db_ref, weight_ref, out_ref):
        part = weight_ref[pl.ds(pl.multiple_of(lax.axis_index("mp") * half, 128), half)]
        out_ref[...] = lax.dot_general(
            part, db_ref[...], (((1,), (1,)), ((), ())), preferred_element_type=f32
        )

    return call(kernel, [((half, rows), f32)], [(VMEM, db), (VMEM, weight)])[0]


def carry(order, exits, cotangent, gain, keep, got, sums, others, kept, sent, gain1, features):
    rows, half = keep.shape

    def kernel(order_ref, exits_ref, cot_ref, gain_ref, keep_ref, got_ref, sums_ref, others_ref,
               kept_ref, sent_ref, gain1_ref, carried_ref, inner_ref, gain_out):
        sec = lax.axis_index("section")
        micro = order_ref[0, own_slot()]
        passed = (kept_ref[...] + sent_ref[...].astype(f32)).astype(bf16).astype(f32).T
        cot = cot_ref[micro].astype(f32)
        carried = jnp.where(exits_ref[micro] > 1, passed, cot)
        carried_ref[...] = carried
        pre = jnp.where(sec == 0, keep_ref[...], got_ref[...])
        inner = jnp.sum(carried * gain_ref[...] * pre, axis=1, keepdims=True)
        inner_ref[...] = to_rows([inner])
        squares = to_columns(sums_ref[...] + others_ref[...])[:, 2:3]
        inverse = 1.0 / jnp.sqrt(squares / features + epsilon)
        gains = jnp.sum(carried * (pre * inverse), axis=0, keepdims=True) + gain1_ref[...]
        gain_out[...] = jnp.broadcast_to(gains, (8, half))

    return call(
        kernel,
        [((rows, half), f32), ((8, rows), f32), ((8, half), f32)],
        [(SMEM, order), (SMEM, exits)]
        + [
            (VMEM, value)
            for value in (cotangent, gain, keep, got, sums, others, kept, sent, gain1)
        ],
    )


def iteration0(gain, keep, got, sums, others, carried, inner, inner_other, delta1, features):
    rows, half = keep.shape

    def kernel(gain_ref, keep_ref, got_ref, sums_ref, others_ref, carried_ref, inner_ref, other_ref,
               delta1_ref, total_ref, db_ref):
        sec = lax.axis_index("section")
        squares = to_columns(sums_ref[...] + others_ref[...])[:, 2:3]
        inner = to_columns(inner_ref[...] + other_ref[...])[:, 0:1]
        pre = jnp.where(sec == 0, keep_ref[...], got_ref[...])
        _, delta = delta_of(pre, carried_ref[...] * gain_ref[...], squares, inner, features)
        total_ref[...] = delta + delta1_ref[...]
        db_ref[...] = delta.astype(bf16)

    values = [gain, keep, got, sums, others, carried, inner, inner_other, delta1]
    return call(
        kernel,
        [((rows, half), f32), ((rows, half), bf16)],
        [(VMEM, value) for value in values],
    )


def stacked(columns):
    def kernel(*refs):
        for chip, ref in enumerate(refs[:-1]):
            refs[-1][chip] = ref[...]

    outs = [((len(columns), *columns[0].shape), bf16)]
    return call(kernel, outs, [(VMEM, value) for value in columns])[0]


def left_side(columns, others):
    group, height, rows = columns.shape

    def kernel(own_ref, other_ref, out_ref):
        for index, pair in enumerate([(own_ref, other_ref), (other_ref, own_ref)]):

            @pl.when(lax.axis_index("section") == index)
            def _():
                for k, ref in enumerate(pair):
                    for chip in range(group):
                        base = (k * group + chip) * rows
                        out_ref[:, base : base + rows] = ref[chip]

    return call(
        kernel,
        [((height, 2 * group * rows), bf16)],
        [(VMEM, value) for value in (columns, others)],
    )[0]


def weight_terms(left, grads, lanes):
    rows = grads[0].shape[0]
    height = left.shape[0]
    start, width = lanes

    def kernel(left_ref, *refs):
        grads_refs, (keep_ref, send_ref, right) = refs[:-3], refs[-3:]
        for index, grads_ref in enumerate(grads_refs):
            right[index * rows : (index + 1) * rows] = grads_ref[:, start : start + width]
        for k, (first, second) in enumerate([(keep_ref, send_ref), (send_ref, keep_ref)]):

            @pl.when(lax.axis_index("section") == k)
            def _():
                terms = jnp.dot(left_ref[...], right[...], preferred_element_type=f32)
                first[...] = terms[: height // 2]
                second[...] = terms[height // 2 :]

    return call(
        kernel,
        [((height // 2, width), f32)] * 2,
        [(VMEM, value) for value in [left, *grads]],
        [pltpu.VMEM((len(grads) * rows, width), bf16)],
    )


def chip_sum(keep, other, block):
    height, width = keep.shape

    def kernel(keep_ref, other_ref, own_ref, *away_refs):
        total = keep_ref[...] + other_ref[...]
        own_ref[...] = total[:block]
        for index, away_ref in enumerate(away_refs):
            away_ref[...] = total[(index + 1) * block : (index + 2) * block].astype(bf16)

    outs = [((block, width), f32)] + [((block, width), bf16)] * (height // block - 1)
    return call(kernel, outs, [(VMEM, keep), (VMEM, other)])


def final_sum(own, others, gains, half):
    block = own[0].shape[0]
    count = len(others[0])

    def kernel(*refs):
        gain_refs, refs = refs[: len(gains)], refs[len(gains) :]
        weight_out, gain_out = refs[-2:]
        start = 0
        for part in range(len(own)):
            own_ref, *other_refs = refs[part * (count + 1) : (part + 1) * (count + 1)]
            total = own_ref[...]
            for other_ref in other_refs:
                total = total + other_ref[...].astype(f32)
            width = own_ref.shape[1]
            weight_out[:, start : start + width] = total
            start += width
        sums = [ref[:1] for ref in gain_refs]
        while len(sums) > 1:
            sums = [a + b for a, b in zip(sums[::2], sums[1::2])]
        gain_out[...] = sums[0].reshape(half)

    values = [value for mine, theirs in zip(own, others) for value in (mine, *theirs)]
    ins = [(VMEM, value) for value in (*gains, *values)]
    return call(kernel, [((block, half), f32), ((half,), f32)], ins)


def place(order, total, other):
    rows, half = total.shape

    def kernel(order_ref, total_ref, other_ref, out_ref):
        micro = order_ref[0, own_slot()]
        out_ref[micro] = total_ref[...]
        out_ref[1 - micro] = other_ref[...]

    ins = [(SMEM, order), (VMEM, total), (VMEM, other)]
    return call(kernel, [((2, rows, half), f32)], ins)[0]


def shards(states, injection, cotangent, gain, weight, exits, order):
    stash = states[0]
    slots, rows, features = stash.shape
    half = weight.shape[1]
    dp = lax.axis_index("dp")
    chips = lax.axis_size("dp")
    group = 4
    groups = chips // group
    assert slots == 2 and lax.axis_size("section") == 2 and lax.axis_size("mp") == 2
    assert chips % group == 0 and groups & (groups - 1) == 0

    def across(value, distance):
        return lax.ppermute(value, "dp", [(i, i ^ distance) for i in range(chips)])

    def gathered(value):
        return [value] + [across(value, distance) for distance in range(1, group)]

    block = features // (2 * chips)
    gain = gain.reshape(1, half)
    weight = load(weight)
    keep, send, columns = forward(stash, weight, injection, order, chips, group)
    columns = columns[:1] + [across(columns[distance], distance) for distance in range(1, group)]
    got = swap(send, "section")
    sums = row_sums(order, cotangent, gain, keep, got)
    others = opposite(sums)
    db1, delta1, gain1, away = lower_iteration1(
        order, exits, cotangent, gain, keep, got, sums, others, weight
    )
    db1, away, columns = lax.optimization_barrier((db1, away, columns))
    sent = opposite(away)
    grads1 = gathered(db1)
    kept = kept_half(db1, weight)
    kept, sent = lax.optimization_barrier((kept, sent))

    carried, inner, gains = carry(
        order, exits, cotangent, gain, keep, got, sums, others, kept, sent, gain1, features
    )
    inner_other, gains_other = opposite(inner), swap(gains, "section")
    columns = stacked(columns)
    gains = gains + gains_other
    near_gains = across(gains, 1)
    total, db0 = iteration0(
        gain, keep, got, sums, others, carried, inner, inner_other, delta1, features
    )
    db0, near_gains, columns, *grads1[1:] = lax.optimization_barrier(
        (db0, near_gains, columns, *grads1[1:])
    )
    grads0 = gathered(db0)
    columns, total = lax.optimization_barrier((columns, total))
    left = left_side(columns, opposite(columns))

    gains = gains + near_gains
    far_gains = across(gains, 2)
    left, grads0, far_gains = lax.optimization_barrier((left, grads0, far_gains))
    gains = gains + far_gains

    cut = (half // 2 + 127) // 128 * 128
    terms = [
        weight_terms(left, grads0 + grads1, lanes) for lanes in [(0, cut), (cut, half - cut)]
    ]
    arrived = [swap(send, "section") for _, send in terms]
    own, others = [], []
    for part, (keep, _) in enumerate(terms):
        if part:
            keep, *_ = lax.optimization_barrier((keep, *aways))
            total, *_ = lax.optimization_barrier((total, *aways))
        mine, *aways = chip_sum(keep, arrived[part], block)
        own.append(mine)
        others.append([across(away, group * (i + 1)) for i, away in enumerate(aways)])
    gains, *_ = lax.optimization_barrier((gains, *aways))
    gains = [gains] + [across(gains, group * other) for other in range(1, groups)]
    d_injection = place(order, total, swap(total, "section"))
    others[1], d_injection = lax.optimization_barrier((others[1], d_injection))
    d_weight, d_gain = final_sum(own, others, gains, half)
    return (d_injection, d_weight, d_gain)


def solution(mesh):
    return jax.shard_map(
        shards,
        mesh=mesh,
        in_specs=(
            P("section", "dp", None, None),
            P("dp", None, "mp"),
            P("dp", None, "mp"),
            P("mp"),
            P(None, "mp"),
            P("dp"),
            P("dp", None),
        ),
        out_specs=(P("dp", None, "mp"), P(("section", "dp"), "mp"), P("mp")),
        check_vma=False,
    )
```

```python
import jax
import jax.numpy as jnp
from jax import lax
from jax.experimental import pallas as pl
from jax.experimental.pallas import tpu as pltpu
from jax.sharding import PartitionSpec as P

epsilon = 1e-06
f32, bf16 = jnp.float32, jnp.bfloat16
VMEM = pl.BlockSpec(memory_space=pltpu.VMEM)
SMEM = pl.BlockSpec(memory_space=pltpu.SMEM)
HBM = pl.BlockSpec(memory_space=pltpu.HBM)


def call(kernel, outs, ins, scratch=(), limit=24):
    shapes = [jax.ShapeDtypeStruct(shape, kind) for shape, kind in outs]
    specs, values = zip(*ins)
    return pl.pallas_call(
        kernel,
        out_shape=shapes,
        in_specs=list(specs),
        out_specs=[VMEM] * len(shapes),
        scratch_shapes=list(scratch),
        compiler_params=pltpu.CompilerParams(vmem_limit_bytes=limit * 2**20),
        cost_estimate=pl.CostEstimate(flops=1000, bytes_accessed=1000, transcendentals=0),
    )(*values)


def swap(value, axis):
    return lax.ppermute(value, axis, [(0, 1), (1, 0)])


def opposite(value):
    return lax.ppermute(value, ("section", "mp"), [(i, 3 - i) for i in range(4)])


def own_slot():
    return lax.axis_index("section") ^ lax.axis_index("mp")


def chunks_of(total, size):
    return [(start, min(size, total - start)) for start in range(0, total, size)]


def to_rows(columns):
    rows = columns[0].shape[0]
    lane = lax.broadcasted_iota(jnp.int32, (rows, 128), 1)
    wide = jnp.zeros((rows, 128), f32)
    for index, column in enumerate(columns):
        wide = jnp.where(lane == index, column, wide)
    return wide.T[:8]


def to_columns(packed):
    return jnp.concatenate([packed] * 16, axis=0).T


def load(weight):
    parts = chunks_of(weight.shape[0], 512)

    def kernel(weight_hbm, w, sems):
        copies = []
        for index, (start, size) in enumerate(parts):
            part = pl.ds(start, size)
            copies.append(pltpu.make_async_copy(weight_hbm.at[part], w.at[part], sems.at[index]))
            copies[-1].start()
        for copy in copies:
            copy.wait()

    return call(
        kernel,
        [(weight.shape, bf16)],
        [(HBM, weight)],
        [pltpu.SemaphoreType.DMA((len(parts),))],
        limit=42,
    )[0]


def forward(stash, weight, injection, order, chips, group):
    slots, rows, features = stash.shape
    half = weight.shape[1]
    block = features // (2 * chips)
    groups = chips // group
    height = 2 * groups * block

    def kernel(order_ref, stash_ref, weight_ref, inj_ref, keep_ref, send_ref, *refs):
        *out_refs, turned, acc = refs
        slot = own_slot()
        left = stash_ref[...].reshape(slots * rows, features)
        for start, size in chunks_of(half, 256):
            part = slice(start, start + size)
            term = jnp.dot(left, weight_ref[:, part], preferred_element_type=f32)
            acc[:, :, part] = term.reshape(slots, rows, size)
        keep_ref[...] = acc[slot] + inj_ref[order_ref[0, slot]].astype(f32)
        send_ref[...] = acc[1 - slot] + inj_ref[order_ref[0, 1 - slot]].astype(f32)
        if out_refs:
            turned[...] = stash_ref[slot].T
        dp = lax.axis_index("dp")
        for distance, out_ref in enumerate(out_refs):
            for half_index in range(2):
                for other in range(groups):
                    chip = dp ^ (distance + group * other)
                    source = pl.multiple_of((half_index * chips + chip) * block, 16)
                    base = (half_index * groups + other) * block
                    out_ref[base : base + block] = turned[pl.ds(source, block)]

    pieces = group if block % 16 == 0 else 0
    keep, send, *columns = call(
        kernel,
        [((rows, half), f32)] * 2 + [((height, rows), bf16)] * pieces,
        [(SMEM, order), (VMEM, stash), (VMEM, weight), (VMEM, injection)],
        [pltpu.VMEM((features, rows), bf16), pltpu.VMEM((slots, rows, half), f32)],
    )
    if not columns:
        turned = lax.dynamic_index_in_dim(stash, own_slot(), 0, keepdims=False).T
        turned = turned.reshape(2, chips, block, rows)
        for distance in range(group):
            picked = [
                lax.dynamic_index_in_dim(
                    turned, lax.axis_index("dp") ^ (distance + group * other), 1, keepdims=False
                )
                for other in range(groups)
            ]
            columns.append(jnp.stack(picked, axis=1).reshape(height, rows))
    return keep, send, columns


def row_sums(order, cotangent, gain, keep, got):
    rows = keep.shape[0]

    def kernel(order_ref, cot_ref, gain_ref, keep_ref, got_ref, out_ref):
        sec = lax.axis_index("section")
        first = sec == 0
        keep, got = keep_ref[...], got_ref[...]
        pre1, pre0 = jnp.where(first, got, keep), jnp.where(first, keep, got)
        u = cot_ref[order_ref[0, own_slot()]].astype(f32) * gain_ref[...]
        sums = [pre1 * pre1, u * pre1, pre0 * pre0]
        out_ref[...] = to_rows([jnp.sum(each, axis=1, keepdims=True) for each in sums])

    ins = [(SMEM, order), (VMEM, cotangent), (VMEM, gain), (VMEM, keep), (VMEM, got)]
    return call(kernel, [((8, rows), f32)], ins)[0]


def delta_of(pre, u, squares, inner, features):
    radius = jnp.sqrt(squares / features + epsilon)
    inverse = 1.0 / radius
    normed = pre * inverse
    return normed, (u - normed * (inner * inverse / features)) * inverse


def lower_iteration1(order, exits, cotangent, gain, keep, got, sums, others, weight):
    rows, half = keep.shape
    features = weight.shape[0]

    def kernel(order_ref, exits_ref, cot_ref, gain_ref, keep_ref, got_ref, sums_ref, others_ref,
               weight_ref, db_ref, delta_ref, gain_out, away_ref):
        sec, mp = lax.axis_index("section"), lax.axis_index("mp")
        micro = order_ref[0, own_slot()]
        live = jnp.where(exits_ref[micro] > 1, 1.0, 0.0)
        stats = to_columns(sums_ref[...] + others_ref[...])
        pre = jnp.where(sec == 0, got_ref[...], keep_ref[...])
        cot = cot_ref[micro].astype(f32)
        normed, delta = delta_of(pre, cot * gain_ref[...], stats[:, 0:1], stats[:, 1:2], features)
        delta = delta * live
        delta_ref[...] = delta
        db = delta.astype(bf16)
        db_ref[...] = db
        gain_out[...] = jnp.sum(cot * normed, axis=0, keepdims=True) * live
        part = weight_ref[pl.ds(pl.multiple_of((1 - mp) * half, 128), half)]
        away_ref[...] = lax.dot_general(
            part, db, (((1,), (1,)), ((), ())), preferred_element_type=f32
        ).astype(bf16)

    return call(
        kernel,
        [((rows, half), bf16), ((rows, half), f32), ((1, half), f32), ((half, rows), bf16)],
        [(SMEM, order), (SMEM, exits), (VMEM, cotangent), (VMEM, gain), (VMEM, keep), (VMEM, got),
         (VMEM, sums), (VMEM, others), (VMEM, weight)],
    )


def kept_half(db, weight):
    rows, half = db.shape

    def kernel(db_ref, weight_ref, out_ref):
        part = weight_ref[pl.ds(pl.multiple_of(lax.axis_index("mp") * half, 128), half)]
        out_ref[...] = lax.dot_general(
            part, db_ref[...], (((1,), (1,)), ((), ())), preferred_element_type=f32
        )

    return call(kernel, [((half, rows), f32)], [(VMEM, db), (VMEM, weight)])[0]


def carry(order, exits, cotangent, gain, keep, got, sums, others, kept, sent, gain1, features):
    rows, half = keep.shape

    def kernel(order_ref, exits_ref, cot_ref, gain_ref, keep_ref, got_ref, sums_ref, others_ref,
               kept_ref, sent_ref, gain1_ref, carried_ref, inner_ref, gain_out):
        sec = lax.axis_index("section")
        micro = order_ref[0, own_slot()]
        passed = (kept_ref[...] + sent_ref[...].astype(f32)).astype(bf16).astype(f32).T
        cot = cot_ref[micro].astype(f32)
        carried = jnp.where(exits_ref[micro] > 1, passed, cot)
        carried_ref[...] = carried
        pre = jnp.where(sec == 0, keep_ref[...], got_ref[...])
        inner = jnp.sum(carried * gain_ref[...] * pre, axis=1, keepdims=True)
        inner_ref[...] = to_rows([inner])
        squares = to_columns(sums_ref[...] + others_ref[...])[:, 2:3]
        inverse = 1.0 / jnp.sqrt(squares / features + epsilon)
        gains = jnp.sum(carried * (pre * inverse), axis=0, keepdims=True) + gain1_ref[...]
        gain_out[...] = jnp.broadcast_to(gains, (8, half))

    return call(
        kernel,
        [((rows, half), f32), ((8, rows), f32), ((8, half), f32)],
        [(SMEM, order), (SMEM, exits)]
        + [
            (VMEM, value)
            for value in (cotangent, gain, keep, got, sums, others, kept, sent, gain1)
        ],
    )


def iteration0(gain, keep, got, sums, others, carried, inner, inner_other, delta1, features):
    rows, half = keep.shape

    def kernel(gain_ref, keep_ref, got_ref, sums_ref, others_ref, carried_ref, inner_ref, other_ref,
               delta1_ref, total_ref, db_ref):
        sec = lax.axis_index("section")
        squares = to_columns(sums_ref[...] + others_ref[...])[:, 2:3]
        inner = to_columns(inner_ref[...] + other_ref[...])[:, 0:1]
        pre = jnp.where(sec == 0, keep_ref[...], got_ref[...])
        _, delta = delta_of(pre, carried_ref[...] * gain_ref[...], squares, inner, features)
        total_ref[...] = delta + delta1_ref[...]
        db_ref[...] = delta.astype(bf16)

    values = [gain, keep, got, sums, others, carried, inner, inner_other, delta1]
    return call(
        kernel,
        [((rows, half), f32), ((rows, half), bf16)],
        [(VMEM, value) for value in values],
    )


def stacked(columns):
    def kernel(*refs):
        for chip, ref in enumerate(refs[:-1]):
            refs[-1][chip] = ref[...]

    outs = [((len(columns), *columns[0].shape), bf16)]
    return call(kernel, outs, [(VMEM, value) for value in columns])[0]


def left_side(columns, others):
    group, height, rows = columns.shape

    def kernel(own_ref, other_ref, out_ref):
        for index, pair in enumerate([(own_ref, other_ref), (other_ref, own_ref)]):

            @pl.when(lax.axis_index("section") == index)
            def _():
                for k, ref in enumerate(pair):
                    for chip in range(group):
                        base = (k * group + chip) * rows
                        out_ref[:, base : base + rows] = ref[chip]

    return call(
        kernel,
        [((height, 2 * group * rows), bf16)],
        [(VMEM, value) for value in (columns, others)],
    )[0]


def weight_terms(left, grads, lanes):
    rows = grads[0].shape[0]
    height = left.shape[0]
    start, width = lanes

    def kernel(left_ref, *refs):
        grads_refs, (keep_ref, send_ref, right) = refs[:-3], refs[-3:]
        for index, grads_ref in enumerate(grads_refs):
            right[index * rows : (index + 1) * rows] = grads_ref[:, start : start + width]
        for k, (first, second) in enumerate([(keep_ref, send_ref), (send_ref, keep_ref)]):

            @pl.when(lax.axis_index("section") == k)
            def _():
                terms = jnp.dot(left_ref[...], right[...], preferred_element_type=f32)
                first[...] = terms[: height // 2]
                second[...] = terms[height // 2 :]

    return call(
        kernel,
        [((height // 2, width), f32)] * 2,
        [(VMEM, value) for value in [left, *grads]],
        [pltpu.VMEM((len(grads) * rows, width), bf16)],
    )


def chip_sum(keep, other, block):
    height, width = keep.shape

    def kernel(keep_ref, other_ref, own_ref, *away_refs):
        total = keep_ref[...] + other_ref[...]
        own_ref[...] = total[:block]
        for index, away_ref in enumerate(away_refs):
            away_ref[...] = total[(index + 1) * block : (index + 2) * block].astype(bf16)

    outs = [((block, width), f32)] + [((block, width), bf16)] * (height // block - 1)
    return call(kernel, outs, [(VMEM, keep), (VMEM, other)])


def final_sum(own, others, gains, half):
    block = own[0].shape[0]
    count = len(others[0])

    def kernel(*refs):
        gain_refs, refs = refs[: len(gains)], refs[len(gains) :]
        weight_out, gain_out = refs[-2:]
        start = 0
        for part in range(len(own)):
            own_ref, *other_refs = refs[part * (count + 1) : (part + 1) * (count + 1)]
            total = own_ref[...]
            for other_ref in other_refs:
                total = total + other_ref[...].astype(f32)
            width = own_ref.shape[1]
            weight_out[:, start : start + width] = total
            start += width
        sums = [ref[:1] for ref in gain_refs]
        while len(sums) > 1:
            sums = [a + b for a, b in zip(sums[::2], sums[1::2])]
        gain_out[...] = sums[0].reshape(half)

    values = [value for mine, theirs in zip(own, others) for value in (mine, *theirs)]
    ins = [(VMEM, value) for value in (*gains, *values)]
    return call(kernel, [((block, half), f32), ((half,), f32)], ins)


def place(order, total, other):
    rows, half = total.shape

    def kernel(order_ref, total_ref, other_ref, out_ref):
        micro = order_ref[0, own_slot()]
        out_ref[micro] = total_ref[...]
        out_ref[1 - micro] = other_ref[...]

    ins = [(SMEM, order), (VMEM, total), (VMEM, other)]
    return call(kernel, [((2, rows, half), f32)], ins)[0]


def shards(states, injection, cotangent, gain, weight, exits, order):
    stash = states[0]
    slots, rows, features = stash.shape
    half = weight.shape[1]
    dp = lax.axis_index("dp")
    chips = lax.axis_size("dp")
    group = 4
    groups = chips // group
    assert slots == 2 and lax.axis_size("section") == 2 and lax.axis_size("mp") == 2
    assert chips % group == 0 and groups & (groups - 1) == 0

    def across(value, distance):
        return lax.ppermute(value, "dp", [(i, i ^ distance) for i in range(chips)])

    def gathered(value):
        return [value] + [across(value, distance) for distance in range(1, group)]

    block = features // (2 * chips)
    gain = gain.reshape(1, half)
    weight = load(weight)
    keep, send, columns = forward(stash, weight, injection, order, chips, group)
    moved = [across(columns[distance], distance) for distance in range(group - 1, 0, -1)]
    columns = columns[:1] + moved[::-1]
    got = swap(send, "section")
    sums = row_sums(order, cotangent, gain, keep, got)
    others = opposite(sums)
    db1, delta1, gain1, away = lower_iteration1(
        order, exits, cotangent, gain, keep, got, sums, others, weight
    )
    blocks1, *moved = lax.optimization_barrier((db1, *columns[:0:-1]))
    columns = columns[:1] + moved[::-1]
    sent = opposite(away)
    grads1 = gathered(blocks1)
    kept = kept_half(db1, weight)
    kept, sent = lax.optimization_barrier((kept, sent))

    carried, inner, gains = carry(
        order, exits, cotangent, gain, keep, got, sums, others, kept, sent, gain1, features
    )
    inner_other, gains_other = opposite(inner), swap(gains, "section")
    columns = stacked(columns)
    gains = gains + gains_other
    total, db0 = iteration0(
        gain, keep, got, sums, others, carried, inner, inner_other, delta1, features
    )
    db0, gains, columns, *grads1[1:] = lax.optimization_barrier(
        (db0, gains, columns, *grads1[1:])
    )
    grads0 = gathered(db0)
    columns, total = lax.optimization_barrier((columns, total))
    left = left_side(columns, opposite(columns))

    far_gains = across(gains, 2)
    left, grads0, far_gains = lax.optimization_barrier((left, grads0, far_gains))
    gains = gains + far_gains

    cut = (half // 2 + 127) // 128 * 128
    terms = [
        weight_terms(left, grads0 + grads1, lanes) for lanes in [(0, cut), (cut, half - cut)]
    ]
    arrived = [swap(send, "section") for _, send in terms]
    own, others = [], []
    for part, (keep, _) in enumerate(terms):
        if part:
            keep, *_ = lax.optimization_barrier((keep, *aways))
            total, *_ = lax.optimization_barrier((total, *aways))
        mine, *aways = chip_sum(keep, arrived[part], block)
        own.append(mine)
        others.append([across(away, group * (i + 1)) for i, away in enumerate(aways)])
    gains, *_ = lax.optimization_barrier((gains, *aways))
    gains = gains + across(gains, 1)
    gains = [gains] + [across(gains, group * other) for other in range(1, groups)]
    d_injection = place(order, total, swap(total, "section"))
    others[1], d_injection = lax.optimization_barrier((others[1], d_injection))
    d_weight, d_gain = final_sum(own, others, gains, half)
    return (d_injection, d_weight, d_gain)


def solution(mesh):
    return jax.shard_map(
        shards,
        mesh=mesh,
        in_specs=(
            P("section", "dp", None, None),
            P("dp", None, "mp"),
            P("dp", None, "mp"),
            P("mp"),
            P(None, "mp"),
            P("dp"),
            P("dp", None),
        ),
        out_specs=(P("dp", None, "mp"), P(("section", "dp"), "mp"), P("mp")),
        check_vma=False,
    )
```

```python
import jax
import jax.numpy as jnp
from jax import lax
from jax.experimental import pallas as pl
from jax.experimental.pallas import tpu as pltpu
from jax.sharding import PartitionSpec as P

epsilon = 1e-06
f32, bf16 = jnp.float32, jnp.bfloat16
VMEM = pl.BlockSpec(memory_space=pltpu.VMEM)
SMEM = pl.BlockSpec(memory_space=pltpu.SMEM)
HBM = pl.BlockSpec(memory_space=pltpu.HBM)


def call(kernel, outs, ins, scratch=(), limit=24):
    shapes = [jax.ShapeDtypeStruct(shape, kind) for shape, kind in outs]
    specs, values = zip(*ins)
    return pl.pallas_call(
        kernel,
        out_shape=shapes,
        in_specs=list(specs),
        out_specs=[VMEM] * len(shapes),
        scratch_shapes=list(scratch),
        compiler_params=pltpu.CompilerParams(vmem_limit_bytes=limit * 2**20),
        cost_estimate=pl.CostEstimate(flops=1000, bytes_accessed=1000, transcendentals=0),
    )(*values)


def swap(value, axis):
    return lax.ppermute(value, axis, [(0, 1), (1, 0)])


def opposite(value):
    return lax.ppermute(value, ("section", "mp"), [(i, 3 - i) for i in range(4)])


def own_slot():
    return lax.axis_index("section") ^ lax.axis_index("mp")


def chunks_of(total, size):
    return [(start, min(size, total - start)) for start in range(0, total, size)]


def to_rows(columns):
    rows = columns[0].shape[0]
    lane = lax.broadcasted_iota(jnp.int32, (rows, 128), 1)
    wide = jnp.zeros((rows, 128), f32)
    for index, column in enumerate(columns):
        wide = jnp.where(lane == index, column, wide)
    return wide.T[:8]


def to_columns(packed):
    return jnp.concatenate([packed] * 16, axis=0).T


def load(weight):
    parts = chunks_of(weight.shape[0], 512)

    def kernel(weight_hbm, w, sems):
        copies = []
        for index, (start, size) in enumerate(parts):
            part = pl.ds(start, size)
            copies.append(pltpu.make_async_copy(weight_hbm.at[part], w.at[part], sems.at[index]))
            copies[-1].start()
        for copy in copies:
            copy.wait()

    return call(
        kernel,
        [(weight.shape, bf16)],
        [(HBM, weight)],
        [pltpu.SemaphoreType.DMA((len(parts),))],
        limit=42,
    )[0]


def forward(stash, weight, injection, order, chips, group):
    slots, rows, features = stash.shape
    half = weight.shape[1]
    block = features // (2 * chips)
    groups = chips // group
    height = 2 * groups * block

    def kernel(order_ref, stash_ref, weight_ref, inj_ref, keep_ref, send_ref, *refs):
        *out_refs, turned, acc = refs
        slot = own_slot()
        left = stash_ref[...].reshape(slots * rows, features)
        for start, size in chunks_of(half, 256):
            part = slice(start, start + size)
            term = jnp.dot(left, weight_ref[:, part], preferred_element_type=f32)
            acc[:, :, part] = term.reshape(slots, rows, size)
        keep_ref[...] = acc[slot] + inj_ref[order_ref[0, slot]].astype(f32)
        send_ref[...] = acc[1 - slot] + inj_ref[order_ref[0, 1 - slot]].astype(f32)
        if out_refs:
            turned[...] = stash_ref[slot].T
        dp = lax.axis_index("dp")
        for distance, out_ref in enumerate(out_refs):
            for half_index in range(2):
                for other in range(groups):
                    chip = dp ^ (distance + group * other)
                    source = pl.multiple_of((half_index * chips + chip) * block, 16)
                    base = (half_index * groups + other) * block
                    out_ref[base : base + block] = turned[pl.ds(source, block)]

    pieces = group if block % 16 == 0 else 0
    keep, send, *columns = call(
        kernel,
        [((rows, half), f32)] * 2 + [((height, rows), bf16)] * pieces,
        [(SMEM, order), (VMEM, stash), (VMEM, weight), (VMEM, injection)],
        [pltpu.VMEM((features, rows), bf16), pltpu.VMEM((slots, rows, half), f32)],
    )
    if not columns:
        turned = lax.dynamic_index_in_dim(stash, own_slot(), 0, keepdims=False).T
        turned = turned.reshape(2, chips, block, rows)
        for distance in range(group):
            picked = [
                lax.dynamic_index_in_dim(
                    turned, lax.axis_index("dp") ^ (distance + group * other), 1, keepdims=False
                )
                for other in range(groups)
            ]
            columns.append(jnp.stack(picked, axis=1).reshape(height, rows))
    return keep, send, columns


def row_sums(order, cotangent, gain, keep, got):
    rows = keep.shape[0]

    def kernel(order_ref, cot_ref, gain_ref, keep_ref, got_ref, out_ref):
        sec = lax.axis_index("section")
        first = sec == 0
        keep, got = keep_ref[...], got_ref[...]
        pre1, pre0 = jnp.where(first, got, keep), jnp.where(first, keep, got)
        u = cot_ref[order_ref[0, own_slot()]].astype(f32) * gain_ref[...]
        sums = [pre1 * pre1, u * pre1, pre0 * pre0]
        out_ref[...] = to_rows([jnp.sum(each, axis=1, keepdims=True) for each in sums])

    ins = [(SMEM, order), (VMEM, cotangent), (VMEM, gain), (VMEM, keep), (VMEM, got)]
    return call(kernel, [((8, rows), f32)], ins)[0]


def delta_of(pre, u, squares, inner, features):
    radius = jnp.sqrt(squares / features + epsilon)
    inverse = 1.0 / radius
    normed = pre * inverse
    return normed, (u - normed * (inner * inverse / features)) * inverse


def lower_iteration1(order, exits, cotangent, gain, keep, got, sums, others, weight):
    rows, half = keep.shape
    features = weight.shape[0]

    def kernel(order_ref, exits_ref, cot_ref, gain_ref, keep_ref, got_ref, sums_ref, others_ref,
               weight_ref, db_ref, delta_ref, gain_out, away_ref):
        sec, mp = lax.axis_index("section"), lax.axis_index("mp")
        micro = order_ref[0, own_slot()]
        live = jnp.where(exits_ref[micro] > 1, 1.0, 0.0)
        stats = to_columns(sums_ref[...] + others_ref[...])
        pre = jnp.where(sec == 0, got_ref[...], keep_ref[...])
        cot = cot_ref[micro].astype(f32)
        normed, delta = delta_of(pre, cot * gain_ref[...], stats[:, 0:1], stats[:, 1:2], features)
        delta = delta * live
        delta_ref[...] = delta
        db = delta.astype(bf16)
        db_ref[...] = db
        gain_out[...] = jnp.sum(cot * normed, axis=0, keepdims=True) * live
        part = weight_ref[pl.ds(pl.multiple_of((1 - mp) * half, 128), half)]
        away_ref[...] = lax.dot_general(
            part, db, (((1,), (1,)), ((), ())), preferred_element_type=f32
        ).astype(bf16)

    return call(
        kernel,
        [((rows, half), bf16), ((rows, half), f32), ((1, half), f32), ((half, rows), bf16)],
        [(SMEM, order), (SMEM, exits), (VMEM, cotangent), (VMEM, gain), (VMEM, keep), (VMEM, got),
         (VMEM, sums), (VMEM, others), (VMEM, weight)],
    )


def kept_half(db, weight):
    rows, half = db.shape

    def kernel(db_ref, weight_ref, out_ref):
        part = weight_ref[pl.ds(pl.multiple_of(lax.axis_index("mp") * half, 128), half)]
        out_ref[...] = lax.dot_general(
            part, db_ref[...], (((1,), (1,)), ((), ())), preferred_element_type=f32
        )

    return call(kernel, [((half, rows), f32)], [(VMEM, db), (VMEM, weight)])[0]


def carry(order, exits, cotangent, gain, keep, got, sums, others, kept, sent, gain1, features):
    rows, half = keep.shape

    def kernel(order_ref, exits_ref, cot_ref, gain_ref, keep_ref, got_ref, sums_ref, others_ref,
               kept_ref, sent_ref, gain1_ref, carried_ref, inner_ref, gain_out):
        sec = lax.axis_index("section")
        micro = order_ref[0, own_slot()]
        passed = (kept_ref[...] + sent_ref[...].astype(f32)).astype(bf16).astype(f32).T
        cot = cot_ref[micro].astype(f32)
        carried = jnp.where(exits_ref[micro] > 1, passed, cot)
        carried_ref[...] = carried
        pre = jnp.where(sec == 0, keep_ref[...], got_ref[...])
        inner = jnp.sum(carried * gain_ref[...] * pre, axis=1, keepdims=True)
        inner_ref[...] = to_rows([inner])
        squares = to_columns(sums_ref[...] + others_ref[...])[:, 2:3]
        inverse = 1.0 / jnp.sqrt(squares / features + epsilon)
        gains = jnp.sum(carried * (pre * inverse), axis=0, keepdims=True) + gain1_ref[...]
        gain_out[...] = jnp.broadcast_to(gains, (8, half))

    return call(
        kernel,
        [((rows, half), f32), ((8, rows), f32), ((8, half), f32)],
        [(SMEM, order), (SMEM, exits)]
        + [
            (VMEM, value)
            for value in (cotangent, gain, keep, got, sums, others, kept, sent, gain1)
        ],
    )


def iteration0(gain, keep, got, sums, others, carried, inner, inner_other, delta1, features):
    rows, half = keep.shape

    def kernel(gain_ref, keep_ref, got_ref, sums_ref, others_ref, carried_ref, inner_ref, other_ref,
               delta1_ref, total_ref, db_ref):
        sec = lax.axis_index("section")
        squares = to_columns(sums_ref[...] + others_ref[...])[:, 2:3]
        inner = to_columns(inner_ref[...] + other_ref[...])[:, 0:1]
        pre = jnp.where(sec == 0, keep_ref[...], got_ref[...])
        _, delta = delta_of(pre, carried_ref[...] * gain_ref[...], squares, inner, features)
        total_ref[...] = delta + delta1_ref[...]
        db_ref[...] = delta.astype(bf16)

    values = [gain, keep, got, sums, others, carried, inner, inner_other, delta1]
    return call(
        kernel,
        [((rows, half), f32), ((rows, half), bf16)],
        [(VMEM, value) for value in values],
    )


def stacked(columns):
    def kernel(*refs):
        for chip, ref in enumerate(refs[:-1]):
            refs[-1][chip] = ref[...]

    outs = [((len(columns), *columns[0].shape), bf16)]
    return call(kernel, outs, [(VMEM, value) for value in columns])[0]


def left_side(columns, others):
    group, height, rows = columns.shape

    def kernel(own_ref, other_ref, out_ref):
        for index, pair in enumerate([(own_ref, other_ref), (other_ref, own_ref)]):

            @pl.when(lax.axis_index("section") == index)
            def _():
                for k, ref in enumerate(pair):
                    for chip in range(group):
                        base = (k * group + chip) * rows
                        out_ref[:, base : base + rows] = ref[chip]

    return call(
        kernel,
        [((height, 2 * group * rows), bf16)],
        [(VMEM, value) for value in (columns, others)],
    )[0]


def weight_terms(left, grads, k, lanes, base=()):
    rows = grads[0].shape[0]
    depth = len(grads) * rows
    height = left.shape[0]
    start, width = lanes

    def kernel(left_ref, *refs):
        grads_refs, base_refs = refs[: len(grads)], refs[len(grads) : -3]
        keep_ref, send_ref, right = refs[-3:]
        part = slice(start, start + width)
        for index, grads_ref in enumerate(grads_refs):
            right[index * rows : (index + 1) * rows] = grads_ref[:, part]
        for core, (first, second) in enumerate([(0, 1), (1, 0)]):

            @pl.when(lax.axis_index("section") == core)
            def _():
                terms = jnp.dot(
                    left_ref[:, k * depth : (k + 1) * depth],
                    right[...],
                    preferred_element_type=f32,
                )
                halves = [terms[: height // 2], terms[height // 2 :]]
                for out_ref, index in [(keep_ref, first), (send_ref, second)]:
                    total = halves[index]
                    if base_refs:
                        total = total + base_refs[0 if out_ref is keep_ref else 1][:, part]
                    out_ref[...] = total

    return call(
        kernel,
        [((height // 2, width), f32)] * 2,
        [(VMEM, value) for value in [left, *grads, *base]],
        [pltpu.VMEM((depth, width), bf16)],
    )


def chip_sum(keep, other, block):
    height, width = keep.shape

    def kernel(keep_ref, other_ref, own_ref, *away_refs):
        total = keep_ref[...] + other_ref[...]
        own_ref[...] = total[:block]
        for index, away_ref in enumerate(away_refs):
            away_ref[...] = total[(index + 1) * block : (index + 2) * block].astype(bf16)

    outs = [((block, width), f32)] + [((block, width), bf16)] * (height // block - 1)
    return call(kernel, outs, [(VMEM, keep), (VMEM, other)])


def final_sum(own, others, gains, half):
    block = own[0].shape[0]
    count = len(others[0])

    def kernel(*refs):
        gain_refs, refs = refs[: len(gains)], refs[len(gains) :]
        weight_out, gain_out = refs[-2:]
        start = 0
        for part in range(len(own)):
            own_ref, *other_refs = refs[part * (count + 1) : (part + 1) * (count + 1)]
            total = own_ref[...]
            for other_ref in other_refs:
                total = total + other_ref[...].astype(f32)
            width = own_ref.shape[1]
            weight_out[:, start : start + width] = total
            start += width
        sums = [ref[:1] for ref in gain_refs]
        while len(sums) > 1:
            sums = [a + b for a, b in zip(sums[::2], sums[1::2])]
        gain_out[...] = sums[0].reshape(half)

    values = [value for mine, theirs in zip(own, others) for value in (mine, *theirs)]
    ins = [(VMEM, value) for value in (*gains, *values)]
    return call(kernel, [((block, half), f32), ((half,), f32)], ins)


def place(order, total, other):
    rows, half = total.shape

    def kernel(order_ref, total_ref, other_ref, out_ref):
        micro = order_ref[0, own_slot()]
        out_ref[micro] = total_ref[...]
        out_ref[1 - micro] = other_ref[...]

    ins = [(SMEM, order), (VMEM, total), (VMEM, other)]
    return call(kernel, [((2, rows, half), f32)], ins)[0]


def shards(states, injection, cotangent, gain, weight, exits, order):
    stash = states[0]
    slots, rows, features = stash.shape
    half = weight.shape[1]
    dp = lax.axis_index("dp")
    chips = lax.axis_size("dp")
    group = 4
    groups = chips // group
    assert slots == 2 and lax.axis_size("section") == 2 and lax.axis_size("mp") == 2
    assert chips % group == 0 and groups & (groups - 1) == 0

    def across(value, distance):
        return lax.ppermute(value, "dp", [(i, i ^ distance) for i in range(chips)])

    def gathered(value):
        return [value] + [across(value, distance) for distance in range(1, group)]

    block = features // (2 * chips)
    gain = gain.reshape(1, half)
    weight = load(weight)
    keep, send, columns = forward(stash, weight, injection, order, chips, group)
    moved = [across(columns[distance], distance) for distance in range(group - 1, 0, -1)]
    columns = columns[:1] + moved[::-1]
    got = swap(send, "section")
    sums = row_sums(order, cotangent, gain, keep, got)
    others = opposite(sums)
    db1, delta1, gain1, away = lower_iteration1(
        order, exits, cotangent, gain, keep, got, sums, others, weight
    )
    blocks1, *moved = lax.optimization_barrier((db1, *columns[:0:-1]))
    columns = columns[:1] + moved[::-1]
    sent = opposite(away)
    grads1 = gathered(blocks1)
    kept = kept_half(db1, weight)
    kept, sent = lax.optimization_barrier((kept, sent))

    carried, inner, gains = carry(
        order, exits, cotangent, gain, keep, got, sums, others, kept, sent, gain1, features
    )
    inner_other, gains_other = opposite(inner), swap(gains, "section")
    columns = stacked(columns)
    gains = gains + gains_other
    total, db0 = iteration0(
        gain, keep, got, sums, others, carried, inner, inner_other, delta1, features
    )
    db0, gains, columns, *grads1[1:] = lax.optimization_barrier(
        (db0, gains, columns, *grads1[1:])
    )
    grads0 = gathered(db0)
    columns, total = lax.optimization_barrier((columns, total))
    left = left_side(columns, opposite(columns))

    far_gains = across(gains, 2)
    base = weight_terms(left, grads1, 1, (0, half))
    left, base, grads0, far_gains = lax.optimization_barrier((left, base, grads0, far_gains))
    gains = gains + far_gains

    cut = (half // 2 + 127) // 128 * 128
    terms = [
        weight_terms(left, grads0, 0, lanes, base) for lanes in [(0, cut), (cut, half - cut)]
    ]
    arrived = [swap(send, "section") for _, send in terms]
    own, others = [], []
    for part, (keep, _) in enumerate(terms):
        if part:
            keep, *_ = lax.optimization_barrier((keep, *aways))
            total, *_ = lax.optimization_barrier((total, *aways))
        mine, *aways = chip_sum(keep, arrived[part], block)
        own.append(mine)
        others.append([across(away, group * (i + 1)) for i, away in enumerate(aways)])
    gains, *_ = lax.optimization_barrier((gains, *aways))
    gains = gains + across(gains, 1)
    gains = [gains] + [across(gains, group * other) for other in range(1, groups)]
    d_injection = place(order, total, swap(total, "section"))
    others[1], d_injection = lax.optimization_barrier((others[1], d_injection))
    d_weight, d_gain = final_sum(own, others, gains, half)
    return (d_injection, d_weight, d_gain)


def solution(mesh):
    return jax.shard_map(
        shards,
        mesh=mesh,
        in_specs=(
            P("section", "dp", None, None),
            P("dp", None, "mp"),
            P("dp", None, "mp"),
            P("mp"),
            P(None, "mp"),
            P("dp"),
            P("dp", None),
        ),
        out_specs=(P("dp", None, "mp"), P(("section", "dp"), "mp"), P("mp")),
        check_vma=False,
    )
```

```python
import jax
import jax.numpy as jnp
from jax import lax
from jax.experimental import pallas as pl
from jax.experimental.pallas import tpu as pltpu
from jax.sharding import PartitionSpec as P

epsilon = 1e-06
f32, bf16 = jnp.float32, jnp.bfloat16
VMEM = pl.BlockSpec(memory_space=pltpu.VMEM)
SMEM = pl.BlockSpec(memory_space=pltpu.SMEM)
HBM = pl.BlockSpec(memory_space=pltpu.HBM)


def call(kernel, outs, ins, scratch=(), limit=24):
    shapes = [jax.ShapeDtypeStruct(shape, kind) for shape, kind in outs]
    specs, values = zip(*ins)
    return pl.pallas_call(
        kernel,
        out_shape=shapes,
        in_specs=list(specs),
        out_specs=[VMEM] * len(shapes),
        scratch_shapes=list(scratch),
        compiler_params=pltpu.CompilerParams(vmem_limit_bytes=limit * 2**20),
        cost_estimate=pl.CostEstimate(flops=1000, bytes_accessed=1000, transcendentals=0),
    )(*values)


def swap(value, axis):
    return lax.ppermute(value, axis, [(0, 1), (1, 0)])


def opposite(value):
    return lax.ppermute(value, ("section", "mp"), [(i, 3 - i) for i in range(4)])


def own_slot():
    return lax.axis_index("section") ^ lax.axis_index("mp")


def chunks_of(total, size):
    return [(start, min(size, total - start)) for start in range(0, total, size)]


def to_rows(columns):
    rows = columns[0].shape[0]
    lane = lax.broadcasted_iota(jnp.int32, (rows, 128), 1)
    wide = jnp.zeros((rows, 128), f32)
    for index, column in enumerate(columns):
        wide = jnp.where(lane == index, column, wide)
    return wide.T[:8]


def to_columns(packed):
    return jnp.concatenate([packed] * 16, axis=0).T


def load(weight):
    parts = chunks_of(weight.shape[0], 176)

    def kernel(weight_hbm, w, sems):
        copies = []
        for index, (start, size) in enumerate(parts):
            part = pl.ds(start, size)
            copies.append(pltpu.make_async_copy(weight_hbm.at[part], w.at[part], sems.at[index]))
            copies[-1].start()
        for copy in copies:
            copy.wait()

    return call(
        kernel,
        [(weight.shape, bf16)],
        [(HBM, weight)],
        [pltpu.SemaphoreType.DMA((len(parts),))],
        limit=42,
    )[0]


def forward(stash, weight, injection, order, chips, group):
    slots, rows, features = stash.shape
    half = weight.shape[1]
    block = features // (2 * chips)
    groups = chips // group
    height = 2 * groups * block

    def kernel(order_ref, stash_ref, weight_ref, inj_ref, keep_ref, send_ref, *refs):
        *out_refs, turned = refs
        slot = own_slot()
        left = stash_ref[...].reshape(slots * rows, features)
        for start, size in chunks_of(half, 256):
            part = slice(start, start + size)
            term = jnp.dot(left, weight_ref[:, part], preferred_element_type=f32)
            first, second = term[:rows], term[rows:]
            keep, send = jnp.where(slot == 0, first, second), jnp.where(slot == 0, second, first)
            keep_ref[:, part] = keep + inj_ref[order_ref[0, slot], :, part].astype(f32)
            send_ref[:, part] = send + inj_ref[order_ref[0, 1 - slot], :, part].astype(f32)
        if out_refs:
            turned[...] = stash_ref[slot].T
        dp = lax.axis_index("dp")
        for distance, out_ref in enumerate(out_refs):
            for half_index in range(2):
                for other in range(groups):
                    chip = dp ^ (distance + group * other)
                    source = pl.multiple_of((half_index * chips + chip) * block, 16)
                    base = (half_index * groups + other) * block
                    out_ref[base : base + block] = turned[pl.ds(source, block)]

    pieces = group if block % 16 == 0 else 0
    keep, send, *columns = call(
        kernel,
        [((rows, half), f32)] * 2 + [((height, rows), bf16)] * pieces,
        [(SMEM, order), (VMEM, stash), (VMEM, weight), (VMEM, injection)],
        [pltpu.VMEM((features, rows), bf16)],
    )
    if not columns:
        turned = lax.dynamic_index_in_dim(stash, own_slot(), 0, keepdims=False).T
        turned = turned.reshape(2, chips, block, rows)
        for distance in range(group):
            picked = [
                lax.dynamic_index_in_dim(
                    turned, lax.axis_index("dp") ^ (distance + group * other), 1, keepdims=False
                )
                for other in range(groups)
            ]
            columns.append(jnp.stack(picked, axis=1).reshape(height, rows))
    return keep, send, columns


def row_sums(order, cotangent, gain, keep, got):
    rows = keep.shape[0]

    def kernel(order_ref, cot_ref, gain_ref, keep_ref, got_ref, out_ref):
        sec = lax.axis_index("section")
        first = sec == 0
        keep, got = keep_ref[...], got_ref[...]
        pre1, pre0 = jnp.where(first, got, keep), jnp.where(first, keep, got)
        u = cot_ref[order_ref[0, own_slot()]].astype(f32) * gain_ref[...]
        sums = [pre1 * pre1, u * pre1, pre0 * pre0]
        out_ref[...] = to_rows([jnp.sum(each, axis=1, keepdims=True) for each in sums])

    ins = [(SMEM, order), (VMEM, cotangent), (VMEM, gain), (VMEM, keep), (VMEM, got)]
    return call(kernel, [((8, rows), f32)], ins)[0]


def delta_of(pre, u, squares, inner, features):
    radius = jnp.sqrt(squares / features + epsilon)
    inverse = 1.0 / radius
    normed = pre * inverse
    return normed, (u - normed * (inner * inverse / features)) * inverse


def lower_iteration1(order, exits, cotangent, gain, keep, got, sums, others, weight):
    rows, half = keep.shape
    features = weight.shape[0]

    def kernel(order_ref, exits_ref, cot_ref, gain_ref, keep_ref, got_ref, sums_ref, others_ref,
               weight_ref, db_ref, delta_ref, gain_out, away_ref):
        sec, mp = lax.axis_index("section"), lax.axis_index("mp")
        micro = order_ref[0, own_slot()]
        live = jnp.where(exits_ref[micro] > 1, 1.0, 0.0)
        stats = to_columns(sums_ref[...] + others_ref[...])
        pre = jnp.where(sec == 0, got_ref[...], keep_ref[...])
        cot = cot_ref[micro].astype(f32)
        normed, delta = delta_of(pre, cot * gain_ref[...], stats[:, 0:1], stats[:, 1:2], features)
        delta = delta * live
        delta_ref[...] = delta
        db = delta.astype(bf16)
        db_ref[...] = db
        gain_out[...] = jnp.sum(cot * normed, axis=0, keepdims=True) * live
        part = weight_ref[pl.ds(pl.multiple_of((1 - mp) * half, 128), half)]
        away_ref[...] = lax.dot_general(
            part, db, (((1,), (1,)), ((), ())), preferred_element_type=f32
        ).astype(bf16)

    return call(
        kernel,
        [((rows, half), bf16), ((rows, half), f32), ((1, half), f32), ((half, rows), bf16)],
        [(SMEM, order), (SMEM, exits), (VMEM, cotangent), (VMEM, gain), (VMEM, keep), (VMEM, got),
         (VMEM, sums), (VMEM, others), (VMEM, weight)],
    )


def kept_half(db, weight):
    rows, half = db.shape

    def kernel(db_ref, weight_ref, out_ref):
        part = weight_ref[pl.ds(pl.multiple_of(lax.axis_index("mp") * half, 128), half)]
        out_ref[...] = lax.dot_general(
            part, db_ref[...], (((1,), (1,)), ((), ())), preferred_element_type=f32
        )

    return call(kernel, [((half, rows), f32)], [(VMEM, db), (VMEM, weight)])[0]


def carry(order, exits, cotangent, gain, keep, got, sums, others, kept, sent, gain1, features):
    rows, half = keep.shape

    def kernel(order_ref, exits_ref, cot_ref, gain_ref, keep_ref, got_ref, sums_ref, others_ref,
               kept_ref, sent_ref, gain1_ref, carried_ref, inner_ref, gain_out):
        sec = lax.axis_index("section")
        micro = order_ref[0, own_slot()]
        passed = (kept_ref[...] + sent_ref[...].astype(f32)).astype(bf16).astype(f32).T
        cot = cot_ref[micro].astype(f32)
        carried = jnp.where(exits_ref[micro] > 1, passed, cot)
        carried_ref[...] = carried
        pre = jnp.where(sec == 0, keep_ref[...], got_ref[...])
        inner = jnp.sum(carried * gain_ref[...] * pre, axis=1, keepdims=True)
        inner_ref[...] = to_rows([inner])
        squares = to_columns(sums_ref[...] + others_ref[...])[:, 2:3]
        inverse = 1.0 / jnp.sqrt(squares / features + epsilon)
        gains = jnp.sum(carried * (pre * inverse), axis=0, keepdims=True) + gain1_ref[...]
        gain_out[...] = jnp.broadcast_to(gains, (8, half))

    return call(
        kernel,
        [((rows, half), f32), ((8, rows), f32), ((8, half), f32)],
        [(SMEM, order), (SMEM, exits)]
        + [
            (VMEM, value)
            for value in (cotangent, gain, keep, got, sums, others, kept, sent, gain1)
        ],
    )


def iteration0(gain, keep, got, sums, others, carried, inner, inner_other, delta1, features):
    rows, half = keep.shape

    def kernel(gain_ref, keep_ref, got_ref, sums_ref, others_ref, carried_ref, inner_ref, other_ref,
               delta1_ref, total_ref, db_ref):
        sec = lax.axis_index("section")
        squares = to_columns(sums_ref[...] + others_ref[...])[:, 2:3]
        inner = to_columns(inner_ref[...] + other_ref[...])[:, 0:1]
        pre = jnp.where(sec == 0, keep_ref[...], got_ref[...])
        _, delta = delta_of(pre, carried_ref[...] * gain_ref[...], squares, inner, features)
        total_ref[...] = delta + delta1_ref[...]
        db_ref[...] = delta.astype(bf16)

    values = [gain, keep, got, sums, others, carried, inner, inner_other, delta1]
    return call(
        kernel,
        [((rows, half), f32), ((rows, half), bf16)],
        [(VMEM, value) for value in values],
    )


def stacked(columns):
    def kernel(*refs):
        for chip, ref in enumerate(refs[:-1]):
            refs[-1][chip] = ref[...]

    outs = [((len(columns), *columns[0].shape), bf16)]
    return call(kernel, outs, [(VMEM, value) for value in columns])[0]


def left_side(columns, others):
    group, height, rows = columns.shape

    def kernel(own_ref, other_ref, out_ref):
        for index, pair in enumerate([(own_ref, other_ref), (other_ref, own_ref)]):

            @pl.when(lax.axis_index("section") == index)
            def _():
                for k, ref in enumerate(pair):
                    for chip in range(group):
                        base = (k * group + chip) * rows
                        out_ref[:, base : base + rows] = ref[chip]

    return call(
        kernel,
        [((height, 2 * group * rows), bf16)],
        [(VMEM, value) for value in (columns, others)],
    )[0]


def weight_terms(left, grads, k, lanes, base=()):
    rows = grads[0].shape[0]
    depth = len(grads) * rows
    height = left.shape[0]
    start, width = lanes

    def kernel(left_ref, *refs):
        grads_refs, base_refs = refs[: len(grads)], refs[len(grads) : -3]
        keep_ref, send_ref, right = refs[-3:]
        part = slice(start, start + width)
        for index, grads_ref in enumerate(grads_refs):
            right[index * rows : (index + 1) * rows] = grads_ref[:, part]
        for core, (first, second) in enumerate([(0, 1), (1, 0)]):

            @pl.when(lax.axis_index("section") == core)
            def _():
                terms = jnp.dot(
                    left_ref[:, k * depth : (k + 1) * depth],
                    right[...],
                    preferred_element_type=f32,
                )
                halves = [terms[: height // 2], terms[height // 2 :]]
                for out_ref, index in [(keep_ref, first), (send_ref, second)]:
                    total = halves[index]
                    if base_refs:
                        total = total + base_refs[0 if out_ref is keep_ref else 1][:, part]
                    out_ref[...] = total

    return call(
        kernel,
        [((height // 2, width), f32)] * 2,
        [(VMEM, value) for value in [left, *grads, *base]],
        [pltpu.VMEM((depth, width), bf16)],
    )


def chip_sum(keep, other, block):
    height, width = keep.shape

    def kernel(keep_ref, other_ref, own_ref, *away_refs):
        total = keep_ref[...] + other_ref[...]
        own_ref[...] = total[:block]
        for index, away_ref in enumerate(away_refs):
            away_ref[...] = total[(index + 1) * block : (index + 2) * block].astype(bf16)

    outs = [((block, width), f32)] + [((block, width), bf16)] * (height // block - 1)
    return call(kernel, outs, [(VMEM, keep), (VMEM, other)])


def final_sum(own, others, gains, half):
    block = own[0].shape[0]
    count = len(others[0])

    def kernel(*refs):
        gain_refs, refs = refs[: len(gains)], refs[len(gains) :]
        weight_out, gain_out = refs[-2:]
        start = 0
        for part in range(len(own)):
            own_ref, *other_refs = refs[part * (count + 1) : (part + 1) * (count + 1)]
            total = own_ref[...]
            for other_ref in other_refs:
                total = total + other_ref[...].astype(f32)
            width = own_ref.shape[1]
            weight_out[:, start : start + width] = total
            start += width
        sums = [ref[:1] for ref in gain_refs]
        while len(sums) > 1:
            sums = [a + b for a, b in zip(sums[::2], sums[1::2])]
        gain_out[...] = sums[0].reshape(half)

    values = [value for mine, theirs in zip(own, others) for value in (mine, *theirs)]
    ins = [(VMEM, value) for value in (*gains, *values)]
    return call(kernel, [((block, half), f32), ((half,), f32)], ins)


def place(order, total, other):
    rows, half = total.shape

    def kernel(order_ref, total_ref, other_ref, out_ref):
        micro = order_ref[0, own_slot()]
        out_ref[micro] = total_ref[...]
        out_ref[1 - micro] = other_ref[...]

    ins = [(SMEM, order), (VMEM, total), (VMEM, other)]
    return call(kernel, [((2, rows, half), f32)], ins)[0]


def shards(states, injection, cotangent, gain, weight, exits, order):
    stash = states[0]
    slots, rows, features = stash.shape
    half = weight.shape[1]
    dp = lax.axis_index("dp")
    chips = lax.axis_size("dp")
    group = 4
    groups = chips // group
    assert slots == 2 and lax.axis_size("section") == 2 and lax.axis_size("mp") == 2
    assert chips % group == 0 and groups & (groups - 1) == 0

    def across(value, distance):
        return lax.ppermute(value, "dp", [(i, i ^ distance) for i in range(chips)])

    def gathered(value):
        return [value] + [across(value, distance) for distance in range(1, group)]

    block = features // (2 * chips)
    gain = gain.reshape(1, half)
    weight = load(weight)
    keep, send, columns = forward(stash, weight, injection, order, chips, group)
    moved = [across(columns[distance], distance) for distance in range(group - 1, 0, -1)]
    columns = columns[:1] + moved[::-1]
    got = swap(send, "section")
    sums = row_sums(order, cotangent, gain, keep, got)
    others = opposite(sums)
    db1, delta1, gain1, away = lower_iteration1(
        order, exits, cotangent, gain, keep, got, sums, others, weight
    )
    blocks1, *moved = lax.optimization_barrier((db1, *columns[:0:-1]))
    columns = columns[:1] + moved[::-1]
    sent = opposite(away)
    grads1 = gathered(blocks1)
    kept = kept_half(db1, weight)
    kept, sent = lax.optimization_barrier((kept, sent))

    carried, inner, gains = carry(
        order, exits, cotangent, gain, keep, got, sums, others, kept, sent, gain1, features
    )
    inner_other, gains_other = opposite(inner), swap(gains, "section")
    columns = stacked(columns)
    gains = gains + gains_other
    total, db0 = iteration0(
        gain, keep, got, sums, others, carried, inner, inner_other, delta1, features
    )
    db0, gains, columns, *grads1[1:] = lax.optimization_barrier(
        (db0, gains, columns, *grads1[1:])
    )
    grads0 = gathered(db0)
    columns, total = lax.optimization_barrier((columns, total))
    left = left_side(columns, opposite(columns))

    far_gains = across(gains, 2)
    base = weight_terms(left, grads1, 1, (0, half))
    left, base, grads0, far_gains = lax.optimization_barrier((left, base, grads0, far_gains))
    gains = gains + far_gains

    cut = (half // 2 + 127) // 128 * 128
    terms = [
        weight_terms(left, grads0, 0, lanes, base) for lanes in [(0, cut), (cut, half - cut)]
    ]
    arrived = [swap(send, "section") for _, send in terms]
    own, others = [], []
    for part, (keep, _) in enumerate(terms):
        if part:
            keep, *_ = lax.optimization_barrier((keep, *aways))
            total, *_ = lax.optimization_barrier((total, *aways))
        mine, *aways = chip_sum(keep, arrived[part], block)
        own.append(mine)
        others.append([across(away, group * (i + 1)) for i, away in enumerate(aways)])
    gains, *_ = lax.optimization_barrier((gains, *aways))
    gains = gains + across(gains, 1)
    gains = [gains] + [across(gains, group * other) for other in range(1, groups)]
    d_injection = place(order, total, swap(total, "section"))
    others[1], d_injection = lax.optimization_barrier((others[1], d_injection))
    d_weight, d_gain = final_sum(own, others, gains, half)
    return (d_injection, d_weight, d_gain)


def solution(mesh):
    return jax.shard_map(
        shards,
        mesh=mesh,
        in_specs=(
            P("section", "dp", None, None),
            P("dp", None, "mp"),
            P("dp", None, "mp"),
            P("mp"),
            P(None, "mp"),
            P("dp"),
            P("dp", None),
        ),
        out_specs=(P("dp", None, "mp"), P(("section", "dp"), "mp"), P("mp")),
        check_vma=False,
    )
```

```python
import jax
import jax.numpy as jnp
from jax import lax
from jax.experimental import pallas as pl
from jax.experimental.pallas import tpu as pltpu
from jax.sharding import PartitionSpec as P

epsilon = 1e-06
f32, bf16 = jnp.float32, jnp.bfloat16
VMEM = pl.BlockSpec(memory_space=pltpu.VMEM)
SMEM = pl.BlockSpec(memory_space=pltpu.SMEM)
HBM = pl.BlockSpec(memory_space=pltpu.HBM)


def call(kernel, outs, ins, scratch=(), limit=24):
    shapes = [jax.ShapeDtypeStruct(shape, kind) for shape, kind in outs]
    specs, values = zip(*ins)
    return pl.pallas_call(
        kernel,
        out_shape=shapes,
        in_specs=list(specs),
        out_specs=[VMEM] * len(shapes),
        scratch_shapes=list(scratch),
        compiler_params=pltpu.CompilerParams(vmem_limit_bytes=limit * 2**20),
        cost_estimate=pl.CostEstimate(flops=1000, bytes_accessed=1000, transcendentals=0),
    )(*values)


def swap(value, axis):
    return lax.ppermute(value, axis, [(0, 1), (1, 0)])


def opposite(value):
    return lax.ppermute(value, ("section", "mp"), [(i, 3 - i) for i in range(4)])


def own_slot():
    return lax.axis_index("section") ^ lax.axis_index("mp")


def chunks_of(total, size):
    return [(start, min(size, total - start)) for start in range(0, total, size)]


def to_rows(columns):
    rows = columns[0].shape[0]
    lane = lax.broadcasted_iota(jnp.int32, (rows, 128), 1)
    wide = jnp.zeros((rows, 128), f32)
    for index, column in enumerate(columns):
        wide = jnp.where(lane == index, column, wide)
    return wide.T[:8]


def to_columns(packed):
    return jnp.concatenate([packed] * 16, axis=0).T


def load(weight):
    parts = chunks_of(weight.shape[0], 512)

    def kernel(weight_hbm, w, sems):
        copies = []
        for index, (start, size) in enumerate(parts):
            part = pl.ds(start, size)
            copies.append(pltpu.make_async_copy(weight_hbm.at[part], w.at[part], sems.at[index]))
            copies[-1].start()
        for copy in copies:
            copy.wait()

    return call(
        kernel,
        [(weight.shape, bf16)],
        [(HBM, weight)],
        [pltpu.SemaphoreType.DMA((len(parts),))],
        limit=42,
    )[0]


def forward(stash, weight, injection, order, chips, group):
    slots, rows, features = stash.shape
    half = weight.shape[1]
    block = features // (2 * chips)
    groups = chips // group
    height = 2 * groups * block

    def kernel(order_ref, stash_ref, weight_ref, inj_ref, keep_ref, send_ref, *refs):
        *out_refs, turned = refs
        slot = own_slot()
        left = stash_ref[...].reshape(slots * rows, features)
        for start, size in chunks_of(half, 256):
            part = slice(start, start + size)
            term = jnp.dot(left, weight_ref[:, part], preferred_element_type=f32)
            first, second = term[:rows], term[rows:]
            keep, send = jnp.where(slot == 0, first, second), jnp.where(slot == 0, second, first)
            keep_ref[:, part] = keep + inj_ref[order_ref[0, slot], :, part].astype(f32)
            send_ref[:, part] = send + inj_ref[order_ref[0, 1 - slot], :, part].astype(f32)
        if out_refs:
            turned[...] = stash_ref[slot].T
        dp = lax.axis_index("dp")
        for distance, out_ref in enumerate(out_refs):
            for half_index in range(2):
                for other in range(groups):
                    chip = dp ^ (distance + group * other)
                    source = pl.multiple_of((half_index * chips + chip) * block, 16)
                    base = (half_index * groups + other) * block
                    out_ref[base : base + block] = turned[pl.ds(source, block)]

    pieces = group if block % 16 == 0 else 0
    keep, send, *columns = call(
        kernel,
        [((rows, half), f32)] * 2 + [((height, rows), bf16)] * pieces,
        [(SMEM, order), (VMEM, stash), (VMEM, weight), (VMEM, injection)],
        [pltpu.VMEM((features, rows), bf16)],
    )
    if not columns:
        turned = lax.dynamic_index_in_dim(stash, own_slot(), 0, keepdims=False).T
        turned = turned.reshape(2, chips, block, rows)
        for distance in range(group):
            picked = [
                lax.dynamic_index_in_dim(
                    turned, lax.axis_index("dp") ^ (distance + group * other), 1, keepdims=False
                )
                for other in range(groups)
            ]
            columns.append(jnp.stack(picked, axis=1).reshape(height, rows))
    return keep, send, columns


def row_sums(order, cotangent, gain, keep, got):
    rows = keep.shape[0]

    def kernel(order_ref, cot_ref, gain_ref, keep_ref, got_ref, out_ref):
        sec = lax.axis_index("section")
        first = sec == 0
        keep, got = keep_ref[...], got_ref[...]
        pre1, pre0 = jnp.where(first, got, keep), jnp.where(first, keep, got)
        u = cot_ref[order_ref[0, own_slot()]].astype(f32) * gain_ref[...]
        sums = [pre1 * pre1, u * pre1, pre0 * pre0]
        out_ref[...] = to_rows([jnp.sum(each, axis=1, keepdims=True) for each in sums])

    ins = [(SMEM, order), (VMEM, cotangent), (VMEM, gain), (VMEM, keep), (VMEM, got)]
    return call(kernel, [((8, rows), f32)], ins)[0]


def delta_of(pre, u, squares, inner, features):
    radius = jnp.sqrt(squares / features + epsilon)
    inverse = 1.0 / radius
    normed = pre * inverse
    return normed, (u - normed * (inner * inverse / features)) * inverse


def lower_iteration1(order, exits, cotangent, gain, keep, got, sums, others, weight):
    rows, half = keep.shape
    features = weight.shape[0]

    def kernel(order_ref, exits_ref, cot_ref, gain_ref, keep_ref, got_ref, sums_ref, others_ref,
               weight_ref, db_ref, delta_ref, gain_out, away_ref):
        sec, mp = lax.axis_index("section"), lax.axis_index("mp")
        micro = order_ref[0, own_slot()]
        live = jnp.where(exits_ref[micro] > 1, 1.0, 0.0)
        stats = to_columns(sums_ref[...] + others_ref[...])
        pre = jnp.where(sec == 0, got_ref[...], keep_ref[...])
        cot = cot_ref[micro].astype(f32)
        normed, delta = delta_of(pre, cot * gain_ref[...], stats[:, 0:1], stats[:, 1:2], features)
        delta = delta * live
        delta_ref[...] = delta
        db = delta.astype(bf16)
        db_ref[...] = db
        gain_out[...] = jnp.sum(cot * normed, axis=0, keepdims=True) * live
        part = weight_ref[pl.ds(pl.multiple_of((1 - mp) * half, 128), half)]
        away_ref[...] = lax.dot_general(
            part, db, (((1,), (1,)), ((), ())), preferred_element_type=f32
        ).astype(bf16)

    return call(
        kernel,
        [((rows, half), bf16), ((rows, half), f32), ((1, half), f32), ((half, rows), bf16)],
        [(SMEM, order), (SMEM, exits), (VMEM, cotangent), (VMEM, gain), (VMEM, keep), (VMEM, got),
         (VMEM, sums), (VMEM, others), (VMEM, weight)],
    )


def kept_half(db, weight):
    rows, half = db.shape

    def kernel(db_ref, weight_ref, out_ref):
        part = weight_ref[pl.ds(pl.multiple_of(lax.axis_index("mp") * half, 128), half)]
        out_ref[...] = lax.dot_general(
            part, db_ref[...], (((1,), (1,)), ((), ())), preferred_element_type=f32
        )

    return call(kernel, [((half, rows), f32)], [(VMEM, db), (VMEM, weight)])[0]


def carry(order, exits, cotangent, gain, keep, got, sums, others, kept, sent, gain1, features):
    rows, half = keep.shape

    def kernel(order_ref, exits_ref, cot_ref, gain_ref, keep_ref, got_ref, sums_ref, others_ref,
               kept_ref, sent_ref, gain1_ref, carried_ref, inner_ref, gain_out):
        sec = lax.axis_index("section")
        micro = order_ref[0, own_slot()]
        passed = (kept_ref[...] + sent_ref[...].astype(f32)).astype(bf16).astype(f32).T
        cot = cot_ref[micro].astype(f32)
        carried = jnp.where(exits_ref[micro] > 1, passed, cot)
        carried_ref[...] = carried
        pre = jnp.where(sec == 0, keep_ref[...], got_ref[...])
        inner = jnp.sum(carried * gain_ref[...] * pre, axis=1, keepdims=True)
        inner_ref[...] = to_rows([inner])
        squares = to_columns(sums_ref[...] + others_ref[...])[:, 2:3]
        inverse = 1.0 / jnp.sqrt(squares / features + epsilon)
        gains = jnp.sum(carried * (pre * inverse), axis=0, keepdims=True) + gain1_ref[...]
        gain_out[...] = jnp.broadcast_to(gains, (8, half))

    return call(
        kernel,
        [((rows, half), f32), ((8, rows), f32), ((8, half), f32)],
        [(SMEM, order), (SMEM, exits)]
        + [
            (VMEM, value)
            for value in (cotangent, gain, keep, got, sums, others, kept, sent, gain1)
        ],
    )


def iteration0(gain, keep, got, sums, others, carried, inner, inner_other, delta1, features):
    rows, half = keep.shape

    def kernel(gain_ref, keep_ref, got_ref, sums_ref, others_ref, carried_ref, inner_ref, other_ref,
               delta1_ref, total_ref, db_ref):
        sec = lax.axis_index("section")
        squares = to_columns(sums_ref[...] + others_ref[...])[:, 2:3]
        inner = to_columns(inner_ref[...] + other_ref[...])[:, 0:1]
        pre = jnp.where(sec == 0, keep_ref[...], got_ref[...])
        _, delta = delta_of(pre, carried_ref[...] * gain_ref[...], squares, inner, features)
        total_ref[...] = delta + delta1_ref[...]
        db_ref[...] = delta.astype(bf16)

    values = [gain, keep, got, sums, others, carried, inner, inner_other, delta1]
    return call(
        kernel,
        [((rows, half), f32), ((rows, half), bf16)],
        [(VMEM, value) for value in values],
    )


def stacked(columns):
    def kernel(*refs):
        for chip, ref in enumerate(refs[:-1]):
            refs[-1][chip] = ref[...]

    outs = [((len(columns), *columns[0].shape), bf16)]
    return call(kernel, outs, [(VMEM, value) for value in columns])[0]


def left_side(columns, others):
    group, height, rows = columns.shape

    def kernel(own_ref, other_ref, out_ref):
        for index, pair in enumerate([(own_ref, other_ref), (other_ref, own_ref)]):

            @pl.when(lax.axis_index("section") == index)
            def _():
                for k, ref in enumerate(pair):
                    for chip in range(group):
                        base = (k * group + chip) * rows
                        out_ref[:, base : base + rows] = ref[chip]

    return call(
        kernel,
        [((height, 2 * group * rows), bf16)],
        [(VMEM, value) for value in (columns, others)],
    )[0]


def weight_terms(left, grads, k, lanes, base=()):
    rows = grads[0].shape[0]
    depth = len(grads) * rows
    height = left.shape[0]
    start, width = lanes

    def kernel(left_ref, *refs):
        grads_refs, base_refs = refs[: len(grads)], refs[len(grads) : -3]
        keep_ref, send_ref, right = refs[-3:]
        part = slice(start, start + width)
        for index, grads_ref in enumerate(grads_refs):
            right[index * rows : (index + 1) * rows] = grads_ref[:, part]
        for core, (first, second) in enumerate([(0, 1), (1, 0)]):

            @pl.when(lax.axis_index("section") == core)
            def _():
                terms = jnp.dot(
                    left_ref[:, k * depth : (k + 1) * depth],
                    right[...],
                    preferred_element_type=f32,
                )
                halves = [terms[: height // 2], terms[height // 2 :]]
                for out_ref, index in [(keep_ref, first), (send_ref, second)]:
                    total = halves[index]
                    if base_refs:
                        total = total + base_refs[0 if out_ref is keep_ref else 1][:, part]
                    out_ref[...] = total

    return call(
        kernel,
        [((height // 2, width), f32)] * 2,
        [(VMEM, value) for value in [left, *grads, *base]],
        [pltpu.VMEM((depth, width), bf16)],
    )


def chip_sum(keep, other, block):
    height, width = keep.shape

    def kernel(keep_ref, other_ref, own_ref, *away_refs):
        total = keep_ref[...] + other_ref[...]
        own_ref[...] = total[:block]
        for index, away_ref in enumerate(away_refs):
            away_ref[...] = total[(index + 1) * block : (index + 2) * block].astype(bf16)

    outs = [((block, width), f32)] + [((block, width), bf16)] * (height // block - 1)
    return call(kernel, outs, [(VMEM, keep), (VMEM, other)])


def final_sum(own, others, gains, half):
    block = own[0].shape[0]
    count = len(others[0])

    def kernel(*refs):
        gain_refs, refs = refs[: len(gains)], refs[len(gains) :]
        weight_out, gain_out = refs[-2:]
        start = 0
        for part in range(len(own)):
            own_ref, *other_refs = refs[part * (count + 1) : (part + 1) * (count + 1)]
            total = own_ref[...]
            for other_ref in other_refs:
                total = total + other_ref[...].astype(f32)
            width = own_ref.shape[1]
            weight_out[:, start : start + width] = total
            start += width
        sums = [ref[:1] for ref in gain_refs]
        while len(sums) > 1:
            sums = [a + b for a, b in zip(sums[::2], sums[1::2])]
        gain_out[...] = sums[0].reshape(half)

    values = [value for mine, theirs in zip(own, others) for value in (mine, *theirs)]
    ins = [(VMEM, value) for value in (*gains, *values)]
    return call(kernel, [((block, half), f32), ((half,), f32)], ins)


def place(order, total, other):
    rows, half = total.shape

    def kernel(order_ref, total_ref, other_ref, out_ref):
        micro = order_ref[0, own_slot()]
        out_ref[micro] = total_ref[...]
        out_ref[1 - micro] = other_ref[...]

    ins = [(SMEM, order), (VMEM, total), (VMEM, other)]
    return call(kernel, [((2, rows, half), f32)], ins)[0]


def shards(states, injection, cotangent, gain, weight, exits, order):
    stash = states[0]
    slots, rows, features = stash.shape
    half = weight.shape[1]
    dp = lax.axis_index("dp")
    chips = lax.axis_size("dp")
    group = 4
    groups = chips // group
    assert slots == 2 and lax.axis_size("section") == 2 and lax.axis_size("mp") == 2
    assert chips % group == 0 and groups & (groups - 1) == 0

    def across(value, distance):
        return lax.ppermute(value, "dp", [(i, i ^ distance) for i in range(chips)])

    def gathered(value):
        return [value] + [across(value, distance) for distance in range(1, group)]

    block = features // (2 * chips)
    gain = gain.reshape(1, half)
    weight = load(weight)
    keep, send, columns = forward(stash, weight, injection, order, chips, group)
    moved = [across(columns[distance], distance) for distance in range(group - 1, 0, -1)]
    columns = columns[:1] + moved[::-1]
    got = swap(send, "section")
    sums = row_sums(order, cotangent, gain, keep, got)
    others = opposite(sums)
    db1, delta1, gain1, away = lower_iteration1(
        order, exits, cotangent, gain, keep, got, sums, others, weight
    )
    blocks1, *moved = lax.optimization_barrier((db1, *columns[:0:-1]))
    columns = columns[:1] + moved[::-1]
    sent = opposite(away)
    grads1 = gathered(blocks1)
    kept = kept_half(db1, weight)
    kept, sent = lax.optimization_barrier((kept, sent))

    carried, inner, gains = carry(
        order, exits, cotangent, gain, keep, got, sums, others, kept, sent, gain1, features
    )
    inner_other, gains_other = opposite(inner), swap(gains, "section")
    columns = stacked(columns)
    gains = gains + gains_other
    total, db0 = iteration0(
        gain, keep, got, sums, others, carried, inner, inner_other, delta1, features
    )
    db0, gains, columns, *grads1[1:] = lax.optimization_barrier(
        (db0, gains, columns, *grads1[1:])
    )
    grads0 = gathered(db0)
    columns, total = lax.optimization_barrier((columns, total))
    left = left_side(columns, opposite(columns))

    far_gains = across(gains, 2)
    base = weight_terms(left, grads1, 1, (0, half))
    left, base, grads0, far_gains = lax.optimization_barrier((left, base, grads0, far_gains))
    gains = gains + far_gains

    cut = (half // 3 + 127) // 128 * 128
    terms = [weight_terms(left, grads0, 0, lanes, base) for lanes in chunks_of(half, cut)]
    arrived = [swap(send, "section") for _, send in terms]
    own, others = [], []
    for part, (keep, _) in enumerate(terms):
        if not part:
            keep, *_ = lax.optimization_barrier((keep, *terms[-1]))
        else:
            keep, *_ = lax.optimization_barrier((keep, *aways))
            if part == 1:
                total, *_ = lax.optimization_barrier((total, *aways))
        mine, *aways = chip_sum(keep, arrived[part], block)
        own.append(mine)
        others.append([across(away, group * (i + 1)) for i, away in enumerate(aways)])
    gains, *_ = lax.optimization_barrier((gains, *aways))
    gains = gains + across(gains, 1)
    gains = [gains] + [across(gains, group * other) for other in range(1, groups)]
    d_injection = place(order, total, swap(total, "section"))
    others[-1], d_injection = lax.optimization_barrier((others[-1], d_injection))
    d_weight, d_gain = final_sum(own, others, gains, half)
    return (d_injection, d_weight, d_gain)


def solution(mesh):
    return jax.shard_map(
        shards,
        mesh=mesh,
        in_specs=(
            P("section", "dp", None, None),
            P("dp", None, "mp"),
            P("dp", None, "mp"),
            P("mp"),
            P(None, "mp"),
            P("dp"),
            P("dp", None),
        ),
        out_specs=(P("dp", None, "mp"), P(("section", "dp"), "mp"), P("mp")),
        check_vma=False,
    )
```

```python
import jax
import jax.numpy as jnp
from jax import lax
from jax.experimental import pallas as pl
from jax.experimental.pallas import tpu as pltpu
from jax.sharding import PartitionSpec as P

epsilon = 1e-06
f32, bf16 = jnp.float32, jnp.bfloat16
VMEM = pl.BlockSpec(memory_space=pltpu.VMEM)
SMEM = pl.BlockSpec(memory_space=pltpu.SMEM)
HBM = pl.BlockSpec(memory_space=pltpu.HBM)


def call(kernel, outs, ins, scratch=(), limit=24):
    shapes = [jax.ShapeDtypeStruct(shape, kind) for shape, kind in outs]
    specs, values = zip(*ins)
    return pl.pallas_call(
        kernel,
        out_shape=shapes,
        in_specs=list(specs),
        out_specs=[VMEM] * len(shapes),
        scratch_shapes=list(scratch),
        compiler_params=pltpu.CompilerParams(vmem_limit_bytes=limit * 2**20),
        cost_estimate=pl.CostEstimate(flops=1000, bytes_accessed=1000, transcendentals=0),
    )(*values)


def swap(value, axis):
    return lax.ppermute(value, axis, [(0, 1), (1, 0)])


def opposite(value):
    return lax.ppermute(value, ("section", "mp"), [(i, 3 - i) for i in range(4)])


def own_slot():
    return lax.axis_index("section") ^ lax.axis_index("mp")


def chunks_of(total, size):
    return [(start, min(size, total - start)) for start in range(0, total, size)]


def to_rows(columns):
    rows = columns[0].shape[0]
    lane = lax.broadcasted_iota(jnp.int32, (rows, 128), 1)
    wide = jnp.zeros((rows, 128), f32)
    for index, column in enumerate(columns):
        wide = jnp.where(lane == index, column, wide)
    return wide.T[:8]


def to_columns(packed):
    return jnp.concatenate([packed] * 16, axis=0).T


def load(weight):
    parts = chunks_of(weight.shape[0], 512)

    def kernel(weight_hbm, w, sems):
        copies = []
        for index, (start, size) in enumerate(parts):
            part = pl.ds(start, size)
            copies.append(pltpu.make_async_copy(weight_hbm.at[part], w.at[part], sems.at[index]))
            copies[-1].start()
        for copy in copies:
            copy.wait()

    return call(
        kernel,
        [(weight.shape, bf16)],
        [(HBM, weight)],
        [pltpu.SemaphoreType.DMA((len(parts),))],
        limit=42,
    )[0]


def forward(stash, weight, injection, order, chips, group):
    slots, rows, features = stash.shape
    half = weight.shape[1]
    block = features // (2 * chips)
    groups = chips // group
    height = 2 * groups * block

    def kernel(order_ref, stash_ref, weight_ref, inj_ref, keep_ref, send_ref, *refs):
        *out_refs, turned = refs
        slot = own_slot()
        left = stash_ref[...].reshape(slots * rows, features)
        for start, size in chunks_of(half, 256):
            part = slice(start, start + size)
            term = jnp.dot(left, weight_ref[:, part], preferred_element_type=f32)
            first, second = term[:rows], term[rows:]
            keep, send = jnp.where(slot == 0, first, second), jnp.where(slot == 0, second, first)
            keep_ref[:, part] = keep + inj_ref[order_ref[0, slot], :, part].astype(f32)
            send_ref[:, part] = send + inj_ref[order_ref[0, 1 - slot], :, part].astype(f32)
        if out_refs:
            turned[...] = stash_ref[slot].T
        dp = lax.axis_index("dp")
        for distance, out_ref in enumerate(out_refs):
            for half_index in range(2):
                for other in range(groups):
                    chip = dp ^ (distance + group * other)
                    source = pl.multiple_of((half_index * chips + chip) * block, 16)
                    base = (half_index * groups + other) * block
                    out_ref[base : base + block] = turned[pl.ds(source, block)]

    pieces = group if block % 16 == 0 else 0
    keep, send, *columns = call(
        kernel,
        [((rows, half), f32)] * 2 + [((height, rows), bf16)] * pieces,
        [(SMEM, order), (VMEM, stash), (VMEM, weight), (VMEM, injection)],
        [pltpu.VMEM((features, rows), bf16)],
    )
    if not columns:
        turned = lax.dynamic_index_in_dim(stash, own_slot(), 0, keepdims=False).T
        turned = turned.reshape(2, chips, block, rows)
        for distance in range(group):
            picked = [
                lax.dynamic_index_in_dim(
                    turned, lax.axis_index("dp") ^ (distance + group * other), 1, keepdims=False
                )
                for other in range(groups)
            ]
            columns.append(jnp.stack(picked, axis=1).reshape(height, rows))
    return keep, send, columns


def row_sums(order, cotangent, gain, keep, got):
    rows = keep.shape[0]

    def kernel(order_ref, cot_ref, gain_ref, keep_ref, got_ref, out_ref):
        sec = lax.axis_index("section")
        first = sec == 0
        keep, got = keep_ref[...], got_ref[...]
        pre1, pre0 = jnp.where(first, got, keep), jnp.where(first, keep, got)
        u = cot_ref[order_ref[0, own_slot()]].astype(f32) * gain_ref[...]
        sums = [pre1 * pre1, u * pre1, pre0 * pre0]
        out_ref[...] = to_rows([jnp.sum(each, axis=1, keepdims=True) for each in sums])

    ins = [(SMEM, order), (VMEM, cotangent), (VMEM, gain), (VMEM, keep), (VMEM, got)]
    return call(kernel, [((8, rows), f32)], ins)[0]


def delta_of(pre, u, squares, inner, features):
    radius = jnp.sqrt(squares / features + epsilon)
    inverse = 1.0 / radius
    normed = pre * inverse
    return normed, (u - normed * (inner * inverse / features)) * inverse


def lower_iteration1(order, exits, cotangent, gain, keep, got, sums, others, weight):
    rows, half = keep.shape
    features = weight.shape[0]

    def kernel(order_ref, exits_ref, cot_ref, gain_ref, keep_ref, got_ref, sums_ref, others_ref,
               weight_ref, db_ref, delta_ref, gain_out, away_ref):
        sec, mp = lax.axis_index("section"), lax.axis_index("mp")
        micro = order_ref[0, own_slot()]
        live = jnp.where(exits_ref[micro] > 1, 1.0, 0.0)
        stats = to_columns(sums_ref[...] + others_ref[...])
        pre = jnp.where(sec == 0, got_ref[...], keep_ref[...])
        cot = cot_ref[micro].astype(f32)
        normed, delta = delta_of(pre, cot * gain_ref[...], stats[:, 0:1], stats[:, 1:2], features)
        delta = delta * live
        delta_ref[...] = delta
        db = delta.astype(bf16)
        db_ref[...] = db
        gain_out[...] = jnp.sum(cot * normed, axis=0, keepdims=True) * live
        part = weight_ref[pl.ds(pl.multiple_of((1 - mp) * half, 128), half)]
        away_ref[...] = lax.dot_general(
            part, db, (((1,), (1,)), ((), ())), preferred_element_type=f32
        ).astype(bf16)

    return call(
        kernel,
        [((rows, half), bf16), ((rows, half), f32), ((1, half), f32), ((half, rows), bf16)],
        [(SMEM, order), (SMEM, exits), (VMEM, cotangent), (VMEM, gain), (VMEM, keep), (VMEM, got),
         (VMEM, sums), (VMEM, others), (VMEM, weight)],
    )


def kept_half(db, weight):
    rows, half = db.shape

    def kernel(db_ref, weight_ref, out_ref):
        part = weight_ref[pl.ds(pl.multiple_of(lax.axis_index("mp") * half, 128), half)]
        out_ref[...] = lax.dot_general(
            part, db_ref[...], (((1,), (1,)), ((), ())), preferred_element_type=f32
        )

    return call(kernel, [((half, rows), f32)], [(VMEM, db), (VMEM, weight)])[0]


def carry(order, exits, cotangent, gain, keep, got, sums, others, kept, sent, gain1, features):
    rows, half = keep.shape

    def kernel(order_ref, exits_ref, cot_ref, gain_ref, keep_ref, got_ref, sums_ref, others_ref,
               kept_ref, sent_ref, gain1_ref, carried_ref, inner_ref, gain_out):
        sec = lax.axis_index("section")
        micro = order_ref[0, own_slot()]
        passed = (kept_ref[...] + sent_ref[...].astype(f32)).astype(bf16).astype(f32).T
        cot = cot_ref[micro].astype(f32)
        carried = jnp.where(exits_ref[micro] > 1, passed, cot)
        carried_ref[...] = carried
        pre = jnp.where(sec == 0, keep_ref[...], got_ref[...])
        inner = jnp.sum(carried * gain_ref[...] * pre, axis=1, keepdims=True)
        inner_ref[...] = to_rows([inner])
        squares = to_columns(sums_ref[...] + others_ref[...])[:, 2:3]
        inverse = 1.0 / jnp.sqrt(squares / features + epsilon)
        gains = jnp.sum(carried * (pre * inverse), axis=0, keepdims=True) + gain1_ref[...]
        gain_out[...] = jnp.broadcast_to(gains, (8, half))

    return call(
        kernel,
        [((rows, half), f32), ((8, rows), f32), ((8, half), f32)],
        [(SMEM, order), (SMEM, exits)]
        + [
            (VMEM, value)
            for value in (cotangent, gain, keep, got, sums, others, kept, sent, gain1)
        ],
    )


def iteration0(gain, keep, got, sums, others, carried, inner, inner_other, delta1, features):
    rows, half = keep.shape

    def kernel(gain_ref, keep_ref, got_ref, sums_ref, others_ref, carried_ref, inner_ref, other_ref,
               delta1_ref, total_ref, db_ref):
        sec = lax.axis_index("section")
        squares = to_columns(sums_ref[...] + others_ref[...])[:, 2:3]
        inner = to_columns(inner_ref[...] + other_ref[...])[:, 0:1]
        pre = jnp.where(sec == 0, keep_ref[...], got_ref[...])
        _, delta = delta_of(pre, carried_ref[...] * gain_ref[...], squares, inner, features)
        total_ref[...] = delta + delta1_ref[...]
        db_ref[...] = delta.astype(bf16)

    values = [gain, keep, got, sums, others, carried, inner, inner_other, delta1]
    return call(
        kernel,
        [((rows, half), f32), ((rows, half), bf16)],
        [(VMEM, value) for value in values],
    )


def stacked(columns):
    def kernel(*refs):
        for chip, ref in enumerate(refs[:-1]):
            refs[-1][chip] = ref[...]

    outs = [((len(columns), *columns[0].shape), bf16)]
    return call(kernel, outs, [(VMEM, value) for value in columns])[0]


def left_side(columns, others):
    group, height, rows = columns.shape

    def kernel(own_ref, other_ref, out_ref):
        for index, pair in enumerate([(own_ref, other_ref), (other_ref, own_ref)]):

            @pl.when(lax.axis_index("section") == index)
            def _():
                for k, ref in enumerate(pair):
                    for chip in range(group):
                        base = (k * group + chip) * rows
                        out_ref[:, base : base + rows] = ref[chip]

    return call(
        kernel,
        [((height, 2 * group * rows), bf16)],
        [(VMEM, value) for value in (columns, others)],
    )[0]


def weight_terms(left, grads, k, lanes, base=()):
    rows = grads[0].shape[0]
    depth = len(grads) * rows
    height = left.shape[0]
    start, width = lanes

    def kernel(left_ref, *refs):
        grads_refs, base_refs = refs[: len(grads)], refs[len(grads) : -3]
        keep_ref, send_ref, right = refs[-3:]
        part = slice(start, start + width)
        for index, grads_ref in enumerate(grads_refs):
            right[index * rows : (index + 1) * rows] = grads_ref[:, part]
        for core, (first, second) in enumerate([(0, 1), (1, 0)]):

            @pl.when(lax.axis_index("section") == core)
            def _():
                terms = jnp.dot(
                    left_ref[:, k * depth : (k + 1) * depth],
                    right[...],
                    preferred_element_type=f32,
                )
                halves = [terms[: height // 2], terms[height // 2 :]]
                for out_ref, index in [(keep_ref, first), (send_ref, second)]:
                    total = halves[index]
                    if base_refs:
                        total = total + base_refs[0 if out_ref is keep_ref else 1][:, part]
                    out_ref[...] = total

    return call(
        kernel,
        [((height // 2, width), f32)] * 2,
        [(VMEM, value) for value in [left, *grads, *base]],
        [pltpu.VMEM((depth, width), bf16)],
    )


def chip_sum(keep, other, block):
    height, width = keep.shape

    def kernel(keep_ref, other_ref, own_ref, *away_refs):
        total = keep_ref[...] + other_ref[...]
        own_ref[...] = total[:block]
        for index, away_ref in enumerate(away_refs):
            away_ref[...] = total[(index + 1) * block : (index + 2) * block].astype(bf16)

    outs = [((block, width), f32)] + [((block, width), bf16)] * (height // block - 1)
    return call(kernel, outs, [(VMEM, keep), (VMEM, other)])


def final_sum(own, others, gains, half):
    block = own[0].shape[0]
    count = len(others[0])

    def kernel(*refs):
        gain_refs, refs = refs[: len(gains)], refs[len(gains) :]
        weight_out, gain_out = refs[-2:]
        start = 0
        for part in range(len(own)):
            own_ref, *other_refs = refs[part * (count + 1) : (part + 1) * (count + 1)]
            total = own_ref[...]
            for other_ref in other_refs:
                total = total + other_ref[...].astype(f32)
            width = own_ref.shape[1]
            weight_out[:, start : start + width] = total
            start += width
        sums = [ref[:1] for ref in gain_refs]
        while len(sums) > 1:
            sums = [a + b for a, b in zip(sums[::2], sums[1::2])]
        gain_out[...] = sums[0].reshape(half)

    values = [value for mine, theirs in zip(own, others) for value in (mine, *theirs)]
    ins = [(VMEM, value) for value in (*gains, *values)]
    return call(kernel, [((block, half), f32), ((half,), f32)], ins)


def place(order, total, other):
    rows, half = total.shape

    def kernel(order_ref, total_ref, other_ref, out_ref):
        micro = order_ref[0, own_slot()]
        out_ref[micro] = total_ref[...]
        out_ref[1 - micro] = other_ref[...]

    ins = [(SMEM, order), (VMEM, total), (VMEM, other)]
    return call(kernel, [((2, rows, half), f32)], ins)[0]


def shards(states, injection, cotangent, gain, weight, exits, order):
    stash = states[0]
    slots, rows, features = stash.shape
    half = weight.shape[1]
    dp = lax.axis_index("dp")
    chips = lax.axis_size("dp")
    group = 4
    groups = chips // group
    assert slots == 2 and lax.axis_size("section") == 2 and lax.axis_size("mp") == 2
    assert chips % group == 0 and groups & (groups - 1) == 0

    def across(value, distance):
        return lax.ppermute(value, "dp", [(i, i ^ distance) for i in range(chips)])

    def gathered(value):
        moved = [across(value, distance) for distance in range(group - 1, 0, -1)]
        return [value] + moved[::-1]

    block = features // (2 * chips)
    gain = gain.reshape(1, half)
    weight = load(weight)
    keep, send, columns = forward(stash, weight, injection, order, chips, group)
    moved = [across(columns[distance], distance) for distance in range(group - 1, 0, -1)]
    columns = columns[:1] + moved[::-1]
    got = swap(send, "section")
    sums = row_sums(order, cotangent, gain, keep, got)
    others = opposite(sums)
    db1, delta1, gain1, away = lower_iteration1(
        order, exits, cotangent, gain, keep, got, sums, others, weight
    )
    blocks1, *moved = lax.optimization_barrier((db1, *columns[:0:-1]))
    columns = columns[:1] + moved[::-1]
    sent = opposite(away)
    grads1 = gathered(blocks1)
    kept = kept_half(db1, weight)
    kept, sent = lax.optimization_barrier((kept, sent))

    carried, inner, gains = carry(
        order, exits, cotangent, gain, keep, got, sums, others, kept, sent, gain1, features
    )
    inner_other, gains_other = opposite(inner), swap(gains, "section")
    columns = stacked(columns)
    gains = gains + gains_other
    total, db0 = iteration0(
        gain, keep, got, sums, others, carried, inner, inner_other, delta1, features
    )
    db0, gains, columns, *moved = lax.optimization_barrier(
        (db0, gains, columns, *grads1[:0:-1])
    )
    grads1[1:] = moved[::-1]
    grads0 = gathered(db0)
    columns, total = lax.optimization_barrier((columns, total))
    left = left_side(columns, opposite(columns))

    far_gains = across(gains, 2)
    base = weight_terms(left, grads1, 1, (0, half))
    grads0[1:] = grads0[:0:-1]
    left, base, grads0, far_gains = lax.optimization_barrier((left, base, grads0, far_gains))
    grads0[1:] = grads0[:0:-1]
    gains = gains + far_gains

    cut = (half // 3 + 127) // 128 * 128
    terms = [weight_terms(left, grads0, 0, lanes, base) for lanes in chunks_of(half, cut)]
    arrived = [swap(send, "section") for _, send in terms]
    own, others = [], []
    for part, (keep, _) in enumerate(terms):
        if not part:
            keep, *_ = lax.optimization_barrier((keep, *terms[-1]))
        else:
            keep, *_ = lax.optimization_barrier((keep, *aways))
            if part == 1:
                total, *_ = lax.optimization_barrier((total, *aways))
        mine, *aways = chip_sum(keep, arrived[part], block)
        own.append(mine)
        others.append([across(away, group * (i + 1)) for i, away in enumerate(aways)])
    gains, *_ = lax.optimization_barrier((gains, *aways))
    gains = gains + across(gains, 1)
    gains = [gains] + [across(gains, group * other) for other in range(1, groups)]
    d_injection = place(order, total, swap(total, "section"))
    others[-1], d_injection = lax.optimization_barrier((others[-1], d_injection))
    d_weight, d_gain = final_sum(own, others, gains, half)
    return (d_injection, d_weight, d_gain)


def solution(mesh):
    return jax.shard_map(
        shards,
        mesh=mesh,
        in_specs=(
            P("section", "dp", None, None),
            P("dp", None, "mp"),
            P("dp", None, "mp"),
            P("mp"),
            P(None, "mp"),
            P("dp"),
            P("dp", None),
        ),
        out_specs=(P("dp", None, "mp"), P(("section", "dp"), "mp"), P("mp")),
        check_vma=False,
    )
```

```python
import jax
import jax.numpy as jnp
from jax import lax
from jax.experimental import pallas as pl
from jax.experimental.pallas import tpu as pltpu
from jax.sharding import PartitionSpec as P

epsilon = 1e-06
f32, bf16 = jnp.float32, jnp.bfloat16
VMEM = pl.BlockSpec(memory_space=pltpu.VMEM)
SMEM = pl.BlockSpec(memory_space=pltpu.SMEM)
HBM = pl.BlockSpec(memory_space=pltpu.HBM)


def call(kernel, outs, ins, scratch=(), limit=24, out_specs=None):
    shapes = [jax.ShapeDtypeStruct(shape, kind) for shape, kind in outs]
    specs, values = zip(*ins)
    return pl.pallas_call(
        kernel,
        out_shape=shapes,
        in_specs=list(specs),
        out_specs=out_specs or [VMEM] * len(shapes),
        scratch_shapes=list(scratch),
        compiler_params=pltpu.CompilerParams(vmem_limit_bytes=limit * 2**20),
        cost_estimate=pl.CostEstimate(flops=1000, bytes_accessed=1000, transcendentals=0),
    )(*values)


def swap(value, axis):
    return lax.ppermute(value, axis, [(0, 1), (1, 0)])


def opposite(value):
    return lax.ppermute(value, ("section", "mp"), [(i, 3 - i) for i in range(4)])


def own_slot():
    return lax.axis_index("section") ^ lax.axis_index("mp")


def chunks_of(total, size):
    return [(start, min(size, total - start)) for start in range(0, total, size)]


def to_rows(columns):
    rows = columns[0].shape[0]
    lane = lax.broadcasted_iota(jnp.int32, (rows, 128), 1)
    wide = jnp.zeros((rows, 128), f32)
    for index, column in enumerate(columns):
        wide = jnp.where(lane == index, column, wide)
    return wide.T[:8]


def to_columns(packed):
    return jnp.concatenate([packed] * 16, axis=0).T


def load(weight):
    parts = chunks_of(weight.shape[0], 512)

    def kernel(weight_hbm, w, sems):
        copies = []
        for index, (start, size) in enumerate(parts):
            part = pl.ds(start, size)
            copies.append(pltpu.make_async_copy(weight_hbm.at[part], w.at[part], sems.at[index]))
            copies[-1].start()
        for copy in copies:
            copy.wait()

    return call(
        kernel,
        [(weight.shape, bf16)],
        [(HBM, weight)],
        [pltpu.SemaphoreType.DMA((len(parts),))],
        limit=42,
    )[0]


def forward(stash, weight, injection, order, chips, group):
    slots, rows, features = stash.shape
    half = weight.shape[1]
    block = features // (2 * chips)
    groups = chips // group
    height = 2 * groups * block

    def kernel(order_ref, stash_ref, weight_ref, inj_ref, keep_ref, send_ref, *refs):
        *out_refs, turned = refs
        slot = own_slot()
        left = stash_ref[...].reshape(slots * rows, features)
        for start, size in chunks_of(half, 256):
            part = slice(start, start + size)
            term = jnp.dot(left, weight_ref[:, part], preferred_element_type=f32)
            first, second = term[:rows], term[rows:]
            keep, send = jnp.where(slot == 0, first, second), jnp.where(slot == 0, second, first)
            keep_ref[:, part] = keep + inj_ref[order_ref[0, slot], :, part].astype(f32)
            send_ref[:, part] = send + inj_ref[order_ref[0, 1 - slot], :, part].astype(f32)
        if out_refs:
            turned[...] = stash_ref[slot].T
        dp = lax.axis_index("dp")
        for distance, out_ref in enumerate(out_refs):
            for half_index in range(2):
                for other in range(groups):
                    chip = dp ^ (distance + group * other)
                    source = pl.multiple_of((half_index * chips + chip) * block, 16)
                    base = (half_index * groups + other) * block
                    out_ref[base : base + block] = turned[pl.ds(source, block)]

    pieces = group if block % 16 == 0 else 0
    keep, send, *columns = call(
        kernel,
        [((rows, half), f32)] * 2 + [((height, rows), bf16)] * pieces,
        [(SMEM, order), (VMEM, stash), (VMEM, weight), (VMEM, injection)],
        [pltpu.VMEM((features, rows), bf16)],
    )
    if not columns:
        turned = lax.dynamic_index_in_dim(stash, own_slot(), 0, keepdims=False).T
        turned = turned.reshape(2, chips, block, rows)
        for distance in range(group):
            picked = [
                lax.dynamic_index_in_dim(
                    turned, lax.axis_index("dp") ^ (distance + group * other), 1, keepdims=False
                )
                for other in range(groups)
            ]
            columns.append(jnp.stack(picked, axis=1).reshape(height, rows))
    return keep, send, columns


def row_sums(order, cotangent, gain, keep, got):
    rows = keep.shape[0]

    def kernel(order_ref, cot_ref, gain_ref, keep_ref, got_ref, out_ref):
        sec = lax.axis_index("section")
        first = sec == 0
        keep, got = keep_ref[...], got_ref[...]
        pre1, pre0 = jnp.where(first, got, keep), jnp.where(first, keep, got)
        u = cot_ref[order_ref[0, own_slot()]].astype(f32) * gain_ref[...]
        sums = [pre1 * pre1, u * pre1, pre0 * pre0]
        out_ref[...] = to_rows([jnp.sum(each, axis=1, keepdims=True) for each in sums])

    ins = [(SMEM, order), (VMEM, cotangent), (VMEM, gain), (VMEM, keep), (VMEM, got)]
    return call(kernel, [((8, rows), f32)], ins)[0]


def delta_of(pre, u, squares, inner, features):
    radius = jnp.sqrt(squares / features + epsilon)
    inverse = 1.0 / radius
    normed = pre * inverse
    return normed, (u - normed * (inner * inverse / features)) * inverse


def lower_iteration1(order, exits, cotangent, gain, keep, got, sums, others, weight):
    rows, half = keep.shape
    features = weight.shape[0]

    def kernel(order_ref, exits_ref, cot_ref, gain_ref, keep_ref, got_ref, sums_ref, others_ref,
               weight_ref, db_ref, delta_ref, gain_out, away_ref):
        sec, mp = lax.axis_index("section"), lax.axis_index("mp")
        micro = order_ref[0, own_slot()]
        live = jnp.where(exits_ref[micro] > 1, 1.0, 0.0)
        stats = to_columns(sums_ref[...] + others_ref[...])
        pre = jnp.where(sec == 0, got_ref[...], keep_ref[...])
        cot = cot_ref[micro].astype(f32)
        normed, delta = delta_of(pre, cot * gain_ref[...], stats[:, 0:1], stats[:, 1:2], features)
        delta = delta * live
        delta_ref[...] = delta
        db = delta.astype(bf16)
        db_ref[...] = db
        gain_out[...] = jnp.sum(cot * normed, axis=0, keepdims=True) * live
        part = weight_ref[pl.ds(pl.multiple_of((1 - mp) * half, 128), half)]
        away_ref[...] = lax.dot_general(
            part, db, (((1,), (1,)), ((), ())), preferred_element_type=f32
        ).astype(bf16)

    return call(
        kernel,
        [((rows, half), bf16), ((rows, half), f32), ((1, half), f32), ((half, rows), bf16)],
        [(SMEM, order), (SMEM, exits), (VMEM, cotangent), (VMEM, gain), (VMEM, keep), (VMEM, got),
         (VMEM, sums), (VMEM, others), (VMEM, weight)],
    )


def kept_half(db, weight):
    rows, half = db.shape

    def kernel(db_ref, weight_ref, out_ref):
        part = weight_ref[pl.ds(pl.multiple_of(lax.axis_index("mp") * half, 128), half)]
        out_ref[...] = lax.dot_general(
            part, db_ref[...], (((1,), (1,)), ((), ())), preferred_element_type=f32
        )

    return call(kernel, [((half, rows), f32)], [(VMEM, db), (VMEM, weight)])[0]


def carry(order, exits, cotangent, gain, keep, got, sums, others, kept, sent, gain1, features):
    rows, half = keep.shape

    def kernel(order_ref, exits_ref, cot_ref, gain_ref, keep_ref, got_ref, sums_ref, others_ref,
               kept_ref, sent_ref, gain1_ref, carried_ref, inner_ref, gain_out):
        sec = lax.axis_index("section")
        micro = order_ref[0, own_slot()]
        passed = (kept_ref[...] + sent_ref[...].astype(f32)).astype(bf16).astype(f32).T
        cot = cot_ref[micro].astype(f32)
        carried = jnp.where(exits_ref[micro] > 1, passed, cot)
        carried_ref[...] = carried
        pre = jnp.where(sec == 0, keep_ref[...], got_ref[...])
        inner = jnp.sum(carried * gain_ref[...] * pre, axis=1, keepdims=True)
        inner_ref[...] = to_rows([inner])
        squares = to_columns(sums_ref[...] + others_ref[...])[:, 2:3]
        inverse = 1.0 / jnp.sqrt(squares / features + epsilon)
        gains = jnp.sum(carried * (pre * inverse), axis=0, keepdims=True) + gain1_ref[...]
        gain_out[...] = jnp.broadcast_to(gains, (8, half))

    return call(
        kernel,
        [((rows, half), f32), ((8, rows), f32), ((8, half), f32)],
        [(SMEM, order), (SMEM, exits)]
        + [
            (VMEM, value)
            for value in (cotangent, gain, keep, got, sums, others, kept, sent, gain1)
        ],
    )


def iteration0(gain, keep, got, sums, others, carried, inner, inner_other, delta1, features):
    rows, half = keep.shape

    def kernel(gain_ref, keep_ref, got_ref, sums_ref, others_ref, carried_ref, inner_ref, other_ref,
               delta1_ref, total_ref, db_ref):
        sec = lax.axis_index("section")
        squares = to_columns(sums_ref[...] + others_ref[...])[:, 2:3]
        inner = to_columns(inner_ref[...] + other_ref[...])[:, 0:1]
        pre = jnp.where(sec == 0, keep_ref[...], got_ref[...])
        _, delta = delta_of(pre, carried_ref[...] * gain_ref[...], squares, inner, features)
        total_ref[...] = delta + delta1_ref[...]
        db_ref[...] = delta.astype(bf16)

    values = [gain, keep, got, sums, others, carried, inner, inner_other, delta1]
    return call(
        kernel,
        [((rows, half), f32), ((rows, half), bf16)],
        [(VMEM, value) for value in values],
    )


def stacked(columns):
    def kernel(*refs):
        for chip, ref in enumerate(refs[:-1]):
            refs[-1][chip] = ref[...]

    outs = [((len(columns), *columns[0].shape), bf16)]
    return call(kernel, outs, [(VMEM, value) for value in columns])[0]


def left_side(columns, others):
    group, height, rows = columns.shape

    def kernel(own_ref, other_ref, out_ref):
        for index, pair in enumerate([(own_ref, other_ref), (other_ref, own_ref)]):

            @pl.when(lax.axis_index("section") == index)
            def _():
                for k, ref in enumerate(pair):
                    for chip in range(group):
                        base = (k * group + chip) * rows
                        out_ref[:, base : base + rows] = ref[chip]

    return call(
        kernel,
        [((height, 2 * group * rows), bf16)],
        [(VMEM, value) for value in (columns, others)],
    )[0]


def weight_terms(left, grads, k, lanes, base=()):
    rows = grads[0].shape[0]
    depth = len(grads) * rows
    height = left.shape[0]
    start, width = lanes

    def kernel(left_ref, *refs):
        grads_refs, base_refs = refs[: len(grads)], refs[len(grads) : -3]
        keep_ref, send_ref, right = refs[-3:]
        part = slice(start, start + width)
        for index, grads_ref in enumerate(grads_refs):
            right[index * rows : (index + 1) * rows] = grads_ref[:, part]
        for core, (first, second) in enumerate([(0, 1), (1, 0)]):

            @pl.when(lax.axis_index("section") == core)
            def _():
                terms = jnp.dot(
                    left_ref[:, k * depth : (k + 1) * depth],
                    right[...],
                    preferred_element_type=f32,
                )
                halves = [terms[: height // 2], terms[height // 2 :]]
                for out_ref, index in [(keep_ref, first), (send_ref, second)]:
                    total = halves[index]
                    if base_refs:
                        total = total + base_refs[0 if out_ref is keep_ref else 1][:, part]
                    out_ref[...] = total

    return call(
        kernel,
        [((height // 2, width), f32)] * 2,
        [(VMEM, value) for value in [left, *grads, *base]],
        [pltpu.VMEM((depth, width), bf16)],
    )


def chip_sum(keep, other, block):
    height, width = keep.shape

    def kernel(keep_ref, other_ref, own_ref, *away_refs):
        total = keep_ref[...] + other_ref[...]
        own_ref[...] = total[:block]
        for index, away_ref in enumerate(away_refs):
            away_ref[...] = total[(index + 1) * block : (index + 2) * block].astype(bf16)

    outs = [((block, width), f32)] + [((block, width), bf16)] * (height // block - 1)
    return call(kernel, outs, [(VMEM, keep), (VMEM, other)])


def final_sum(own, others, gains, half):
    block = own[0].shape[0]
    count = len(others[0])

    def kernel(*refs):
        gain_refs, refs = refs[: len(gains)], refs[len(gains) :]
        weight_out, gain_out, sums_ref, sems = refs[-4:]
        start = 0
        copies = []
        for part in range(len(own)):
            own_ref, *other_refs = refs[part * (count + 1) : (part + 1) * (count + 1)]
            total = own_ref[...]
            for other_ref in other_refs:
                total = total + other_ref[...].astype(f32)
            width = own_ref.shape[1]
            sums_ref[:, start : start + width] = total
            part_of = pl.ds(start, width)
            copies.append(
                pltpu.make_async_copy(
                    sums_ref.at[:, part_of], weight_out.at[:, part_of], sems.at[part]
                )
            )
            copies[-1].start()
            start += width
        sums = [ref[:1] for ref in gain_refs]
        while len(sums) > 1:
            sums = [a + b for a, b in zip(sums[::2], sums[1::2])]
        gain_out[...] = sums[0].reshape(half)
        for copy in copies:
            copy.wait()

    values = [value for mine, theirs in zip(own, others) for value in (mine, *theirs)]
    ins = [(VMEM, value) for value in (*gains, *values)]
    return call(
        kernel,
        [((block, half), f32), ((half,), f32)],
        ins,
        [pltpu.VMEM((block, half), f32), pltpu.SemaphoreType.DMA((len(own),))],
        out_specs=[HBM, VMEM],
    )


def place(order, total, other):
    rows, half = total.shape

    def kernel(order_ref, total_ref, other_ref, out_ref):
        micro = order_ref[0, own_slot()]
        out_ref[micro] = total_ref[...]
        out_ref[1 - micro] = other_ref[...]

    ins = [(SMEM, order), (VMEM, total), (VMEM, other)]
    return call(kernel, [((2, rows, half), f32)], ins)[0]


def shards(states, injection, cotangent, gain, weight, exits, order):
    stash = states[0]
    slots, rows, features = stash.shape
    half = weight.shape[1]
    dp = lax.axis_index("dp")
    chips = lax.axis_size("dp")
    group = 4
    groups = chips // group
    assert slots == 2 and lax.axis_size("section") == 2 and lax.axis_size("mp") == 2
    assert chips % group == 0 and groups & (groups - 1) == 0

    def across(value, distance):
        return lax.ppermute(value, "dp", [(i, i ^ distance) for i in range(chips)])

    def gathered(value):
        moved = [across(value, distance) for distance in range(group - 1, 0, -1)]
        return [value] + moved[::-1]

    block = features // (2 * chips)
    gain = gain.reshape(1, half)
    weight = load(weight)
    keep, send, columns = forward(stash, weight, injection, order, chips, group)
    moved = [across(columns[distance], distance) for distance in range(group - 1, 0, -1)]
    columns = columns[:1] + moved[::-1]
    got = swap(send, "section")
    sums = row_sums(order, cotangent, gain, keep, got)
    others = opposite(sums)
    db1, delta1, gain1, away = lower_iteration1(
        order, exits, cotangent, gain, keep, got, sums, others, weight
    )
    blocks1, *moved = lax.optimization_barrier((db1, *columns[:0:-1]))
    columns = columns[:1] + moved[::-1]
    sent = opposite(away)
    grads1 = gathered(blocks1)
    kept = kept_half(db1, weight)
    kept, sent = lax.optimization_barrier((kept, sent))

    carried, inner, gains = carry(
        order, exits, cotangent, gain, keep, got, sums, others, kept, sent, gain1, features
    )
    inner_other, gains_other = opposite(inner), swap(gains, "section")
    columns = stacked(columns)
    gains = gains + gains_other
    total, db0 = iteration0(
        gain, keep, got, sums, others, carried, inner, inner_other, delta1, features
    )
    db0, gains, columns, *moved = lax.optimization_barrier(
        (db0, gains, columns, *grads1[:0:-1])
    )
    grads1[1:] = moved[::-1]
    grads0 = gathered(db0)
    columns, total = lax.optimization_barrier((columns, total))
    left = left_side(columns, opposite(columns))

    far_gains = across(gains, 2)
    base = weight_terms(left, grads1, 1, (0, half))
    grads0[1:] = grads0[:0:-1]
    left, base, grads0, far_gains = lax.optimization_barrier((left, base, grads0, far_gains))
    grads0[1:] = grads0[:0:-1]
    gains = gains + far_gains

    cut = (half // 3 + 127) // 128 * 128
    terms = [weight_terms(left, grads0, 0, lanes, base) for lanes in chunks_of(half, cut)]
    arrived = [swap(send, "section") for _, send in terms]
    own, others = [], []
    for part, (keep, _) in enumerate(terms):
        if not part:
            keep, *_ = lax.optimization_barrier((keep, *terms[-1]))
        else:
            keep, *_ = lax.optimization_barrier((keep, *aways))
            if part == 1:
                total, *_ = lax.optimization_barrier((total, *aways))
        mine, *aways = chip_sum(keep, arrived[part], block)
        own.append(mine)
        others.append([across(away, group * (i + 1)) for i, away in enumerate(aways)])
    gains, *_ = lax.optimization_barrier((gains, *aways))
    gains = gains + across(gains, 1)
    gains = [gains] + [across(gains, group * other) for other in range(1, groups)]
    d_injection = place(order, total, swap(total, "section"))
    others[-1], d_injection = lax.optimization_barrier((others[-1], d_injection))
    d_weight, d_gain = final_sum(own, others, gains, half)
    return (d_injection, d_weight, d_gain)


def solution(mesh):
    return jax.shard_map(
        shards,
        mesh=mesh,
        in_specs=(
            P("section", "dp", None, None),
            P("dp", None, "mp"),
            P("dp", None, "mp"),
            P("mp"),
            P(None, "mp"),
            P("dp"),
            P("dp", None),
        ),
        out_specs=(P("dp", None, "mp"), P(("section", "dp"), "mp"), P("mp")),
        check_vma=False,
    )
```
